32 devices in a mesh: wide: 8 (over z, core), narrow: 4 (over y, x).
Axes of the slice: x: 2, y: 2, z: 4, core: 2. Of those that a mesh axis runs over, the one named last changes fastest.
Arguments:
- tokens: bfloat16 [32768, 768], P(('wide', 'narrow')), may hold values from -6 to 6
- segment_ids: int32 [32768], P(('wide', 'narrow')), may hold values from -1 to 7, as said below
- out_grad: bfloat16 [32768, 768], P(('wide', 'narrow')), may hold values from -6 to 6
- first_gain: bfloat16 [768], P('narrow'), may hold values from 0.099609375 to 1.8984375
- first_shift: bfloat16 [768], P('narrow'), may hold values from -3 to 3
- query_weight: bfloat16 [768, 768], P('narrow'), may hold values from -0.21875 to 0.21875
- query_bias: bfloat16 [768], P('narrow'), may hold values from -3 to 3
- key_weight: bfloat16 [768, 768], P('narrow'), may hold values from -0.21875 to 0.21875
- value_weight: bfloat16 [768, 768], P('narrow'), may hold values from -0.21875 to 0.21875
- value_bias: bfloat16 [768], P('narrow'), may hold values from -3 to 3
- output_weight: bfloat16 [768, 768], P('narrow'), may hold values from -1.25 to 1.25
- output_bias: bfloat16 [768], P('narrow'), may hold values from -3 to 3
- second_gain: bfloat16 [768], P('narrow'), may hold values from 0.099609375 to 1.8984375
- second_shift: bfloat16 [768], P('narrow'), may hold values from -3 to 3
- up_weight: bfloat16 [768, 3072], P('narrow'), may hold values from -0.21875 to 0.21875
- up_bias: bfloat16 [3072], P('narrow'), may hold values from -3 to 3
- down_weight: bfloat16 [3072, 768], P('narrow'), may hold values from -0.109375 to 0.109375
- down_bias: bfloat16 [768], P('narrow'), may hold values from -3 to 3
Outputs:
- layer_out: bfloat16 [32768, 768], P(('wide', 'narrow'))
- input_grad: bfloat16 [32768, 768], P(('wide', 'narrow'))
- first_gain_grad: float32 [768], P('narrow')
- first_shift_grad: float32 [768], P('narrow')
- query_weight_grad: float32 [768, 768], P('narrow')
- query_bias_grad: float32 [768], P('narrow')
- key_weight_grad: float32 [768, 768], P('narrow')
- value_weight_grad: float32 [768, 768], P('narrow')
- value_bias_grad: float32 [768], P('narrow')
- output_weight_grad: float32 [768, 768], P('narrow')
- output_bias_grad: float32 [768], P('narrow')
- second_gain_grad: float32 [768], P('narrow')
- second_shift_grad: float32 [768], P('narrow')
- up_weight_grad: float32 [768, 3072], P('narrow')
- up_bias_grad: float32 [3072], P('narrow')
- down_weight_grad: float32 [3072, 768], P('narrow')
- down_bias_grad: float32 [768], P('narrow')
The draws below stay inside these ranges and needn't reach their ends.
Inputs may be any that keep to these rules, and one draw needn't show every extreme that they name: `segment_ids`: within each sequence of 512 rows the segment numbers start at 0 and never fall until the padding rows at its end, marked -1; every sequence has 1 to 128 padding rows.
All inputs are finite; a program needn't handle non-finite values.
Results may differ from the reference program's by a relative error of at most 0.019.
Values may be sent and summed in bfloat16 or wider, within the bound.
No kernel may reach another device: no remote copies, remote signals or barrier semaphores. Data moves between devices by JAX's collectives and lax.ppermute only.
A program may use at most 192 MiB of HBM per device.

```python
import jax
import jax.numpy as jnp
from jax import lax

D = 768
HEADS = 12
HEAD = 64
FF = 3072
LEN = 512
TOK_DEV = 1024
TOKENS = 32768


def draw_segment_ids(key, part):
    key = jax.random.fold_in(key, 7)
    count = TOKENS // LEN
    cut_key, pad_key = jax.random.split(key)
    starts = (jax.random.randint(cut_key, (count, LEN), 0, LEN // 4) == 0).astype(jnp.int32)
    starts = starts.at[:, 0].set(0)
    place = jnp.arange(LEN)[None, :]
    forced = ((place % (LEN // 16) == 0) & (place > 0) & (place <= LEN // 2)).astype(jnp.int32)
    first_row = (jnp.arange(count)[:, None] == 0).astype(jnp.int32)
    starts = jnp.maximum(starts, forced * first_row)
    numbers = jnp.minimum(jnp.cumsum(starts, axis=1), 7)
    padding = jax.random.randint(pad_key, (count, 1), 1, LEN // 4 + 1)
    numbers = jnp.where(place >= LEN - padding, -1, numbers)
    return numbers.reshape(TOKENS).astype(jnp.int32)


def shard_levels(stream_key, extent, shards, least, top_value):
    def one(axis_at, blocks):
        draws = jax.random.uniform(jax.random.fold_in(jax.random.fold_in(stream_key, 6), axis_at), (blocks,), jnp.float32, least / len(shards), top_value / len(shards))
        return jnp.repeat(jnp.exp(draws), extent[axis_at] // blocks).reshape((-1,) + (1,) * (len(extent) - axis_at - 1))

    level = one(*shards[0])
    for cut in shards[1:]:
        level = level * one(*cut)
    return level


def centred(rng, dims, scale, most, cuts=(), kind=jnp.bfloat16):
    values = jax.random.normal(rng, dims, jnp.float32) * scale
    if len(cuts) > 0:
        values = shard_levels(rng, dims, cuts, -0.22, 0.18) * values
    return jnp.clip(values, min=-most, max=most).astype(kind)


def setup_inputs(seed: int = 0) -> dict:
    key_of = jax.random.split(jax.random.key(seed), 19)
    tokens = centred(key_of[0], (TOKENS, D), 1.0, 6.0, ((0, 32),))
    segment_ids = draw_segment_ids(jax.random.fold_in(key_of[18], 71), 0)
    out_grad = centred(key_of[2], (TOKENS, D), 1.0, 6.0, ((0, 32),))
    first_gain = jnp.clip(1.0 + 0.18 * jax.random.normal(key_of[3], (D,), jnp.float32), 0.099609375, 1.8984375).astype(jnp.bfloat16)
    first_shift = centred(key_of[4], (D,), 0.3, 3.0, ((0, 4),))
    query_weight = centred(key_of[5], (D, D), D ** -0.5, 0.21875, ((0, 4),))
    query_bias = centred(key_of[6], (D,), 0.3, 3.0, ((0, 4),))
    key_weight = centred(key_of[7], (D, D), D ** -0.5, 0.21875, ((0, 4),))
    value_weight = centred(key_of[8], (D, D), D ** -0.5, 0.21875, ((0, 4),))
    value_bias = centred(key_of[9], (D,), 0.3, 3.0, ((0, 4),))
    output_weight = centred(key_of[10], (D, D), (D // 32) ** -0.5, 1.25, ((0, 4),))
    output_bias = centred(key_of[11], (D,), 0.3, 3.0, ((0, 4),))
    second_gain = jnp.clip(1.0 + 0.18 * jax.random.normal(key_of[12], (D,), jnp.float32), 0.099609375, 1.8984375).astype(jnp.bfloat16)
    second_shift = centred(key_of[13], (D,), 0.3, 3.0, ((0, 4),))
    up_weight = centred(key_of[14], (D, FF), D ** -0.5, 0.21875, ((0, 4),))
    up_bias = centred(key_of[15], (FF,), 0.3, 3.0, ((0, 4),))
    down_weight = centred(key_of[16], (FF, D), FF ** -0.5, 0.109375, ((0, 4),))
    down_bias = centred(key_of[17], (D,), 0.3, 3.0, ((0, 4),))
    return dict(tokens=tokens, segment_ids=segment_ids, out_grad=out_grad, first_gain=first_gain, first_shift=first_shift, query_weight=query_weight, query_bias=query_bias, key_weight=key_weight, value_weight=value_weight, value_bias=value_bias, output_weight=output_weight, output_bias=output_bias, second_gain=second_gain, second_shift=second_shift, up_weight=up_weight, up_bias=up_bias, down_weight=down_weight, down_bias=down_bias)


@jax.custom_vjp
def low(v):
    return lax.optimization_barrier(v.astype(jnp.bfloat16)).astype(jnp.float32)

@jax.custom_vjp
def low_back(v):
    return v

def low_keep(v):
    return (low(v), None)

def low_pass(kept, grad):
    return (grad,)

def back_keep(v):
    return (v, None)

def back_low(kept, grad):
    return (low(grad),)
low.defvjp(low_keep, low_pass)
low_back.defvjp(back_keep, back_low)
EPSILON = 1e-06
HIGHEST = lax.Precision.HIGHEST

def rounded_both(v):
    return low(low_back(v))

def normalize(v, gain, shift):
    center = v - lax.optimization_barrier(jnp.mean(v, -1, keepdims=True))
    spread = lax.optimization_barrier(jnp.mean(center * center, -1, keepdims=True))
    return center * lax.rsqrt(spread + EPSILON) * gain + shift

def matmul(left, right):
    return jnp.dot(left, right, precision=HIGHEST)

def attend_plain(queries, keys, values, segs):
    count = segs.shape[0] // LEN
    qsplit = queries.reshape(count, LEN, HEADS, HEAD)
    ksplit = keys.reshape(count, LEN, HEADS, HEAD)
    vsplit = values.reshape(count, LEN, HEADS, HEAD)
    seqsegs = segs.reshape(count, LEN)
    raw = jnp.einsum('gqhe,gkhe->ghqk', qsplit, ksplit, precision=HIGHEST) * HEAD ** (-0.5)
    raw = low_back(raw)
    same = seqsegs[:, None, :, None] == seqsegs[:, None, None, :]
    raw = jnp.where(same, raw, -1e+30)
    top = lax.optimization_barrier(jnp.max(raw, -1, keepdims=True))
    expo = jnp.exp(raw - top)
    probs = expo / lax.optimization_barrier(jnp.sum(expo, -1, keepdims=True))
    result = jnp.einsum('ghqk,gkhe->gqhe', low(probs), vsplit, precision=HIGHEST)
    return result.reshape(count * LEN, D)
attend = jax.checkpoint(attend_plain)

def forward(x, params, segs):
    first_gain, first_shift, query_weight, query_bias, key_weight, value_weight, value_bias, output_weight, output_bias, second_gain, second_shift, up_weight, up_bias, down_weight, down_bias = params
    first_normed = low(normalize(x, first_gain, first_shift))
    queries = rounded_both(matmul(first_normed, query_weight) + query_bias)
    keys = rounded_both(matmul(first_normed, key_weight))
    values = rounded_both(matmul(first_normed, value_weight) + value_bias)
    attended = rounded_both(attend(queries, keys, values, segs))
    branch = low_back(matmul(attended, output_weight) + output_bias)
    mid = x + branch
    second_normed = low(normalize(mid, second_gain, second_shift))
    pre = low_back(matmul(second_normed, up_weight) + up_bias)
    hidden = low(jax.nn.gelu(pre, approximate=False))
    final = low_back(matmul(hidden, down_weight) + down_bias)
    return mid + final

def reference(tokens, segment_ids, out_grad, first_gain, first_shift, query_weight, query_bias, key_weight, value_weight, value_bias, output_weight, output_bias, second_gain, second_shift, up_weight, up_bias, down_weight, down_bias):
    params = tuple((p.astype(jnp.float32) for p in (first_gain, first_shift, query_weight, query_bias, key_weight, value_weight, value_bias, output_weight, output_bias, second_gain, second_shift, up_weight, up_bias, down_weight, down_bias)))
    groups = TOKENS // TOK_DEV
    inputs = tokens.astype(jnp.float32).reshape(groups, TOK_DEV, D)
    segs = segment_ids.reshape(groups, TOK_DEV)
    live = (segs >= 0).astype(jnp.float32)[:, :, None]
    cotangent = out_grad.astype(jnp.float32).reshape(groups, TOK_DEV, D) * live

    def step(total, item):
        block, block_segs, block_cot = item
        result, pull = jax.vjp(lambda xv, pv: forward(xv, pv, block_segs), block, params)
        grad_block, grad_params = pull(block_cot)
        total = jax.tree.map(jnp.add, total, grad_params)
        return (total, (result.astype(jnp.bfloat16), grad_block.astype(jnp.bfloat16)))
    zeros = tuple((jnp.zeros_like(p) for p in params))
    total, (outputs, grads) = lax.scan(step, zeros, (inputs, segs, cotangent))
    return (outputs.reshape(TOKENS, D), grads.reshape(TOKENS, D), total[0], total[1], total[2], total[3], total[4], total[5], total[6], total[7], total[8], total[9], total[10], total[11], total[12], total[13], total[14])
```

```python
import functools

import jax
import jax.numpy as jnp
from jax import lax
from jax.experimental import pallas as pl
from jax.experimental.pallas import tpu as pltpu
from jax.sharding import PartitionSpec as P

D = 768
HEADS = 12
HEAD = 64
LEN = 512
FF = 3072
EPSILON = 1e-06
TILE = 256
BAND = D // 8
PAIR = 2 * HEAD
PAIRS = HEADS // 2
CHUNKS = (4, 2)
LOG2E = 1.4426950408889634
LN2 = 0.6931471805599453

bf16 = jnp.bfloat16
f32 = jnp.float32
NN = (((1,), (0,)), ((), ()))
NT = (((1,), (1,)), ((), ()))
TN = (((0,), (0,)), ((), ()))
ANY = pl.BlockSpec(memory_space=pl.ANY)


def dot(left, right, dims=NN):
    return lax.dot_general(left, right, dims, preferred_element_type=f32)


def shape(dims, kind):
    return jax.ShapeDtypeStruct(dims, kind)


def column_sum(values):
    return jnp.sum(values, 0, keepdims=True)


def whole(dims):
    return pl.BlockSpec(dims, lambda *at: (0,) * len(dims))


def rows_block(dims):
    return pl.BlockSpec(dims, lambda at, *rest: (at,) + (0,) * (len(dims) - 1))


class Order:
    def __init__(self, meta):
        self.meta, self.last = meta, []

    def run(
        self, name, body, ins, in_specs, outs, out_specs, grid, scratch, macs, limit, alias={}
    ):
        moved = sum(a.size * a.dtype.itemsize for a in ins)
        moved += sum(o.size * o.dtype.itemsize for o in outs)
        used, extra = len(ins), len(self.last)

        def inner(meta, *refs):
            body(meta, *refs[:used], *refs[used + extra :])

        ins = [pltpu.with_memory_space_constraint(a, pltpu.HBM) for a in ins]
        outs = [pltpu.HBM(o.shape, o.dtype) for o in outs]
        got = pl.pallas_call(
            inner,
            out_shape=outs,
            grid_spec=pltpu.PrefetchScalarGridSpec(
                num_scalar_prefetch=1,
                grid=grid,
                in_specs=[*in_specs] + [ANY] * extra,
                out_specs=out_specs,
                scratch_shapes=scratch,
            ),
            input_output_aliases=alias,
            compiler_params=pltpu.CompilerParams(vmem_limit_bytes=limit * 2**20),
            cost_estimate=pl.CostEstimate(
                flops=int(2 * macs * 1.5), bytes_accessed=moved, transcendentals=0
            ),
            name=name,
        )(self.meta, *ins, *self.last)
        self.last = [got[0]]
        return got

    def small(self, name, body, ins, outs, meta=False):
        moved = sum(a.size * a.dtype.itemsize for a in [*ins, *outs])
        used, extra = len(ins), len(self.last)
        lead = [self.meta] if meta else []

        def inner(*refs):
            held, refs = refs[: len(lead)], refs[len(lead) :]
            body(*held, *refs[:used], *refs[used + extra :])

        vmem = pl.BlockSpec(memory_space=pltpu.VMEM)
        smem = pl.BlockSpec(memory_space=pltpu.SMEM)
        got = pl.pallas_call(
            inner,
            out_shape=outs,
            in_specs=[smem] * len(lead) + [vmem] * used + [ANY] * extra,
            out_specs=[vmem] * len(outs),
            compiler_params=pltpu.CompilerParams(vmem_limit_bytes=16 * 2**20),
            cost_estimate=pl.CostEstimate(flops=0, bytes_accessed=moved, transcendentals=0),
            name=name,
        )(*lead, *ins, *self.last)
        self.last = [got[0]]
        return got


def fill(meta, pieces, target, sems):
    count = 1 if len(pieces) == 1 else len(pieces)
    half = target.shape[0] // 8
    copies = []
    for i in range(count):
        start = pl.multiple_of(meta[i] * half, half) if count > 1 else 0
        copies.append(
            pltpu.make_async_copy(
                pieces[i], target.at[pl.ds(start, pieces[i].shape[0])], sems.at[i]
            )
        )
    return copies


def first_step(copies):
    @pl.when(pl.program_id(0) == 0)
    def _():
        for copy in copies:
            copy.start()
        for copy in copies:
            copy.wait()


def as_column(row):
    return jnp.broadcast_to(row.astype(f32), (8, row.shape[1])).T[:, :1]


def standard(v):
    center = v - jnp.mean(v, -1, keepdims=True)
    rate = lax.rsqrt(jnp.mean(center * center, -1, keepdims=True) + EPSILON)
    return center * rate, rate


def pack(order, parts):
    width = sum(p.shape[1] for p in parts)

    def body(*refs):
        at = 0
        for src in refs[:-1]:
            refs[-1][:, at : at + src.shape[1]] = src[...]
            at += src.shape[1]

    return order.small("pack", body, parts, [shape((parts[0].shape[0], width), bf16)])[0]


def copies(order, halves, wholes=()):
    ins = [*halves, *wholes]
    dims = [(a.shape[0] // 2, a.shape[1]) for a in halves] + [a.shape for a in wholes]

    def body(meta, *refs):
        for i, (src, dst) in enumerate(zip(refs[: len(ins)], refs[len(ins) :])):
            if i < len(halves):
                half = dst.shape[0]
                dst[...] = src[pl.ds(pl.multiple_of(meta[13] * half, half), half)]
            else:
                dst[...] = src[...]

    return order.small("copies", body, ins, [shape(d, bf16) for d in dims], True)


def sums_of(order, plan):
    ins, where = [], {}
    for _, terms in plan:
        for array, _ in terms:
            if id(array) not in where:
                where[id(array)] = len(ins)
                ins.append(array)

    def body(*refs):
        for (rows, terms), out in zip(plan, refs[len(ins) :]):
            total = None
            for array, start in terms:
                term = refs[where[id(array)]][start : start + rows].astype(f32)
                total = term if total is None else total + term
            out[...] = total.astype(bf16)

    dims = [(rows, terms[0][0].shape[1]) for rows, terms in plan]
    return order.small("sums_of", body, ins, [shape(d, bf16) for d in dims])


def pick(order, own, got):
    def body(meta, own, got, out):
        inner = jnp.full(out.shape, meta[14], jnp.int32) == 1
        out[...] = jnp.where(inner, own[...], got[...])

    return order.small("pick", body, [own, got], [shape(own.shape, bf16)], True)[0]


def finish(order, pairs, plan):
    flat = [a for pair in pairs for a in pair]
    half = flat[0].shape[0]

    def body(meta, *refs):
        core = meta[13]
        for (width, parts), out in zip(plan, refs[len(flat) :]):
            at = 0
            for which, first, cols in parts:
                for i in range(2):
                    place = core if i == 0 else 1 - core
                    rows = pl.ds(pl.multiple_of(place * half, half), half)
                    value = refs[2 * which + i][:, first : first + cols]
                    out[rows, at : at + cols] = value.astype(f32)
                at += cols

    outs = [shape((2 * half, width), f32) for width, _ in plan]
    return order.small("finish", body, flat, outs, True)


def attend(order, tokens, vec, segs, pieces, at_seq, before):
    count = len(pieces)
    rows = tokens.shape[0]
    seqs = rows // LEN
    held = 0 if before is None else len(before)

    def body(meta, tok, vec, seg, *rest):
        pieces, rest = rest[:count], rest[count + held :]
        fn_t, q, k, v, att, att_t, expo, inv, bias, w, sems = rest
        p = pl.program_id(0)

        @pl.when(p == 0)
        def _():
            copies = fill(meta, pieces, w, sems)
            for copy in copies:
                copy.start()
            row = seg[0].astype(f32)
            bias[...] = jnp.where(as_column(row) == row, 0.0, -1e30)
            normed = standard(tok[...].astype(f32))[0] * vec[0:1] + vec[1:2]
            low = normed.astype(bf16)
            fn_t[...] = low.T
            for copy in copies:
                copy.wait()
            q[...] = ((dot(low, w[:, :D]) + vec[2:3]) * (LOG2E * HEAD**-0.5)).astype(bf16)
            k[...] = dot(low, w[:, D : 2 * D]).astype(bf16)
            v[...] = (dot(low, w[:, 2 * D :]) + vec[3:4]).astype(bf16)

        lane = lax.broadcasted_iota(jnp.int32, (LEN, PAIR), 1)
        mine_cols = pl.ds(pl.multiple_of(p * PAIR, PAIR), PAIR)
        vt = v[:, mine_cols].T
        keys = k[:, mine_cols]
        queries = q[:, mine_cols]
        parts = []
        for h in range(2):
            mine = (lane < HEAD) if h == 0 else (lane >= HEAD)
            scores = dot(jnp.where(mine, keys, 0).astype(bf16), queries, NT) + bias[...]
            e = jnp.exp2(scores - jnp.max(scores, 0, keepdims=True))
            rate = 1.0 / jnp.sum(e, 0, keepdims=True)
            low = e.astype(bf16)
            expo[h] = low
            inv[0, h : h + 1] = rate
            parts.append(dot(vt[HEAD * h : HEAD * h + HEAD], low) * rate)
        both = jnp.concatenate(parts, 0)
        att_t[...] = both.astype(bf16)
        att[...] = both.T.astype(bf16)

    seq = pl.BlockSpec((LEN, D), lambda p, m: (at_seq, 0))
    ins = [tokens, vec, segs.reshape(seqs, 1, LEN), *pieces]
    alias = {}
    if before is not None:
        alias = {1 + len(ins) + i: i for i in range(held)}
        ins += before
    return order.run(
        "attend",
        body,
        ins,
        [
            seq,
            whole((8, D)),
            pl.BlockSpec((1, 1, LEN), lambda p, m: (at_seq, 0, 0)),
        ]
        + [ANY] * (count + held),
        [
            shape((D, rows), bf16),
            shape((rows, D), bf16),
            shape((rows, D), bf16),
            shape((rows, D), bf16),
            shape((rows, D), bf16),
            shape((D, rows), bf16),
            shape((seqs * HEADS, LEN, LEN), bf16),
            shape((seqs * PAIRS, 8, LEN), f32),
        ],
        [
            pl.BlockSpec((D, LEN), lambda p, m: (0, at_seq)),
            seq,
            seq,
            seq,
            pl.BlockSpec((LEN, PAIR), lambda p, m: (at_seq, p)),
            pl.BlockSpec((PAIR, LEN), lambda p, m: (p, at_seq)),
            pl.BlockSpec((2, LEN, LEN), lambda p, m: (at_seq * PAIRS + p, 0, 0)),
            pl.BlockSpec((1, 8, LEN), lambda p, m: (at_seq * PAIRS + p, 0, 0)),
        ],
        (PAIRS,),
        [
            pltpu.VMEM((LEN, LEN), f32),
            pltpu.VMEM((D, 3 * D), bf16),
            pltpu.SemaphoreType.DMA((count,)),
        ],
        LEN * D * D * 3 + LEN * LEN * D * 8,
        28,
        alias,
    )


def vectors(order, sources):
    n, share = len(sources), sources[0].shape[1]

    def body(meta, *refs):
        srcs, (vec, ub) = refs[:n], refs[n:]
        rows = []
        for s in range(n):
            total = jnp.zeros((12, share), f32)
            for i in range(n):
                total = jnp.where(meta[15 + i] == s, srcs[i][...].astype(f32), total)
            rows.append(total)
        vec[...] = jnp.concatenate([r[:8] for r in rows], 1)
        ub[...] = jnp.concatenate([r[8 + i : 9 + i] for r in rows for i in range(4)], 1)

    outs = [shape((8, D), f32), shape((1, FF), f32)]
    return order.small("vectors", body, sources, outs, True)


def gelu_both(x):
    size = jnp.abs(x) * 0.7071067811865476
    t = 1.0 / (1.0 + 0.3275911 * size)
    bell = jnp.exp2(x * x * (-0.5 * LOG2E))
    poly = 0.5 * 1.061405429
    for c in (-1.453152027, 1.421413741, -0.284496736, 0.254829592):
        poly = poly * t + 0.5 * c
    tail = poly * t * bell
    cdf = jnp.where(x >= 0, 1.0 - tail, tail)
    return x * cdf, cdf + x * bell * 0.3989422804014327


def feed(order, attended, tokens, out_grad, live, vec, up_bias, pieces):
    count = len(pieces)
    rows = tokens.shape[0]

    def body(meta, att, tok, og, seg, vec, ub, *rest):
        pieces, (mid, sn_t, hid, slope, gb, down_sum, w, sems) = rest[:count], rest[count:]
        first_step(fill(meta, pieces, w, sems))
        m = tok[...].astype(f32) + dot(att[...], w[:, FF:]) + vec[4:5]
        mid[...] = m
        low = (standard(m)[0] * vec[5:6] + vec[6:7]).astype(bf16)
        sn_t[...] = low.T
        grad = jnp.where(as_column(seg[0]) >= 0, og[...].astype(f32), 0.0)
        gb[...] = grad.astype(bf16)

        @pl.when(pl.program_id(0) == 0)
        def _():
            down_sum[...] = jnp.zeros_like(down_sum)

        down_sum[0:1] += column_sum(grad)
        for at in range(0, FF, 512):
            pre = dot(low, w[:, at : at + 512]) + ub[:, at : at + 512]
            act, der = gelu_both(pre)
            hid[:, at : at + 512] = act.astype(bf16)
            slope[:, at : at + 512] = der.astype(bf16)

    blk = rows_block((TILE, D))
    wide = rows_block((TILE, FF))
    return order.run(
        "feed",
        body,
        [attended, tokens, out_grad, live, vec, up_bias, *pieces],
        [blk, blk, blk, rows_block((1, 1, TILE)), whole((8, D)), whole((1, FF))] + [ANY] * count,
        [
            shape((rows, D), f32),
            shape((D, rows), bf16),
            shape((rows, FF), bf16),
            shape((rows, FF), bf16),
            shape((rows, D), bf16),
            shape((8, D), f32),
        ],
        [blk, pl.BlockSpec((D, TILE), lambda at, m: (0, at)), wide, wide, blk, whole((8, D))],
        (rows // TILE,),
        [pltpu.VMEM((D, FF + D), bf16), pltpu.SemaphoreType.DMA((count,))],
        rows * D * (FF + D) * 3,
        32,
    )


def down_out(order, hidden, mid, vec, pieces):
    count = len(pieces)
    rows = hidden.shape[0]

    def body(meta, hid, mid, vec, *rest):
        pieces, (out, w, sems) = rest[:count], rest[count:]
        first_step(fill(meta, pieces, w, sems))
        out[...] = (mid[...] + dot(hid[...], w[...]) + vec[7:8]).astype(bf16)

    blk = rows_block((TILE, D))
    return order.run(
        "down_out",
        body,
        [hidden, mid, vec, *pieces],
        [rows_block((TILE, FF)), blk, whole((8, D))] + [ANY] * count,
        [shape((rows, D), bf16)],
        [blk],
        (rows // TILE,),
        [pltpu.VMEM((FF, D), bf16), pltpu.SemaphoreType.DMA((count,))],
        rows * D * FF,
        24,
    )[0]


def normal_grad(grad, gain, hat, rate):
    inner = grad * gain
    return rate * (
        inner
        - jnp.mean(inner, -1, keepdims=True)
        - hat * jnp.mean(inner * hat, -1, keepdims=True)
    )


def back(order, slope, mid, gb, vec, downs, pieces):
    nd, count = len(downs), len(pieces)
    rows = gb.shape[0]

    def body(meta, slope, mid, gb, vec, *rest):
        downs, pieces, rest = rest[:nd], rest[nd : nd + count], rest[nd + count :]
        gpre, gmid, gattn, gatt, sums, up_sum, wd, w, sems_d, sems = rest
        first_step(fill(meta, downs, wd, sems_d) + fill(meta, pieces, w, sems))

        @pl.when(pl.program_id(0) == 0)
        def _():
            sums[...] = jnp.zeros_like(sums)
            up_sum[...] = jnp.zeros_like(up_sum)

        grad = None
        for at in range(0, FF, 512):
            cols = slice(at, at + 512)
            low = (dot(gb[...], wd[cols], NT) * slope[:, cols].astype(f32)).astype(bf16)
            gpre[:, cols] = low
            up_sum[0:1, cols] += column_sum(low.astype(f32))
            term = dot(low, w[:, cols], NT)
            grad = term if grad is None else grad + term
        hat, rate = standard(mid[...])
        sums[0:1] += column_sum(grad * hat)
        sums[1:2] += column_sum(grad)
        g = gb[...].astype(f32) + normal_grad(grad, vec[5:6], hat, rate)
        gmid[...] = g
        low = g.astype(bf16)
        gattn[...] = low
        sums[2:3] += column_sum(low.astype(f32))
        gatt[...] = dot(low, w[:, FF:], NT).astype(bf16)

    blk = rows_block((TILE, D))
    wide = rows_block((TILE, FF))
    return order.run(
        "back",
        body,
        [slope, mid, gb, vec, *downs, *pieces],
        [wide, blk, blk, whole((8, D))] + [ANY] * (nd + count),
        [
            shape((rows, FF), bf16),
            shape((rows, D), f32),
            shape((rows, D), bf16),
            shape((rows, D), bf16),
            shape((8, D), f32),
            shape((8, FF), f32),
        ],
        [wide, blk, blk, blk, whole((8, D)), whole((8, FF))],
        (rows // TILE,),
        [
            pltpu.VMEM((FF, D), bf16),
            pltpu.VMEM((D, FF + D), bf16),
            pltpu.SemaphoreType.DMA((nd,)),
            pltpu.SemaphoreType.DMA((count,)),
        ],
        rows * D * (2 * FF + D),
        32,
    )


def attend_back(order, fn_t, q, k, v, att_t, gatt, expo, inv, first, pairs):
    rows = q.shape[0]
    count = rows // LEN
    width = PAIR * pairs

    def body(meta, q, k, v, att_t, g, expo, inv, fn_t, *rest):
        dq, dk, dv, send, own, near, far, sums, grads, held, sems = rest
        s, p = pl.program_id(0), pl.program_id(1)

        def moves():
            return [
                pltpu.make_async_copy(
                    fn_t.at[pl.ds(pl.multiple_of(meta[5 + j] * BAND, BAND), BAND)],
                    held.at[pl.ds(j * BAND, BAND)],
                    sems.at[j],
                )
                for j in range(8)
            ]

        @pl.when((s == 0) & (p == 0))
        def _():
            for copy in moves():
                copy.start()

        queries, values = q[...], v[...]
        kt = k[...].T
        gt = g[...].astype(f32).T
        both = att_t[...].astype(f32) * gt
        parts, dks, dvs = [], [], []
        for h in range(2):
            at = slice(HEAD * h, HEAD * h + HEAD)
            rate = inv[0, h : h + 1]
            delta = jnp.sum(both[at], 0, keepdims=True) * rate
            scaled = (gt[at] * rate).astype(bf16)
            e = expo[h]
            ds = (e.astype(f32) * (dot(values[:, at], scaled) - delta)).astype(bf16)
            parts.append(dot(kt[at], ds))
            dvs.append(dot(e, scaled, NT))
            dks.append(dot(ds, queries[:, at]) * LN2)
        three = (
            (jnp.concatenate(parts, 0).T * HEAD**-0.5).astype(bf16),
            jnp.concatenate(dks, 1).astype(bf16),
            jnp.concatenate(dvs, 1).astype(bf16),
        )
        mine = pl.ds(pl.multiple_of(s * LEN, LEN), LEN)
        for i, (ref, value) in enumerate(zip((dq, dk, dv), three)):
            ref[...] = value
            grads[mine, pl.ds(pl.multiple_of(i * width + p * PAIR, PAIR), PAIR)] = value

        @pl.when((s == count - 1) & (p == pairs - 1))
        def _():
            for copy in moves():
                copy.wait()
            right = grads[...]
            send[...] = dot(held[: 4 * BAND], right).astype(bf16)
            kept = dot(held[4 * BAND :], right).astype(bf16)
            own[...] = kept[:BAND]
            near[...] = kept[BAND : 2 * BAND]
            far[...] = kept[2 * BAND :]
            sums[...] = jnp.broadcast_to(column_sum(right.astype(f32)), sums.shape)

    blk = pl.BlockSpec((LEN, PAIR), lambda s, p, m: (s, p + first))
    out = pl.BlockSpec((LEN, PAIR), lambda s, p, m: (s, p))
    widths = [4 * BAND, BAND, BAND, 2 * BAND]
    return order.run(
        "attend_back",
        body,
        [q, k, v, att_t, gatt, expo, inv, fn_t],
        [blk] * 3
        + [
            pl.BlockSpec((PAIR, LEN), lambda s, p, m: (p + first, s)),
            blk,
            pl.BlockSpec((2, LEN, LEN), lambda s, p, m: (s * PAIRS + p + first, 0, 0)),
            pl.BlockSpec((1, 8, LEN), lambda s, p, m: (s * PAIRS + p + first, 0, 0)),
            ANY,
        ],
        [shape((rows, width), bf16)] * 3
        + [shape((n, 3 * width), bf16) for n in widths]
        + [shape((8, 3 * width), f32)],
        [out] * 3 + [whole((n, 3 * width)) for n in widths] + [whole((8, 3 * width))],
        (count, pairs),
        [
            pltpu.VMEM((rows, 3 * width), bf16),
            pltpu.VMEM((D, rows), bf16),
            pltpu.SemaphoreType.DMA((8,)),
        ],
        rows * LEN * PAIR * pairs * 9 + rows * D * 3 * width,
        28,
    )


def grad_first(order, dqkv, tokens, gmid, vec, pieces):
    count = len(pieces)
    rows = tokens.shape[0]
    flat = [t for chunk in dqkv for t in chunk]
    starts = [0]
    for chunk in dqkv:
        starts.append(starts[-1] + chunk[0].shape[1])

    def body(meta, tok, gmid, vec, *rest):
        grads, rest = rest[: len(flat)], rest[len(flat) :]
        pieces, (out, sums, w, sems) = rest[:count], rest[count:]
        first_step(fill(meta, pieces, w, sems))

        @pl.when(pl.program_id(0) == 0)
        def _():
            sums[...] = jnp.zeros_like(sums)

        total = None
        for i, ref in enumerate(grads):
            at = (i % 3) * D + starts[i // 3]
            term = dot(ref[...], w[:, at : at + ref.shape[1]], NT)
            total = term if total is None else total + term
        hat, rate = standard(tok[...].astype(f32))
        sums[0:1] += column_sum(total * hat)
        sums[1:2] += column_sum(total)
        out[...] = (gmid[...] + normal_grad(total, vec[0:1], hat, rate)).astype(bf16)

    blk = rows_block((TILE, D))
    return order.run(
        "grad_first",
        body,
        [tokens, gmid, vec, *flat, *pieces],
        [blk, blk, whole((8, D))] + [rows_block((TILE, t.shape[1])) for t in flat] + [ANY] * count,
        [shape((rows, D), bf16), shape((8, D), f32)],
        [blk, whole((8, D))],
        (rows // TILE,),
        [pltpu.VMEM((D, 3 * D), bf16), pltpu.SemaphoreType.DMA((count,))],
        rows * D * D * 3,
        24,
    )


def down_grad(order, hidden, gb):
    rows = gb.shape[0]
    band = FF // 8

    def body(meta, hid, gb, send, own, near, far):
        low = dot(hid[...], gb[...], TN).astype(bf16)
        at = pl.program_id(0)

        @pl.when(at < 4)
        def _():
            send[...] = low

        @pl.when(at == 4)
        def _():
            own[...] = low

        @pl.when(at == 5)
        def _():
            near[...] = low

        @pl.when(at >= 6)
        def _():
            far[...] = low

    return order.run(
        "down_grad",
        body,
        [hidden, gb],
        [pl.BlockSpec((rows, band), lambda j, m: (0, m[5 + j])), whole((rows, D))],
        [shape((n * band, D), bf16) for n in (4, 1, 1, 2)],
        [
            pl.BlockSpec((band, D), lambda j, m: (jnp.minimum(j, 3), 0)),
            whole((band, D)),
            whole((band, D)),
            pl.BlockSpec((band, D), lambda j, m: (jnp.maximum(j - 6, 0), 0)),
        ],
        (8,),
        [],
        rows * D * FF,
        24,
    )


def weight_grad(name, order, left, first, recv):
    rows = left[0][0].shape[1]
    width = min(r.shape[1] for _, rights in left for r in rights)
    width = min(width, D)
    plan = []
    flat = []
    for i, (_, rights) in enumerate(left):
        for r in rights:
            for at in range(r.shape[1] // width):
                plan.append((i, len(flat), at))
            flat.append(r)
    steps = len(plan)
    nl, nr = len(left), len(flat)
    total = steps * width

    def body(meta, *rest):
        lefts, rights, rest = rest[:nl], rest[nl : nl + nr], rest[nl + nr :]
        got = None
        if recv is not None:
            got, rest = rest[0], rest[1:]
        nout = 1 if recv is None else 3
        outs, rest = rest[:nout], rest[nout:]
        held, sems = rest
        step = pl.program_id(0)

        @pl.when(step == 0)
        def _():
            copies = []
            for i in range(nl):
                for j in range(4):
                    start = pl.multiple_of(meta[first + j] * BAND, BAND)
                    copies.append(
                        pltpu.make_async_copy(
                            lefts[i].at[pl.ds(start, BAND)],
                            held.at[i, pl.ds(j * BAND, BAND)],
                            sems.at[i * 4 + j],
                        )
                    )
            for copy in copies:
                copy.start()
            for copy in copies:
                copy.wait()

        def emit(which, right):
            value = dot(held[which], right)
            if recv is None:
                outs[0][...] = value.astype(bf16)
                return
            low = (value + got[...].astype(f32)).astype(bf16)
            outs[0][...] = low[:BAND]
            outs[1][...] = low[BAND : 2 * BAND]
            outs[2][...] = low[2 * BAND :]

        begin = 0
        for r in range(nr):
            mine = [s for s, p in enumerate(plan) if p[1] == r]

            @pl.when((step >= mine[0]) & (step <= mine[-1]))
            def _(r=r):
                which = plan[[s for s, p in enumerate(plan) if p[1] == r][0]][0]
                emit(which, rights[r][...])

    def right_spec(r):
        mine = [s for s, p in enumerate(plan) if p[1] == r]
        return pl.BlockSpec((rows, width), lambda s, m: (0, jnp.clip(s - mine[0], 0, len(mine) - 1)))

    cols = lambda n: pl.BlockSpec((n, width), lambda s, m: (0, s))
    ins = [l for l, _ in left] + flat + ([] if recv is None else [recv])
    in_specs = [ANY] * nl + [right_spec(r) for r in range(nr)]
    if recv is None:
        outs, out_specs = [shape((4 * BAND, total), bf16)], [cols(4 * BAND)]
    else:
        in_specs.append(cols(4 * BAND))
        outs = [shape((n * BAND, total), bf16) for n in (1, 1, 2)]
        out_specs = [cols(n * BAND) for n in (1, 1, 2)]
    return order.run(
        name,
        body,
        ins,
        in_specs,
        outs,
        out_specs,
        (steps,),
        [pltpu.VMEM((nl, 4 * BAND, rows), bf16), pltpu.SemaphoreType.DMA((4 * nl,))],
        rows * 4 * BAND * total,
        24,
    )


class Links:
    def __init__(self, mesh):
        self.wide, self.narrow = mesh.shape["wide"], mesh.shape["narrow"]
        self.paired = self.wide == 8 and self.narrow == 4

    def move(self, value, target):
        pairs = []
        for w in range(self.wide):
            for n in range(self.narrow):
                to = target(w, n)
                if to is not None:
                    pairs.append((w * self.narrow + n, to[0] * self.narrow + to[1]))
        return lax.ppermute(value, ("wide", "narrow"), pairs)

    def swap(self, value):
        return self.move(value, lambda w, n: (w ^ 1, n))

    def near(self, value):
        return self.move(value, lambda w, n: (w, n ^ (1 + (w & 1))))

    def far(self, value):
        return self.move(value, lambda w, n: (w, n ^ (2 - (w & 1))))

    def inward(self, value):
        return self.move(value, lambda w, n: {0: (w + 2, n), 3: (w - 2, n)}.get(w >> 1))

    def across(self, value):
        return self.move(value, lambda w, n: {1: (w + 2, n), 2: (w - 2, n)}.get(w >> 1))

    def outward(self, value):
        return self.move(value, lambda w, n: {1: (w - 2, n), 2: (w + 2, n)}.get(w >> 1))

    def along(self, value, step):
        return self.move(value, lambda w, n: (w, n ^ step))

    def level(self, value, step):
        return self.move(value, lambda w, n: (w ^ (2 * step), n))

    def meta(self):
        table = []
        for w in range(self.wide):
            for n in range(self.narrow):
                core, level = w & 1, w >> 1
                a, b, d = n ^ (1 + core), n ^ (2 - core), n ^ 3
                if not self.paired:
                    row = [0] * 5 + list(range(8)) + [0, 0] + list(range(self.narrow))
                else:
                    row = [2 * n, 2 * a, 2 * d + core, 2 * b, 2 * d + 1 - core]
                    row += [2 * s + 1 - core for s in (n, a, b, d)]
                    row += [2 * s + core for s in (n, b, a, d)]
                    row += [core, int(level in (1, 2)), n, n ^ 1, n ^ 2, d]
                table.append(row)
        place = lax.axis_index(("wide", "narrow"))
        return lax.dynamic_index_in_dim(jnp.array(table, jnp.int32), place, keepdims=False)

    def shares(self, packed):
        if not self.paired:
            sources = lax.all_gather(packed, "narrow", axis=0)
            return [sources[i] for i in range(self.narrow)]
        return [packed] + [self.along(packed, i) for i in (1, 2, 3)]

    def sum_all(self, value):
        if not self.paired:
            return lax.psum(value, ("wide", "narrow"))
        value = value + self.swap(value)
        value = value + self.along(value, 1) + self.along(value, 2) + self.along(value, 3)
        return value + self.level(value, 1) + self.level(value, 2) + self.level(value, 3)

    def sum_levels(self, own):
        groups = [list(range(c, self.wide, 2)) for c in range(2)]
        return lax.psum(own, "wide", axis_index_groups=groups)

    def whole_sum(self, sent, kept):
        full = jnp.concatenate([sent, *kept], 0)
        mine = lax.psum_scatter(full, "narrow", scatter_dimension=0, tiled=True)
        mine = lax.psum(mine, "wide")
        half = mine.shape[0] // 2
        return mine[:half], mine[half:]


def layer(links, *args):
    (
        tokens,
        segment_ids,
        out_grad,
        first_gain,
        first_shift,
        query_weight,
        query_bias,
        key_weight,
        value_weight,
        value_bias,
        output_weight,
        output_bias,
        second_gain,
        second_shift,
        up_weight,
        up_bias,
        down_weight,
        down_bias,
    ) = args
    order = Order(links.meta())
    paired = links.paired
    share = first_gain.shape[0]
    gather = lambda v: [lax.all_gather(v, "narrow", axis=0, tiled=True)]
    small = (
        first_gain,
        first_shift,
        query_bias,
        value_bias,
        output_bias,
        second_gain,
        second_shift,
        down_bias,
    )
    live = segment_ids.reshape(-1, 1, TILE)

    pack_one = pack(order, [query_weight, key_weight, value_weight])
    shares = links.shares(jnp.concatenate([*small, up_bias]).reshape(-1, share))
    vec, up_b = vectors(order, shares)
    if paired:
        near_one = links.near(pack_one)
        far_one = links.far(copies(order, [near_one])[0])
        w_one = [pack_one, near_one, far_one, links.swap(near_one), links.swap(far_one)]
    else:
        w_one = gather(pack_one)
    pack_two = pack(order, [up_weight, output_weight])
    kept = attend(order, tokens, vec, segment_ids, w_one, 0, None)
    if paired:
        near_two = links.near(pack_two)
        far_two = links.far(copies(order, [near_two])[0])
        w_two = [pack_two, near_two, far_two, links.swap(near_two), links.swap(far_two)]
    else:
        w_two = gather(pack_two)
    for s in range(1, tokens.shape[0] // LEN):
        kept = attend(order, tokens, vec, segment_ids, w_one, s, list(kept))
    fn_t, q, k, v, att, att_t, expo, inv = kept
    if paired:
        down_half, down_copy = copies(order, [down_weight], [down_weight])
        near_down = links.near(down_copy)
        far_down = links.along(down_half, 3)
        w_down = [down_weight, near_down, far_down, links.swap(near_down), links.swap(far_down)]
    else:
        w_down = gather(down_weight)
    mid, sn_t, hidden, slope, gb, down_sum = feed(
        order, att, tokens, out_grad, live, vec, up_b, w_two
    )

    d_send, d_own, d_near, d_far = down_grad(order, hidden, gb)
    gpre, gmid, gattn, gatt, mid_sums, up_sum = back(order, slope, mid, gb, vec, w_down, w_two)
    lefts = [(sn_t, [gpre]), (att_t, [gattn])]
    if paired:
        high = d_own.shape[0]
        d_got = links.swap(d_send)
        (d_far,) = sums_of(order, [(2 * high, [(d_far, 0), (d_got, 2 * high)])])
        d_got2 = links.near(d_far)
    s_send = weight_grad("second_send", order, lefts, 5, None)[0]
    s_got = links.swap(s_send) if paired else jnp.zeros_like(s_send)

    chunks, first = [], 0
    for c, pairs in enumerate(CHUNKS):
        chunks.append(attend_back(order, fn_t, q, k, v, att_t, gatt, expo, inv, first, pairs))
        first += pairs
        if c == 0:
            if paired:
                c_send, c_own, c_near, c_far = chunks[0][3:7]
                d_near, d_own = sums_of(
                    order,
                    [
                        (high, [(d_near, 0), (d_got, high), (d_got2, high)]),
                        (high, [(d_own, 0), (d_got, 0), (d_got2, 0)]),
                    ],
                )
                d_got3 = links.far(d_near)
                c_got = links.swap(c_send)
            s_own, s_near, s_far = weight_grad("second_keep", order, lefts, 9, s_got)
            if paired:
                s_got2 = links.near(s_far)
                d_own, c_far = sums_of(
                    order,
                    [
                        (high, [(d_own, 0), (d_got3, 0)]),
                        (2 * BAND, [(c_far, 0), (c_got, 2 * BAND)]),
                    ],
                )
                d_got = links.inward(d_own)
                c_got2 = links.near(c_far)
    dqkv = [chunk[:3] for chunk in chunks]
    if paired:
        e_send, e_own, e_near, e_far = chunks[1][3:7]
        e_got = links.swap(e_send)
        s_near, s_own, d_own = sums_of(
            order,
            [
                (BAND, [(s_near, 0), (s_got2, BAND)]),
                (BAND, [(s_own, 0), (s_got2, 0)]),
                (high, [(d_own, 0), (d_got, 0)]),
            ],
        )
        s_got = links.far(s_near)
        d_got = links.across(d_own)
        c_near, c_own, e_far = sums_of(
            order,
            [
                (BAND, [(c_near, 0), (c_got, BAND), (c_got2, BAND)]),
                (BAND, [(c_own, 0), (c_got, 0), (c_got2, 0)]),
                (2 * BAND, [(e_far, 0), (e_got, 2 * BAND)]),
            ],
        )
        c_got = links.far(c_near)
        e_got2 = links.near(e_far)
    input_grad, first_sums = grad_first(order, dqkv, tokens, gmid, vec, w_one)
    cols = lambda c, i: slice(i * PAIR * CHUNKS[c], (i + 1) * PAIR * CHUNKS[c])
    bias = lambda i: jnp.concatenate([chunks[c][7][:1, cols(c, i)] for c in range(2)], 1)
    total = links.sum_all(
        jnp.concatenate(
            [
                first_sums[:2],
                bias(0),
                bias(2),
                mid_sums[2:3],
                mid_sums[:2],
                down_sum[:1],
                up_sum[:1].reshape(4, D),
            ],
            0,
        )
    )
    if paired:
        e_near, e_own, c_own, s_own, d_own = sums_of(
            order,
            [
                (BAND, [(e_near, 0), (e_got, BAND), (e_got2, BAND)]),
                (BAND, [(e_own, 0), (e_got, 0), (e_got2, 0)]),
                (BAND, [(c_own, 0), (c_got, 0)]),
                (BAND, [(s_own, 0), (s_got, 0)]),
                (high, [(d_own, 0), (d_got, 0)]),
            ],
        )
        e_got = links.far(e_near)
        c_got = links.level(c_own, 1)
        s_own = links.sum_levels(s_own)
        d_got = links.outward(d_own)
    layer_out = down_out(order, hidden, mid, vec, w_down)
    if paired:
        e_own, c_own = sums_of(
            order,
            [(BAND, [(e_own, 0), (e_got, 0)]), (BAND, [(c_own, 0), (c_got, 0)])],
        )
        e_got, c_got = links.level(e_own, 1), links.level(c_own, 2)
        d_own = pick(order, d_own, d_got)
        d_pair = (d_own, links.swap(d_own))
        e_own, c_own = sums_of(
            order,
            [(BAND, [(e_own, 0), (e_got, 0)]), (BAND, [(c_own, 0), (c_got, 0)])],
        )
        e_got = links.level(e_own, 2)
        c_pair = (c_own, links.swap(c_own))
        s_pair = (s_own, links.swap(s_own))
        (down_weight_grad,) = finish(order, [d_pair], [(D, [(0, 0, D)])])
        (e_own,) = sums_of(order, [(BAND, [(e_own, 0), (e_got, 0)])])
        e_pair = (e_own, links.swap(e_own))
    else:
        d_pair = links.whole_sum(d_send, (d_own, d_near, d_far))
        s_pair = links.whole_sum(s_send, (s_own, s_near, s_far))
        c_pair, e_pair = [links.whole_sum(c[3], c[4:7]) for c in chunks]
        (down_weight_grad,) = finish(order, [d_pair], [(D, [(0, 0, D)])])
    first_grads = finish(
        order,
        [c_pair, e_pair],
        [(D, [(c, cols(c, i).start, PAIR * CHUNKS[c]) for c in range(2)]) for i in range(3)],
    )
    up_weight_grad, output_weight_grad = finish(
        order, [s_pair], [(FF, [(0, 0, FF)]), (D, [(0, FF, D)])]
    )

    n = lax.axis_index("narrow")
    mine = lax.dynamic_slice_in_dim(total[:8], n * share, share, 1)
    up_share = up_bias.shape[0]
    up_mine = lax.dynamic_slice_in_dim(total[8:].reshape(FF), n * up_share, up_share)
    return (
        layer_out,
        input_grad,
        mine[0],
        mine[1],
        first_grads[0],
        mine[2],
        first_grads[1],
        first_grads[2],
        mine[3],
        output_weight_grad,
        mine[4],
        mine[5],
        mine[6],
        up_weight_grad,
        up_mine,
        down_weight_grad,
        mine[7],
    )


def solution(mesh):
    rows, vector, matrix = P(("wide", "narrow"), None), P("narrow"), P("narrow", None)
    in_specs = (rows, P(("wide", "narrow")), rows) + tuple(
        matrix if i in (2, 4, 5, 7, 11, 13) else vector for i in range(15)
    )
    out_specs = (rows, rows) + in_specs[3:]
    return jax.shard_map(
        functools.partial(layer, Links(mesh)),
        mesh=mesh,
        in_specs=in_specs,
        out_specs=out_specs,
        check_vma=False,
    )
```

```python
import functools

import jax
import jax.numpy as jnp
from jax import lax
from jax.experimental import pallas as pl
from jax.experimental.pallas import tpu as pltpu
from jax.sharding import PartitionSpec as P

D = 768
HEADS = 12
HEAD = 64
LEN = 512
FF = 3072
EPSILON = 1e-06
TILE = 256
BAND = D // 8
PAIR = 2 * HEAD
PAIRS = HEADS // 2
CHUNKS = (4, 2)
LOG2E = 1.4426950408889634
LN2 = 0.6931471805599453

bf16 = jnp.bfloat16
f32 = jnp.float32
NN = (((1,), (0,)), ((), ()))
NT = (((1,), (1,)), ((), ()))
TN = (((0,), (0,)), ((), ()))
ANY = pl.BlockSpec(memory_space=pl.ANY)


def dot(left, right, dims=NN):
    return lax.dot_general(left, right, dims, preferred_element_type=f32)


def shape(dims, kind):
    return jax.ShapeDtypeStruct(dims, kind)


def column_sum(values):
    return jnp.sum(values, 0, keepdims=True)


def whole(dims):
    return pl.BlockSpec(dims, lambda *at: (0,) * len(dims))


def rows_block(dims):
    return pl.BlockSpec(dims, lambda at, *rest: (at,) + (0,) * (len(dims) - 1))


class Order:
    def __init__(self, meta):
        self.meta, self.last, self.far = meta, [], []

    def run(
        self,
        name,
        body,
        ins,
        in_specs,
        outs,
        out_specs,
        grid,
        scratch,
        macs,
        limit,
        alias={},
        near=False,
    ):
        moved = sum(a.size * a.dtype.itemsize for a in ins)
        moved += sum(o.size * o.dtype.itemsize for o in outs)
        used, extra = len(ins), len(self.last)

        def inner(meta, *refs):
            body(meta, *refs[:used], *refs[used + extra :])

        ins = [
            a if spec is ANY else pltpu.with_memory_space_constraint(a, pltpu.HBM)
            for a, spec in zip(ins, in_specs)
        ]
        if not near:
            outs = [pltpu.HBM(o.shape, o.dtype) for o in outs]
        got = pl.pallas_call(
            inner,
            out_shape=outs,
            grid_spec=pltpu.PrefetchScalarGridSpec(
                num_scalar_prefetch=1,
                grid=grid,
                in_specs=[*in_specs] + [ANY] * extra,
                out_specs=out_specs,
                scratch_shapes=scratch,
            ),
            input_output_aliases=alias,
            compiler_params=pltpu.CompilerParams(vmem_limit_bytes=limit * 2**20),
            cost_estimate=pl.CostEstimate(flops=1, bytes_accessed=1 if near else 4 * 10**8, transcendentals=0),
            name=name,
        )(self.meta, *ins, *self.tokens())
        self.last = [got[0]]
        if not near:
            self.far += got
        return got

    def tokens(self):
        return [
            pltpu.with_memory_space_constraint(t, pltpu.HBM)
            if any(t is a for a in self.far)
            else t
            for t in self.last
        ]

    def small(self, name, body, ins, outs, scratch=()):
        used, extra = len(ins), len(self.last)
        far = [any(a is b for b in self.far) for a in ins]
        held = [i for i in range(used) if far[i]]
        wait = len(held)

        def inner(meta, *refs):
            inputs, refs = list(refs[:used]), refs[used + extra :]
            outputs, refs = refs[: len(outs)], refs[len(outs) :]
            buffers, rest = refs[:wait], refs[wait:]
            moves = []
            for n, i in enumerate(held):
                moves.append(pltpu.make_async_copy(inputs[i], buffers[n], rest[0].at[n]))
                inputs[i] = buffers[n]
            for move in moves:
                move.start()
            for move in moves:
                move.wait()
            body(meta, *inputs, *outputs, *rest[1 if wait else 0 :])

        vmem = pl.BlockSpec(memory_space=pltpu.VMEM)
        got = pl.pallas_call(
            inner,
            out_shape=outs,
            in_specs=[pl.BlockSpec(memory_space=pltpu.SMEM)]
            + [ANY if f else vmem for f in far]
            + [ANY] * extra,
            out_specs=[vmem] * len(outs),
            scratch_shapes=[pltpu.VMEM(ins[i].shape, ins[i].dtype) for i in held]
            + ([pltpu.SemaphoreType.DMA((wait,))] if wait else [])
            + list(scratch),
            compiler_params=pltpu.CompilerParams(vmem_limit_bytes=20 * 2**20),
            cost_estimate=pl.CostEstimate(flops=1, bytes_accessed=1, transcendentals=0),
            name=name,
        )(
            self.meta,
            *[
                pltpu.with_memory_space_constraint(a, pltpu.HBM) if f else a
                for a, f in zip(ins, far)
            ],
            *self.tokens(),
        )
        self.last = [got[0]]
        return got


def fill(meta, pieces, target, sems, cols=None):
    count = 1 if len(pieces) == 1 else len(pieces)
    half = target.shape[0] // 8
    copies = []
    for i in range(count):
        place = meta[19] if count == 4 and i == 2 else meta[i]
        start = pl.multiple_of(place * half, half) if count > 1 else 0
        rows = pl.ds(start, pieces[i].shape[0])
        src, dst = pieces[i], target.at[rows]
        if cols is not None:
            src, dst = src.at[:, cols], target.at[rows, cols]
        copies.append(pltpu.make_async_copy(src, dst, sems.at[i]))
    return copies


def first_step(copies):
    @pl.when(pl.program_id(0) == 0)
    def _():
        for copy in copies:
            copy.start()
        for copy in copies:
            copy.wait()


def as_column(row):
    return jnp.broadcast_to(row.astype(f32), (8, row.shape[1])).T[:, :1]


def standard(v):
    center = v - jnp.mean(v, -1, keepdims=True)
    rate = lax.rsqrt(jnp.mean(center * center, -1, keepdims=True) + EPSILON)
    return center * rate, rate


def pack(order, parts):
    rows = parts[0].shape[0]
    width = sum(p.shape[1] for p in parts)
    count = len(parts)

    def body(meta, *refs):
        out, sems = refs[count:]
        moves, at = [], 0
        for i, src in enumerate(refs[:count]):
            cols = out.at[:, at : at + src.shape[1]]
            moves.append(pltpu.make_async_copy(src, cols, sems.at[i]))
            at += src.shape[1]
        for move in moves:
            move.start()
        for move in moves:
            move.wait()

    return order.run(
        "pack",
        body,
        [pltpu.with_memory_space_constraint(p, pltpu.HBM) for p in parts],
        [ANY] * count,
        [shape((rows, width), bf16)],
        [whole((rows, width))],
        (1,),
        [pltpu.SemaphoreType.DMA((count,))],
        0,
        16,
        near=True,
    )[0]


def gate(order, value):
    return order.run(
        "gate",
        lambda meta, *refs: None,
        [value],
        [ANY],
        [shape(value.shape, value.dtype)],
        [ANY],
        (1,),
        [],
        0,
        16,
        alias={1: 0},
        near=True,
    )[0]


def copies(order, halves, wholes=()):
    ins = [*halves, *wholes]
    dims = [(a.shape[0] // 2, a.shape[1]) for a in halves] + [a.shape for a in wholes]

    def body(meta, *refs):
        for i, (src, dst) in enumerate(zip(refs[: len(ins)], refs[len(ins) :])):
            if i < len(halves):
                half = dst.shape[0]
                dst[...] = src[pl.ds(pl.multiple_of(meta[13] * half, half), half)]
            else:
                dst[...] = src[...]

    return order.small("copies", body, ins, [shape(d, bf16) for d in dims])


def fetch(order, *arrays):
    count = len(arrays)

    def body(meta, *refs):
        moves = [
            pltpu.make_async_copy(refs[i], refs[count + i], refs[-1].at[i]) for i in range(count)
        ]
        for move in moves:
            move.start()
        for move in moves:
            move.wait()

    return order.run(
        "fetch",
        body,
        [pltpu.with_memory_space_constraint(a, pltpu.HBM) for a in arrays],
        [ANY] * count,
        [shape(a.shape, bf16) for a in arrays],
        [whole(a.shape) for a in arrays],
        (1,),
        [pltpu.SemaphoreType.DMA((count,))],
        0,
        20,
        near=True,
    )


def sums_of(order, *plan):
    ins = []
    for parts in plan:
        for array, _ in sum(parts, []):
            if not any(array is other for other in ins):
                ins.append(array)
    where = lambda array: [i for i, other in enumerate(ins) if other is array][0]
    places = [[[(where(a), index) for a, index in terms] for terms in parts] for parts in plan]

    def body(meta, *refs):
        for parts, out in zip(places, refs[len(ins) :]):
            at = 0
            for terms in parts:
                total = None
                for i, index in terms:
                    term = refs[i][index].astype(f32)
                    total = term if total is None else total + term
                rows = slice(at, at + total.shape[-2])
                out[..., rows, :] = total.astype(bf16)
                at += total.shape[-2]

    outs = []
    for parts in plan:
        dims = [
            jax.eval_shape(lambda a, i=terms[0][1]: a[i], terms[0][0]).shape for terms in parts
        ]
        rows = sum(d[-2] for d in dims)
        outs.append(shape((*dims[0][:-2], rows, dims[0][-1]), bf16))
    return order.small("sums_of", body, ins, outs)


def pick(order, own, got):
    def body(meta, own, got, out):
        inner = jnp.full(out.shape, meta[14], jnp.int32) == 1
        out[...] = jnp.where(inner, own[...], got[...])

    return order.small("pick", body, [own, got], [shape(own.shape, bf16)])[0]


def finish(order, half, pairs, plan, last=0):
    flat = [a for pair in pairs for a in pair]

    def body(meta, *refs):
        core = meta[13]
        for (width, parts), out in zip(plan, refs[len(flat) :]):
            at = 0
            for which, block, first, cols in parts:
                for i in range(2):
                    place = core if i == 0 else 1 - core
                    rows = pl.ds(pl.multiple_of(place * half, half), half)
                    value = refs[2 * which + i][
                        block * half : (block + 1) * half, first : first + cols
                    ]
                    out[rows, at : at + cols] = value.astype(f32)
                at += cols
        if last:
            own, other = [ref[ref.shape[0] - last :].astype(f32) for ref in refs[:2]]
            refs[-1][...] = own + other

    outs = [shape((2 * half, width), f32) for width, _ in plan]
    if last:
        outs.append(shape((last, D), f32))
    return order.small("finish", body, flat, outs)


def attend(order, tokens, vec, segs, pieces, at_seq, before):
    count = len(pieces)
    rows = tokens.shape[0]
    seqs = rows // LEN
    held = 0 if before is None else len(before)

    def body(meta, tok, vec, seg, *rest):
        pieces, rest = rest[:count], rest[count + held :]
        fn_t, q, k, v, att, att_t, expo, inv, bias, w, sems = rest
        p = pl.program_id(0)

        @pl.when(p == 0)
        def _():
            copies = fill(meta, pieces, w, sems)
            for copy in copies:
                copy.start()
            row = seg[0].astype(f32)
            bias[...] = jnp.where(as_column(row) == row, 0.0, -1e30)
            normed = standard(tok[...].astype(f32))[0] * vec[0:1] + vec[1:2]
            low = normed.astype(bf16)
            fn_t[...] = low.T
            for copy in copies:
                copy.wait()
            q[...] = ((dot(low, w[:, :D]) + vec[2:3]) * (LOG2E * HEAD**-0.5)).astype(bf16)
            k[...] = dot(low, w[:, D : 2 * D]).astype(bf16)
            v[...] = (dot(low, w[:, 2 * D :]) + vec[3:4]).astype(bf16)

        lane = lax.broadcasted_iota(jnp.int32, (LEN, PAIR), 1)
        mine_cols = pl.ds(pl.multiple_of(p * PAIR, PAIR), PAIR)
        vt = v[:, mine_cols].T
        keys = k[:, mine_cols]
        queries = q[:, mine_cols]
        parts = []
        for h in range(2):
            mine = (lane < HEAD) if h == 0 else (lane >= HEAD)
            scores = dot(jnp.where(mine, keys, 0).astype(bf16), queries, NT) + bias[...]
            e = jnp.exp2(scores - jnp.max(scores, 0, keepdims=True))
            rate = 1.0 / jnp.sum(e, 0, keepdims=True)
            low = e.astype(bf16)
            expo[h] = low
            inv[0, h : h + 1] = rate
            parts.append(dot(vt[HEAD * h : HEAD * h + HEAD], low) * rate)
        both = jnp.concatenate(parts, 0)
        att_t[...] = both.astype(bf16)
        att[...] = both.T.astype(bf16)

    seq = pl.BlockSpec((LEN, D), lambda p, m: (at_seq, 0))
    ins = [tokens, vec, segs.reshape(seqs, 1, LEN), *pieces]
    alias = {}
    if before is not None:
        alias = {1 + len(ins) + i: i for i in range(held)}
        ins += before
    return order.run(
        "attend",
        body,
        ins,
        [
            seq,
            whole((8, D)),
            pl.BlockSpec((1, 1, LEN), lambda p, m: (at_seq, 0, 0)),
        ]
        + [ANY] * (count + held),
        [
            shape((D, rows), bf16),
            shape((rows, D), bf16),
            shape((rows, D), bf16),
            shape((rows, D), bf16),
            shape((rows, D), bf16),
            shape((D, rows), bf16),
            shape((seqs * HEADS, LEN, LEN), bf16),
            shape((seqs * PAIRS, 8, LEN), f32),
        ],
        [
            pl.BlockSpec((D, LEN), lambda p, m: (0, at_seq)),
            seq,
            seq,
            seq,
            pl.BlockSpec((LEN, PAIR), lambda p, m: (at_seq, p)),
            pl.BlockSpec((PAIR, LEN), lambda p, m: (p, at_seq)),
            pl.BlockSpec((2, LEN, LEN), lambda p, m: (at_seq * PAIRS + p, 0, 0)),
            pl.BlockSpec((1, 8, LEN), lambda p, m: (at_seq * PAIRS + p, 0, 0)),
        ],
        (PAIRS,),
        [
            pltpu.VMEM((LEN, LEN), f32),
            pltpu.VMEM((D, 3 * D), bf16),
            pltpu.SemaphoreType.DMA((count,)),
        ],
        LEN * D * D * 3 + LEN * LEN * D * 8,
        28,
        alias,
    )


def vectors(order, sources):
    n, share = len(sources), sources[0].shape[1]

    def body(meta, *refs):
        srcs, (vec, ub) = refs[:n], refs[n:]
        rows = []
        for s in range(n):
            total = jnp.zeros((12, share), f32)
            for i in range(n):
                total = jnp.where(meta[15 + i] == s, srcs[i][...].astype(f32), total)
            rows.append(total)
        vec[...] = jnp.concatenate([r[:8] for r in rows], 1)
        ub[...] = jnp.concatenate([r[8 + i : 9 + i] for r in rows for i in range(4)], 1)

    outs = [shape((8, D), f32), shape((1, FF), f32)]
    return order.small("vectors", body, sources, outs)


def gelu_both(x):
    size = jnp.abs(x) * 0.7071067811865476
    t = 1.0 / (1.0 + 0.3275911 * size)
    bell = jnp.exp2(x * x * (-0.5 * LOG2E))
    poly = 0.5 * 1.061405429
    for c in (-1.453152027, 1.421413741, -0.284496736, 0.254829592):
        poly = poly * t + 0.5 * c
    tail = poly * t * bell
    cdf = jnp.where(x >= 0, 1.0 - tail, tail)
    return x * cdf, cdf + x * bell * 0.3989422804014327


def feed(order, attended, tokens, out_grad, live, vec, up_bias, pieces):
    count = len(pieces)
    rows = tokens.shape[0]

    def body(meta, att, tok, og, seg, vec, ub, *rest):
        pieces, rest = rest[:count], rest[count:]
        mid, sn_t, hid, slope, gb, down_sum, w, sems, sems_up = rest
        first = fill(meta, pieces, w, sems, slice(FF, FF + D))
        others = fill(meta, pieces, w, sems_up, slice(0, FF))
        begin = pl.program_id(0) == 0

        @pl.when(begin)
        def _():
            for copy in [*first, *others]:
                copy.start()
            for copy in first:
                copy.wait()

        m = tok[...].astype(f32) + dot(att[...], w[:, FF:]) + vec[4:5]
        mid[...] = m
        low = (standard(m)[0] * vec[5:6] + vec[6:7]).astype(bf16)
        sn_t[...] = low.T
        grad = jnp.where(as_column(seg[0]) >= 0, og[...].astype(f32), 0.0)
        gb[...] = grad.astype(bf16)

        @pl.when(pl.program_id(0) == 0)
        def _():
            down_sum[...] = jnp.zeros_like(down_sum)

        down_sum[0:1] += column_sum(grad)

        @pl.when(begin)
        def _():
            for copy in others:
                copy.wait()

        for at in range(0, FF, 512):
            pre = dot(low, w[:, at : at + 512]) + ub[:, at : at + 512]
            act, der = gelu_both(pre)
            hid[:, at : at + 512] = act.astype(bf16)
            slope[:, at : at + 512] = der.astype(bf16)

    blk = rows_block((TILE, D))
    wide = rows_block((TILE, FF))
    return order.run(
        "feed",
        body,
        [attended, tokens, out_grad, live, vec, up_bias, *pieces],
        [blk, blk, blk, rows_block((1, 1, TILE)), whole((8, D)), whole((1, FF))] + [ANY] * count,
        [
            shape((rows, D), f32),
            shape((D, rows), bf16),
            shape((rows, FF), bf16),
            shape((rows, FF), bf16),
            shape((rows, D), bf16),
            shape((8, D), f32),
        ],
        [blk, pl.BlockSpec((D, TILE), lambda at, m: (0, at)), wide, wide, blk, whole((8, D))],
        (rows // TILE,),
        [pltpu.VMEM((D, FF + D), bf16)] + [pltpu.SemaphoreType.DMA((count,))] * 2,
        rows * D * (FF + D) * 3,
        32,
    )


def down_out(order, hidden, mid, vec, pieces):
    count = len(pieces)
    rows = hidden.shape[0]

    def body(meta, hid, mid, vec, *rest):
        pieces, (out, w, sems) = rest[:count], rest[count:]
        first_step(fill(meta, pieces, w, sems))
        out[...] = (mid[...] + dot(hid[...], w[...]) + vec[7:8]).astype(bf16)

    blk = rows_block((TILE, D))
    return order.run(
        "down_out",
        body,
        [hidden, mid, vec, *pieces],
        [rows_block((TILE, FF)), blk, whole((8, D))] + [ANY] * count,
        [shape((rows, D), bf16)],
        [blk],
        (rows // TILE,),
        [pltpu.VMEM((FF, D), bf16), pltpu.SemaphoreType.DMA((count,))],
        rows * D * FF,
        24,
    )[0]


def normal_grad(grad, gain, hat, rate):
    inner = grad * gain
    return rate * (
        inner
        - jnp.mean(inner, -1, keepdims=True)
        - hat * jnp.mean(inner * hat, -1, keepdims=True)
    )


def back(order, slope, mid, gb, vec, downs, pieces):
    nd, count = len(downs), len(pieces)
    rows = gb.shape[0]

    def body(meta, slope, mid, gb, vec, *rest):
        downs, pieces, rest = rest[:nd], rest[nd : nd + count], rest[nd + count :]
        gpre, gmid, gattn, gatt, sums, up_sum, wd, w, sems_d, sems = rest
        first, others = fill(meta, downs, wd, sems_d), fill(meta, pieces, w, sems)
        begin = pl.program_id(0) == 0

        @pl.when(begin)
        def _():
            for copy in [*first, *others]:
                copy.start()
            sums[...] = jnp.zeros_like(sums)
            up_sum[...] = jnp.zeros_like(up_sum)
            for copy in first:
                copy.wait()

        for at in range(0, FF, 512):
            cols = slice(at, at + 512)
            low = (dot(gb[...], wd[cols], NT) * slope[:, cols].astype(f32)).astype(bf16)
            gpre[:, cols] = low
            up_sum[0:1, cols] += column_sum(low.astype(f32))

        @pl.when(begin)
        def _():
            for copy in others:
                copy.wait()

        grad = dot(gpre[...], w[:, :FF], NT)
        hat, rate = standard(mid[...])
        sums[0:1] += column_sum(grad * hat)
        sums[1:2] += column_sum(grad)
        g = gb[...].astype(f32) + normal_grad(grad, vec[5:6], hat, rate)
        gmid[...] = g
        low = g.astype(bf16)
        gattn[...] = low
        sums[2:3] += column_sum(low.astype(f32))
        gatt[...] = dot(low, w[:, FF:], NT).astype(bf16)

    blk = rows_block((TILE, D))
    wide = rows_block((TILE, FF))
    return order.run(
        "back",
        body,
        [slope, mid, gb, vec, *downs, *pieces],
        [wide, blk, blk, whole((8, D))] + [ANY] * (nd + count),
        [
            shape((rows, FF), bf16),
            shape((rows, D), f32),
            shape((rows, D), bf16),
            shape((rows, D), bf16),
            shape((8, D), f32),
            shape((8, FF), f32),
        ],
        [wide, blk, blk, blk, whole((8, D)), whole((8, FF))],
        (rows // TILE,),
        [
            pltpu.VMEM((FF, D), bf16),
            pltpu.VMEM((D, FF + D), bf16),
            pltpu.SemaphoreType.DMA((nd,)),
            pltpu.SemaphoreType.DMA((count,)),
        ],
        rows * D * (2 * FF + D),
        32,
    )


def attend_back(order, fn_t, q, k, v, att_t, gatt, expo, inv, first, pairs):
    rows = q.shape[0]
    count = rows // LEN
    width = PAIR * pairs

    def body(meta, q, k, v, att_t, g, expo, inv, fn_t, *rest):
        dq, dk, dv, send, own, near, far, sums, grads, held, sems = rest
        s, p = pl.program_id(0), pl.program_id(1)

        def moves():
            return [
                pltpu.make_async_copy(
                    fn_t.at[pl.ds(pl.multiple_of(meta[5 + j] * BAND, BAND), BAND)],
                    held.at[pl.ds(j * BAND, BAND)],
                    sems.at[j],
                )
                for j in range(8)
            ]

        @pl.when((s == 0) & (p == 0))
        def _():
            for copy in moves():
                copy.start()

        queries, values = q[...], v[...]
        kt = k[...].T
        gt = g[...].astype(f32).T
        both = att_t[...].astype(f32) * gt
        parts, dks, dvs = [], [], []
        for h in range(2):
            at = slice(HEAD * h, HEAD * h + HEAD)
            rate = inv[0, h : h + 1]
            delta = jnp.sum(both[at], 0, keepdims=True) * rate
            scaled = (gt[at] * rate).astype(bf16)
            e = expo[h]
            ds = (e.astype(f32) * (dot(values[:, at], scaled) - delta)).astype(bf16)
            parts.append(dot(kt[at], ds))
            dvs.append(dot(e, scaled, NT))
            dks.append(dot(ds, queries[:, at]) * LN2)
        three = (
            (jnp.concatenate(parts, 0).T * HEAD**-0.5).astype(bf16),
            jnp.concatenate(dks, 1).astype(bf16),
            jnp.concatenate(dvs, 1).astype(bf16),
        )
        mine = pl.ds(pl.multiple_of(s * LEN, LEN), LEN)
        for i, (ref, value) in enumerate(zip((dq, dk, dv), three)):
            ref[...] = value
            grads[mine, pl.ds(pl.multiple_of(i * width + p * PAIR, PAIR), PAIR)] = value

        @pl.when((s == count - 1) & (p == pairs - 1))
        def _():
            for copy in moves():
                copy.wait()
            for i in range(blocks):
                right = grads[:, i * D : (i + 1) * D]
                rows_of = slice(i * BAND, (i + 1) * BAND)
                low = dot(held[...], right).astype(bf16)
                for j in range(4):
                    send[j, rows_of] = low[j * BAND : (j + 1) * BAND]
                own[rows_of] = low[4 * BAND : 5 * BAND]
                near[rows_of] = low[5 * BAND : 6 * BAND]
                for j in range(2):
                    far[j, rows_of] = low[(6 + j) * BAND : (7 + j) * BAND]
            right = grads[...]
            sums[...] = jnp.broadcast_to(column_sum(right.astype(f32)), sums.shape)

    blk = pl.BlockSpec((LEN, PAIR), lambda s, p, m: (s, p + first))
    out = pl.BlockSpec((LEN, PAIR), lambda s, p, m: (s, p))
    blocks = 3 * width // D
    bands = [(n, blocks * BAND, D) for n in (4, 2)]
    bands = [bands[0], bands[0][1:], bands[0][1:], bands[1]]
    return order.run(
        "attend_back",
        body,
        [q, k, v, att_t, gatt, expo, inv, fn_t],
        [blk] * 3
        + [
            pl.BlockSpec((PAIR, LEN), lambda s, p, m: (p + first, s)),
            blk,
            pl.BlockSpec((2, LEN, LEN), lambda s, p, m: (s * PAIRS + p + first, 0, 0)),
            pl.BlockSpec((1, 8, LEN), lambda s, p, m: (s * PAIRS + p + first, 0, 0)),
            ANY,
        ],
        [shape((rows, width), bf16)] * 3
        + [shape(d, bf16) for d in bands]
        + [shape((8, 3 * width), f32)],
        [out] * 3 + [whole(d) for d in bands] + [whole((8, 3 * width))],
        (count, pairs),
        [
            pltpu.VMEM((rows, 3 * width), bf16),
            pltpu.VMEM((D, rows), bf16),
            pltpu.SemaphoreType.DMA((8,)),
        ],
        rows * LEN * PAIR * pairs * 9 + rows * D * 3 * width,
        28,
    )


def grad_first(order, dqkv, tokens, gmid, vec, pieces):
    count = len(pieces)
    rows = tokens.shape[0]
    flat = [t for chunk in dqkv for t in chunk]
    starts = [0]
    for chunk in dqkv:
        starts.append(starts[-1] + chunk[0].shape[1])

    def body(meta, tok, gmid, vec, *rest):
        grads, rest = rest[: len(flat)], rest[len(flat) :]
        pieces, (out, sums, w, sems) = rest[:count], rest[count:]
        first_step(fill(meta, pieces, w, sems))

        @pl.when(pl.program_id(0) == 0)
        def _():
            sums[...] = jnp.zeros_like(sums)

        total = None
        for i, ref in enumerate(grads):
            at = (i % 3) * D + starts[i // 3]
            term = dot(ref[...], w[:, at : at + ref.shape[1]], NT)
            total = term if total is None else total + term
        hat, rate = standard(tok[...].astype(f32))
        sums[0:1] += column_sum(total * hat)
        sums[1:2] += column_sum(total)
        out[...] = (gmid[...] + normal_grad(total, vec[0:1], hat, rate)).astype(bf16)

    blk = rows_block((TILE, D))
    return order.run(
        "grad_first",
        body,
        [tokens, gmid, vec, *flat, *pieces],
        [blk, blk, whole((8, D))] + [rows_block((TILE, t.shape[1])) for t in flat] + [ANY] * count,
        [shape((rows, D), bf16), shape((8, D), f32)],
        [blk, whole((8, D))],
        (rows // TILE,),
        [pltpu.VMEM((D, 3 * D), bf16), pltpu.SemaphoreType.DMA((count,))],
        rows * D * D * 3,
        24,
    )


def down_grad(order, hidden, gb):
    rows = gb.shape[0]
    band = FF // 8

    def body(meta, hid, gb, send, own, near, far):
        low = dot(hid[...], gb[...], TN).astype(bf16)
        at = pl.program_id(0)

        @pl.when(at < 4)
        def _():
            send[0] = low

        @pl.when(at == 4)
        def _():
            own[...] = low

        @pl.when(at == 5)
        def _():
            near[...] = low

        @pl.when(at >= 6)
        def _():
            far[0] = low

    return order.run(
        "down_grad",
        body,
        [hidden, gb],
        [pl.BlockSpec((rows, band), lambda j, m: (0, m[5 + j])), whole((rows, D))],
        [shape(d, bf16) for d in ((4, band, D), (band, D), (band, D), (2, band, D))],
        [
            pl.BlockSpec((1, band, D), lambda j, m: (jnp.minimum(j, 3), 0, 0)),
            whole((band, D)),
            whole((band, D)),
            pl.BlockSpec((1, band, D), lambda j, m: (jnp.maximum(j - 6, 0), 0, 0)),
        ],
        (8,),
        [],
        rows * D * FF,
        24,
    )


def second_grad(order, up_left, up_right, out_left, out_right):
    rows = up_right.shape[0]
    blocks = FF // D + 1

    def body(meta, up_left, out_left, up_right, out_right, send, own, near, far, held):
        def emit(left, right):
            held[...] = dot(left[...], right[...]).astype(bf16)
            for j in range(8):
                low = held[pl.ds(pl.multiple_of(meta[5 + j] * BAND, BAND), BAND)]
                if j < 4:
                    send[j] = low
                elif j < 6:
                    (own, near)[j - 4][...] = low
                else:
                    far[j - 6] = low

        last = pl.program_id(0) == blocks - 1

        @pl.when(jnp.logical_not(last))
        def _():
            emit(up_left, up_right)

        @pl.when(last)
        def _():
            emit(out_left, out_right)

    many = lambda n: pl.BlockSpec((n, BAND, D), lambda s, m: (0, s, 0))
    one = pl.BlockSpec((BAND, D), lambda s, m: (s, 0))
    flat = (blocks * BAND, D)
    return order.run(
        "second_grad",
        body,
        [up_left, out_left, up_right, out_right],
        [
            whole((D, rows)),
            whole((D, rows)),
            pl.BlockSpec((rows, D), lambda s, m: (0, jnp.minimum(s, blocks - 2))),
            whole((rows, D)),
        ],
        [shape((4, *flat), bf16), shape(flat, bf16), shape(flat, bf16), shape((2, *flat), bf16)],
        [many(4), one, one, many(2)],
        (blocks,),
        [pltpu.VMEM((D, D), bf16)],
        rows * D * blocks * D,
        28,
    )


def collect(order, first_sums, chunk_sums, mid_sums, down_sum, up_sum):
    def body(meta, first, *refs):
        chunks, (mid, down, up, out) = refs[:-4], refs[-4:]
        out[...] = jnp.zeros_like(out)
        out[0:2] = first[0:2]
        at = 0
        for ref in chunks:
            w = ref.shape[1] // 3
            out[2:3, at : at + w] = ref[0:1, :w]
            out[3:4, at : at + w] = ref[0:1, 2 * w :]
            at += w
        out[4:5] = mid[2:3]
        out[5:7] = mid[0:2]
        out[7:8] = down[0:1]
        for i in range(FF // D):
            out[8 + i : 9 + i] = up[0:1, i * D : (i + 1) * D]

    ins = [first_sums, *chunk_sums, mid_sums, down_sum, up_sum]
    return order.small("collect", body, ins, [shape((16, D), f32)])[0]


class Links:
    def __init__(self, mesh):
        self.wide, self.narrow = mesh.shape["wide"], mesh.shape["narrow"]
        self.paired = self.wide == 8 and self.narrow == 4

    def move(self, value, target):
        pairs = []
        for w in range(self.wide):
            for n in range(self.narrow):
                to = target(w, n)
                if to is not None:
                    pairs.append((w * self.narrow + n, to[0] * self.narrow + to[1]))
        return lax.ppermute(value, ("wide", "narrow"), pairs)

    def swap(self, value):
        return self.move(value, lambda w, n: (w ^ 1, n))

    def near(self, value):
        return self.move(value, lambda w, n: (w, n ^ (1 + (w & 1))))

    def far(self, value):
        return self.move(value, lambda w, n: (w, n ^ (2 - (w & 1))))

    def along(self, value, step):
        return self.move(value, lambda w, n: (w, n ^ step))

    def level(self, value, step):
        return self.move(value, lambda w, n: (w ^ (2 * step), n))

    def meta(self):
        table = []
        for w in range(self.wide):
            for n in range(self.narrow):
                core, level = w & 1, w >> 1
                a, b, d = n ^ (1 + core), n ^ (2 - core), n ^ 3
                if not self.paired:
                    row = [0] * 5 + list(range(8)) + [0, 0] + list(range(self.narrow))
                    row += [0] * (20 - len(row))
                else:
                    row = [2 * n, 2 * a, 2 * d + core, 2 * b, 2 * d + 1 - core]
                    row += [2 * s + 1 - core for s in (n, a, b, d)]
                    row += [2 * s + core for s in (n, b, a, d)]
                    row += [core, int(level in (1, 2)), n, n ^ 1, n ^ 2, d]
                    row += [2 * d]
                table.append(row)
        place = lax.axis_index(("wide", "narrow"))
        return lax.dynamic_index_in_dim(jnp.array(table, jnp.int32), place, keepdims=False)

    def shares(self, packed):
        if not self.paired:
            sources = lax.all_gather(packed, "narrow", axis=0)
            return [sources[i] for i in range(self.narrow)]
        return [packed] + [self.along(packed, i) for i in (1, 2, 3)]

    def inward(self, value):
        return self.move(value, lambda w, n: {0: (w + 2, n), 3: (w - 2, n)}.get(w >> 1))

    def across(self, value):
        return self.move(value, lambda w, n: {1: (w + 2, n), 2: (w - 2, n)}.get(w >> 1))

    def outward(self, value):
        return self.move(value, lambda w, n: {1: (w - 2, n), 2: (w + 2, n)}.get(w >> 1))

    def whole_sum(self, sent, own, near, far):
        rest = own.shape[0]
        band = rest if rest == FF // 8 else BAND
        full = jnp.concatenate([sent, own[None], near[None], far], 0)
        full = full.reshape(8, rest // band, band, D)
        mine = lax.psum_scatter(full, "narrow", scatter_dimension=0, tiled=True)
        mine = lax.psum(mine, "wide").transpose(1, 0, 2, 3).reshape(rest // band, -1, D)
        half = mine.shape[1] // 2
        return mine[:, :half].reshape(-1, D), mine[:, half:].reshape(-1, D)


def finish_two(order, d_pair, s_pair, half):
    blocks = FF // D
    up, out = finish(
        order,
        half,
        [s_pair],
        [(FF, [(0, i, 0, D) for i in range(blocks)]), (D, [(0, blocks, 0, D)])],
    )
    (down,) = finish(order, d_pair[0].shape[0], [d_pair], [(D, [(0, 0, 0, D)])])
    return down, up, out


def split(got):
    return got[:3], got[3:]


def layer(links, *args):
    (
        tokens,
        segment_ids,
        out_grad,
        first_gain,
        first_shift,
        query_weight,
        query_bias,
        key_weight,
        value_weight,
        value_bias,
        output_weight,
        output_bias,
        second_gain,
        second_shift,
        up_weight,
        up_bias,
        down_weight,
        down_bias,
    ) = args
    order = Order(links.meta())
    paired = links.paired
    share = first_gain.shape[0]
    gather = lambda v: [lax.all_gather(v, "narrow", axis=0, tiled=True)]
    small = (
        first_gain,
        first_shift,
        query_bias,
        value_bias,
        output_bias,
        second_gain,
        second_shift,
        down_bias,
    )
    live = segment_ids.reshape(-1, 1, TILE)

    pack_one = pack(order, [query_weight, key_weight, value_weight])
    pack_two = pack(order, [up_weight, output_weight])
    shares = links.shares(jnp.concatenate([*small, up_bias]).reshape(-1, share))
    vec, up_b = vectors(order, shares)
    if paired:
        near_one = links.near(pack_one)
        far_one = links.far(near_one)
        w_one = [pack_one, near_one, far_one, links.swap(near_one)]
    else:
        w_one = gather(pack_one)
    if paired:
        order.last.append(far_one)
        pack_two = gate(order, pack_two)
    kept = attend(order, tokens, vec, segment_ids, w_one, 0, None)
    if paired:
        near_two = links.near(pack_two)
        half_two, down_copy = copies(order, [near_two], [down_weight])
        far_two = links.far(half_two)
        got_two, near_down = links.swap(near_two), links.near(down_copy)
    else:
        w_two = gather(pack_two)
    for s in range(1, tokens.shape[0] // LEN):
        kept = attend(order, tokens, vec, segment_ids, w_one, s, list(kept))
    fn_t, q, k, v, att, att_t, expo, inv = kept
    if paired:
        down_half, far_two = copies(order, [down_weight], [far_two])
        w_two = [pack_two, near_two, far_two, got_two, links.swap(far_two)]
        far_down = links.along(down_half, 3)
    else:
        w_down = gather(down_weight)
    mid, sn_t, hidden, slope, gb, down_sum = feed(
        order, att, tokens, out_grad, live, vec, up_b, w_two
    )

    if paired:
        near_down, far_down = copies(order, [], [near_down, far_down])
        w_down = [down_weight, near_down, far_down, links.swap(near_down), links.swap(far_down)]
    d_send, d_own, d_near, d_far = down_grad(order, hidden, gb)
    if paired:
        d_got = links.swap(d_send)
    every, pair = ..., slice(2, 4)
    if paired:
        (d_far,) = sums_of(order, [[(d_far, every), (d_got, pair)]])
        d_got2 = links.near(d_far)
    gpre, gmid, gattn, gatt, mid_sums, up_sum = back(order, slope, mid, gb, vec, w_down, w_two)
    if paired:
        d_near, d_own = sums_of(
            order,
            [[(d_near, every), (d_got, 1), (d_got2, 1)]],
            [[(d_own, every), (d_got, 0), (d_got2, 0)]],
        )
        d_got = links.far(d_near)
    s_send, s_own, s_near, s_far = second_grad(order, sn_t, gpre, att_t, gattn)
    if paired:
        s_got = links.swap(s_send)
        (s_far,) = sums_of(order, [[(s_far, every), (s_got, pair)]])
        s_got2 = links.near(s_far)
    c_three, (c_send, c_own, c_near, c_far, c_sums) = split(
        attend_back(order, fn_t, q, k, v, att_t, gatt, expo, inv, 0, CHUNKS[0])
    )
    if paired:
        c_got = links.swap(c_send)
        s_near, s_own, d_own = sums_of(
            order,
            [[(s_near, every), (s_got, 1), (s_got2, 1)]],
            [[(s_own, every), (s_got, 0), (s_got2, 0)]],
            [[(d_own, every), (d_got, every)]],
        )
        s_got = links.far(s_near)
        d_got = links.inward(d_own)
    e_three, (e_send, e_own, e_near, e_far, e_sums) = split(
        attend_back(order, fn_t, q, k, v, att_t, gatt, expo, inv, CHUNKS[0], CHUNKS[1])
    )
    if paired:
        e_got = links.swap(fetch(order, e_send)[0])
        s_own, d_own = sums_of(
            order, [[(s_own, every), (s_got, every)]], [[(d_own, every), (d_got, every)]]
        )
        s_got, d_got = links.inward(s_own), links.across(d_own)
        (g_far,) = sums_of(
            order, [[(c_far, every), (c_got, pair)], [(e_far, every), (e_got, pair)]]
        )
        g_got = links.near(g_far)
    input_grad, first_sums = grad_first(
        order, [c_three, e_three], tokens, gmid, vec, w_one
    )
    total = collect(order, first_sums, [c_sums, e_sums], mid_sums, down_sum, up_sum)
    if paired:
        totals = [total] + [links.along(total, i) for i in (1, 2, 3)]
        cut = c_own.shape[0]
        low, high = (slice(0, cut), slice(None)), (slice(cut, None), slice(None))
        g_near, g_own, s_own, d_own = sums_of(
            order,
            [
                [(c_near, every), (c_got, 1), (g_got, (1, *low))],
                [(e_near, every), (e_got, 1), (g_got, (1, *high))],
            ],
            [
                [(c_own, every), (c_got, 0), (g_got, (0, *low))],
                [(e_own, every), (e_got, 0), (g_got, (0, *high))],
            ],
            [[(s_own, every), (s_got, every)]],
            [[(d_own, every), (d_got, every)]],
        )
        g_got = links.far(g_near)
        s_got, d_got = links.across(s_own), links.outward(d_own)
    layer_out = down_out(order, hidden, mid, vec, w_down)
    if paired:
        g_own, s_own = sums_of(
            order,
            [[(g_own, every), (g_got, every)], [(t, every) for t in totals]],
            [[(s_own, every), (s_got, every)]],
        )
        g_got, s_got = links.inward(g_own), links.outward(s_own)
        d_own = pick(order, d_own, d_got)
        d_pair = (d_own, links.swap(d_own))
        (g_own,) = sums_of(order, [[(g_own, every), (g_got, every)]])
        g_got = links.across(g_own)
        s_own = pick(order, s_own, s_got)
        s_pair = (s_own, links.swap(s_own))
        (g_own,) = sums_of(order, [[(g_own, every), (g_got, every)]])
        g_got = links.outward(g_own)
        finished = finish_two(order, d_pair, s_pair, share // 2)
        g_own = pick(order, g_own, g_got)
        g_pair = (g_own, links.swap(g_own))
    else:
        s_pair = links.whole_sum(s_send, s_own, s_near, s_far)
        d_pair = links.whole_sum(d_send, d_own, d_near, d_far)
        c_pair = links.whole_sum(c_send, c_own, c_near, c_far)
        e_pair = links.whole_sum(e_send, e_own, e_near, e_far)
        g_pair = [jnp.concatenate([c, e], 0) for c, e in zip(c_pair, e_pair)]
        total = lax.psum(total, ("wide", "narrow"))
        finished = finish_two(order, d_pair, s_pair, share // 2)
    down_weight_grad, up_weight_grad, output_weight_grad = finished
    half = share // 2
    plan = []
    for i in range(3):
        parts = []
        for c, pairs in enumerate(CHUNKS):
            at, stop = i * PAIR * pairs, (i + 1) * PAIR * pairs
            while at < stop:
                end = min(stop, (at // D + 1) * D)
                block = at // D + c * (3 * PAIR * CHUNKS[0] // D)
                parts.append((0, block, at % D, end - at))
                at = end
        plan.append((D, parts))
    first_grads = finish(order, half, [g_pair], plan, 16 if paired else 0)
    if paired:
        total = first_grads[3]

    n = lax.axis_index("narrow")
    mine = lax.dynamic_slice_in_dim(total[:8], n * share, share, 1)
    up_share = up_bias.shape[0]
    up_mine = lax.dynamic_slice_in_dim(total[8:12].reshape(FF), n * up_share, up_share)
    return (
        layer_out,
        input_grad,
        mine[0],
        mine[1],
        first_grads[0],
        mine[2],
        first_grads[1],
        first_grads[2],
        mine[3],
        output_weight_grad,
        mine[4],
        mine[5],
        mine[6],
        up_weight_grad,
        up_mine,
        down_weight_grad,
        mine[7],
    )


def solution(mesh):
    rows, vector, matrix = P(("wide", "narrow"), None), P("narrow"), P("narrow", None)
    in_specs = (rows, P(("wide", "narrow")), rows) + tuple(
        matrix if i in (2, 4, 5, 7, 11, 13) else vector for i in range(15)
    )
    out_specs = (rows, rows) + in_specs[3:]
    return jax.shard_map(
        functools.partial(layer, Links(mesh)),
        mesh=mesh,
        in_specs=in_specs,
        out_specs=out_specs,
        check_vma=False,
    )
```

```python
import functools

import jax
import jax.numpy as jnp
from jax import lax
from jax.experimental import pallas as pl
from jax.experimental.pallas import tpu as pltpu
from jax.sharding import PartitionSpec as P

D = 768
HEADS = 12
HEAD = 64
LEN = 512
FF = 3072
EPSILON = 1e-06
TILE = 256
BAND = D // 8
PAIR = 2 * HEAD
PAIRS = HEADS // 2
CHUNKS = (4, 2)
LOG2E = 1.4426950408889634
LN2 = 0.6931471805599453

bf16 = jnp.bfloat16
f32 = jnp.float32
NN = (((1,), (0,)), ((), ()))
NT = (((1,), (1,)), ((), ()))
TN = (((0,), (0,)), ((), ()))
ANY = pl.BlockSpec(memory_space=pl.ANY)


def dot(left, right, dims=NN):
    return lax.dot_general(left, right, dims, preferred_element_type=f32)


def shape(dims, kind):
    return jax.ShapeDtypeStruct(dims, kind)


def column_sum(values):
    return jnp.sum(values, 0, keepdims=True)


def whole(dims):
    return pl.BlockSpec(dims, lambda *at: (0,) * len(dims))


def rows_block(dims):
    return pl.BlockSpec(dims, lambda at, *rest: (at,) + (0,) * (len(dims) - 1))


class Order:
    def __init__(self, meta):
        self.meta, self.last, self.far = meta, [], []

    def run(
        self,
        name,
        body,
        ins,
        in_specs,
        outs,
        out_specs,
        grid,
        scratch,
        macs,
        limit,
        alias={},
        near=False,
    ):
        moved = sum(a.size * a.dtype.itemsize for a in ins)
        moved += sum(o.size * o.dtype.itemsize for o in outs)
        used, extra = len(ins), len(self.last)

        def inner(meta, *refs):
            body(meta, *refs[:used], *refs[used + extra :])

        ins = [
            a if spec is ANY else pltpu.with_memory_space_constraint(a, pltpu.HBM)
            for a, spec in zip(ins, in_specs)
        ]
        if not near:
            outs = [pltpu.HBM(o.shape, o.dtype) for o in outs]
        got = pl.pallas_call(
            inner,
            out_shape=outs,
            grid_spec=pltpu.PrefetchScalarGridSpec(
                num_scalar_prefetch=1,
                grid=grid,
                in_specs=[*in_specs] + [ANY] * extra,
                out_specs=out_specs,
                scratch_shapes=scratch,
            ),
            input_output_aliases=alias,
            compiler_params=pltpu.CompilerParams(vmem_limit_bytes=limit * 2**20),
            cost_estimate=pl.CostEstimate(flops=1, bytes_accessed=1 if near else 4 * 10**8, transcendentals=0),
            name=name,
        )(self.meta, *ins, *self.tokens())
        self.last = [got[0]]
        if not near:
            self.far += got
        return got

    def tokens(self):
        return [
            pltpu.with_memory_space_constraint(t, pltpu.HBM)
            if any(t is a for a in self.far)
            else t
            for t in self.last
        ]

    def small(self, name, body, ins, outs, scratch=()):
        used, extra = len(ins), len(self.last)
        far = [any(a is b for b in self.far) for a in ins]
        held = [i for i in range(used) if far[i]]
        wait = len(held)

        def inner(meta, *refs):
            inputs, refs = list(refs[:used]), refs[used + extra :]
            outputs, refs = refs[: len(outs)], refs[len(outs) :]
            buffers, rest = refs[:wait], refs[wait:]
            moves = []
            for n, i in enumerate(held):
                moves.append(pltpu.make_async_copy(inputs[i], buffers[n], rest[0].at[n]))
                inputs[i] = buffers[n]
            for move in moves:
                move.start()
            for move in moves:
                move.wait()
            body(meta, *inputs, *outputs, *rest[1 if wait else 0 :])

        vmem = pl.BlockSpec(memory_space=pltpu.VMEM)
        got = pl.pallas_call(
            inner,
            out_shape=outs,
            in_specs=[pl.BlockSpec(memory_space=pltpu.SMEM)]
            + [ANY if f else vmem for f in far]
            + [ANY] * extra,
            out_specs=[vmem] * len(outs),
            scratch_shapes=[pltpu.VMEM(ins[i].shape, ins[i].dtype) for i in held]
            + ([pltpu.SemaphoreType.DMA((wait,))] if wait else [])
            + list(scratch),
            compiler_params=pltpu.CompilerParams(vmem_limit_bytes=20 * 2**20),
            cost_estimate=pl.CostEstimate(flops=1, bytes_accessed=1, transcendentals=0),
            name=name,
        )(
            self.meta,
            *[
                pltpu.with_memory_space_constraint(a, pltpu.HBM) if f else a
                for a, f in zip(ins, far)
            ],
            *self.tokens(),
        )
        self.last = [got[0]]
        return got


def fill(meta, pieces, target, sems, cols=None):
    count = 1 if len(pieces) == 1 else len(pieces)
    half = target.shape[0] // 8
    copies = []
    for i in range(count):
        place = meta[19] if count == 4 and i == 2 else meta[i]
        start = pl.multiple_of(place * half, half) if count > 1 else 0
        rows = pl.ds(start, pieces[i].shape[0])
        src, dst = pieces[i], target.at[rows]
        if cols is not None:
            src, dst = src.at[:, cols], target.at[rows, cols]
        copies.append(pltpu.make_async_copy(src, dst, sems.at[i]))
    return copies


def first_step(copies):
    @pl.when(pl.program_id(0) == 0)
    def _():
        for copy in copies:
            copy.start()
        for copy in copies:
            copy.wait()


def as_column(row):
    return jnp.broadcast_to(row.astype(f32), (8, row.shape[1])).T[:, :1]


def standard(v):
    center = v - jnp.mean(v, -1, keepdims=True)
    rate = lax.rsqrt(jnp.mean(center * center, -1, keepdims=True) + EPSILON)
    return center * rate, rate


def pack(order, parts):
    rows = parts[0].shape[0]
    width = sum(p.shape[1] for p in parts)
    count = len(parts)

    def body(meta, *refs):
        out, sems = refs[count:]
        moves, at = [], 0
        for i, src in enumerate(refs[:count]):
            cols = out.at[:, at : at + src.shape[1]]
            moves.append(pltpu.make_async_copy(src, cols, sems.at[i]))
            at += src.shape[1]
        for move in moves:
            move.start()
        for move in moves:
            move.wait()

    return order.run(
        "pack",
        body,
        [pltpu.with_memory_space_constraint(p, pltpu.HBM) for p in parts],
        [ANY] * count,
        [shape((rows, width), bf16)],
        [whole((rows, width))],
        (1,),
        [pltpu.SemaphoreType.DMA((count,))],
        0,
        16,
        near=True,
    )[0]


def gate(order, value):
    return order.run(
        "gate",
        lambda meta, *refs: None,
        [value],
        [ANY],
        [shape(value.shape, value.dtype)],
        [ANY],
        (1,),
        [],
        0,
        16,
        alias={1: 0},
        near=True,
    )[0]


def copies(order, halves, wholes=()):
    ins = [*halves, *wholes]
    dims = [(a.shape[0] // 2, a.shape[1]) for a in halves] + [a.shape for a in wholes]

    def body(meta, *refs):
        for i, (src, dst) in enumerate(zip(refs[: len(ins)], refs[len(ins) :])):
            if i < len(halves):
                half = dst.shape[0]
                dst[...] = src[pl.ds(pl.multiple_of(meta[13] * half, half), half)]
            else:
                dst[...] = src[...]

    return order.small("copies", body, ins, [shape(d, bf16) for d in dims])


def fetch(order, *arrays):
    count = len(arrays)

    def body(meta, *refs):
        moves = [
            pltpu.make_async_copy(refs[i], refs[count + i], refs[-1].at[i]) for i in range(count)
        ]
        for move in moves:
            move.start()
        for move in moves:
            move.wait()

    return order.run(
        "fetch",
        body,
        [pltpu.with_memory_space_constraint(a, pltpu.HBM) for a in arrays],
        [ANY] * count,
        [shape(a.shape, bf16) for a in arrays],
        [whole(a.shape) for a in arrays],
        (1,),
        [pltpu.SemaphoreType.DMA((count,))],
        0,
        20,
        near=True,
    )


def sums_of(order, *plan):
    ins = []
    for parts in plan:
        for array, _ in sum(parts, []):
            if not any(array is other for other in ins):
                ins.append(array)
    where = lambda array: [i for i, other in enumerate(ins) if other is array][0]
    places = [[[(where(a), index) for a, index in terms] for terms in parts] for parts in plan]

    def body(meta, *refs):
        for parts, out in zip(places, refs[len(ins) :]):
            at = 0
            for terms in parts:
                total = None
                for i, index in terms:
                    term = refs[i][index].astype(f32)
                    total = term if total is None else total + term
                rows = slice(at, at + total.shape[-2])
                out[..., rows, :] = total.astype(bf16)
                at += total.shape[-2]

    outs = []
    for parts in plan:
        dims = [
            jax.eval_shape(lambda a, i=terms[0][1]: a[i], terms[0][0]).shape for terms in parts
        ]
        rows = sum(d[-2] for d in dims)
        outs.append(shape((*dims[0][:-2], rows, dims[0][-1]), bf16))
    return order.small("sums_of", body, ins, outs)


def pick(order, own, got):
    def body(meta, own, got, out):
        inner = jnp.full(out.shape, meta[14], jnp.int32) == 1
        out[...] = jnp.where(inner, own[...], got[...])

    return order.small("pick", body, [own, got], [shape(own.shape, bf16)])[0]


def deal(order, parts):
    flat = [a for arrays in parts for a in arrays]
    size = -(-sum(arrays[0].shape[0] for arrays in parts) // 64) * 16

    def body(meta, *refs):
        ins, outs, held = refs[: len(flat)], refs[len(flat) : -1], refs[-1]
        held[...] = jnp.zeros_like(held)
        i, at = 0, 0
        for arrays in parts:
            total = None
            for ref in ins[i : i + len(arrays)]:
                term = ref[...].astype(f32)
                total = term if total is None else total + term
            i += len(arrays)
            held[at : at + total.shape[0]] = total.astype(bf16)
            at += total.shape[0]
        for j in range(4):
            outs[j][...] = held[pl.ds(pl.multiple_of(meta[20 + j] * size, size), size)]

    outs = [shape((size, D), bf16)] * 4
    return order.small("deal", body, flat, outs, [pltpu.VMEM((4 * size, D), bf16)])


def undeal(order, bands):
    size = bands[0].shape[0]

    def body(meta, *refs):
        for j in range(4):
            rows = pl.ds(pl.multiple_of(meta[20 + j] * size, size), size)
            refs[4][rows] = refs[j][...]

    return order.small("undeal", body, bands, [shape((4 * size, D), bf16)])[0]


def turn(order, *pairs):
    def body(meta, *refs):
        ins, outs = refs[:8], refs[8:]
        for i, out in enumerate(outs):
            own, got = ins[2 * i], ins[2 * i + 1]
            if i == 2:
                inner = jnp.full(out.shape, meta[14], jnp.int32) == 1
                out[...] = jnp.where(inner, own[...], got[...])
            else:
                out[...] = (own[...].astype(f32) + got[...].astype(f32)).astype(out.dtype)

    outs = [shape(a.shape, a.dtype) for a in pairs[::2]]
    return order.small("turn", body, list(pairs), outs)


def finish(order, half, pairs, plan, last=None):
    flat = [a for pair in pairs for a in pair]

    def body(meta, *refs):
        core = meta[13]
        for (width, parts), out in zip(plan, refs[len(flat) :]):
            at = 0
            for which, block, first, cols in parts:
                for i in range(2):
                    place = core if i == 0 else 1 - core
                    rows = pl.ds(pl.multiple_of(place * half, half), half)
                    value = refs[2 * which + i][
                        block * half : (block + 1) * half, first : first + cols
                    ]
                    out[rows, at : at + cols] = value.astype(f32)
                at += cols
        if last:
            own, other = [ref[last].astype(f32) for ref in refs[:2]]
            refs[-1][...] = own + other

    outs = [shape((2 * half, width), f32) for width, _ in plan]
    if last:
        outs.append(shape((last.stop - last.start, D), f32))
    return order.small("finish", body, flat, outs)


def attend(order, tokens, vec, segs, pieces, at_seq, before):
    count = len(pieces)
    rows = tokens.shape[0]
    seqs = rows // LEN
    held = 0 if before is None else len(before)

    def body(meta, tok, vec, seg, *rest):
        pieces, rest = rest[:count], rest[count + held :]
        fn_t, q, k, v, att, att_t, expo, inv, bias, w, sems = rest
        p = pl.program_id(0)

        @pl.when(p == 0)
        def _():
            copies = fill(meta, pieces, w, sems)
            for copy in copies:
                copy.start()
            row = seg[0].astype(f32)
            bias[...] = jnp.where(as_column(row) == row, 0.0, -1e30)
            normed = standard(tok[...].astype(f32))[0] * vec[0:1] + vec[1:2]
            low = normed.astype(bf16)
            fn_t[...] = low.T
            for copy in copies:
                copy.wait()
            q[...] = ((dot(low, w[:, :D]) + vec[2:3]) * (LOG2E * HEAD**-0.5)).astype(bf16)
            k[...] = dot(low, w[:, D : 2 * D]).astype(bf16)
            v[...] = (dot(low, w[:, 2 * D :]) + vec[3:4]).astype(bf16)

        lane = lax.broadcasted_iota(jnp.int32, (LEN, PAIR), 1)
        mine_cols = pl.ds(pl.multiple_of(p * PAIR, PAIR), PAIR)
        vt = v[:, mine_cols].T
        keys = k[:, mine_cols]
        queries = q[:, mine_cols]
        parts = []
        for h in range(2):
            mine = (lane < HEAD) if h == 0 else (lane >= HEAD)
            scores = dot(jnp.where(mine, keys, 0).astype(bf16), queries, NT) + bias[...]
            e = jnp.exp2(scores - jnp.max(scores, 0, keepdims=True))
            rate = 1.0 / jnp.sum(e, 0, keepdims=True)
            low = e.astype(bf16)
            expo[h] = low
            inv[0, h : h + 1] = rate
            parts.append(dot(vt[HEAD * h : HEAD * h + HEAD], low) * rate)
        both = jnp.concatenate(parts, 0)
        att_t[...] = both.astype(bf16)
        att[...] = both.T.astype(bf16)

    seq = pl.BlockSpec((LEN, D), lambda p, m: (at_seq, 0))
    ins = [tokens, vec, segs.reshape(seqs, 1, LEN), *pieces]
    alias = {}
    if before is not None:
        alias = {1 + len(ins) + i: i for i in range(held)}
        ins += before
    return order.run(
        "attend",
        body,
        ins,
        [
            seq,
            whole((8, D)),
            pl.BlockSpec((1, 1, LEN), lambda p, m: (at_seq, 0, 0)),
        ]
        + [ANY] * (count + held),
        [
            shape((D, rows), bf16),
            shape((rows, D), bf16),
            shape((rows, D), bf16),
            shape((rows, D), bf16),
            shape((rows, D), bf16),
            shape((D, rows), bf16),
            shape((seqs * HEADS, LEN, LEN), bf16),
            shape((seqs * PAIRS, 8, LEN), f32),
        ],
        [
            pl.BlockSpec((D, LEN), lambda p, m: (0, at_seq)),
            seq,
            seq,
            seq,
            pl.BlockSpec((LEN, PAIR), lambda p, m: (at_seq, p)),
            pl.BlockSpec((PAIR, LEN), lambda p, m: (p, at_seq)),
            pl.BlockSpec((2, LEN, LEN), lambda p, m: (at_seq * PAIRS + p, 0, 0)),
            pl.BlockSpec((1, 8, LEN), lambda p, m: (at_seq * PAIRS + p, 0, 0)),
        ],
        (PAIRS,),
        [
            pltpu.VMEM((LEN, LEN), f32),
            pltpu.VMEM((D, 3 * D), bf16),
            pltpu.SemaphoreType.DMA((count,)),
        ],
        LEN * D * D * 3 + LEN * LEN * D * 8,
        28,
        alias,
    )


def vectors(order, sources):
    n, share = len(sources), sources[0].shape[1]

    def body(meta, *refs):
        srcs, (vec, ub) = refs[:n], refs[n:]
        rows = []
        for s in range(n):
            total = jnp.zeros((12, share), f32)
            for i in range(n):
                total = jnp.where(meta[15 + i] == s, srcs[i][...].astype(f32), total)
            rows.append(total)
        vec[...] = jnp.concatenate([r[:8] for r in rows], 1)
        ub[...] = jnp.concatenate([r[8 + i : 9 + i] for r in rows for i in range(4)], 1)

    outs = [shape((8, D), f32), shape((1, FF), f32)]
    return order.small("vectors", body, sources, outs)


def gelu_both(x):
    size = jnp.abs(x) * 0.7071067811865476
    t = 1.0 / (1.0 + 0.3275911 * size)
    bell = jnp.exp2(x * x * (-0.5 * LOG2E))
    poly = 0.5 * 1.061405429
    for c in (-1.453152027, 1.421413741, -0.284496736, 0.254829592):
        poly = poly * t + 0.5 * c
    tail = poly * t * bell
    cdf = jnp.where(x >= 0, 1.0 - tail, tail)
    return x * cdf, cdf + x * bell * 0.3989422804014327


def feed(order, attended, tokens, out_grad, live, vec, up_bias, pieces):
    count = len(pieces)
    rows = tokens.shape[0]

    def body(meta, att, tok, og, seg, vec, ub, *rest):
        pieces, rest = rest[:count], rest[count:]
        mid, sn_t, hid, slope, gb, down_sum, w, sems, sems_up = rest
        first = fill(meta, pieces, w, sems, slice(FF, FF + D))
        others = fill(meta, pieces, w, sems_up, slice(0, FF))
        begin = pl.program_id(0) == 0

        @pl.when(begin)
        def _():
            for copy in [*first, *others]:
                copy.start()
            for copy in first:
                copy.wait()

        m = tok[...].astype(f32) + dot(att[...], w[:, FF:]) + vec[4:5]
        mid[...] = m
        low = (standard(m)[0] * vec[5:6] + vec[6:7]).astype(bf16)
        sn_t[...] = low.T
        grad = jnp.where(as_column(seg[0]) >= 0, og[...].astype(f32), 0.0)
        gb[...] = grad.astype(bf16)

        @pl.when(pl.program_id(0) == 0)
        def _():
            down_sum[...] = jnp.zeros_like(down_sum)

        down_sum[0:1] += column_sum(grad)

        @pl.when(begin)
        def _():
            for copy in others:
                copy.wait()

        for at in range(0, FF, 512):
            pre = dot(low, w[:, at : at + 512]) + ub[:, at : at + 512]
            act, der = gelu_both(pre)
            hid[:, at : at + 512] = act.astype(bf16)
            slope[:, at : at + 512] = der.astype(bf16)

    blk = rows_block((TILE, D))
    wide = rows_block((TILE, FF))
    return order.run(
        "feed",
        body,
        [attended, tokens, out_grad, live, vec, up_bias, *pieces],
        [blk, blk, blk, rows_block((1, 1, TILE)), whole((8, D)), whole((1, FF))] + [ANY] * count,
        [
            shape((rows, D), f32),
            shape((D, rows), bf16),
            shape((rows, FF), bf16),
            shape((rows, FF), bf16),
            shape((rows, D), bf16),
            shape((8, D), f32),
        ],
        [blk, pl.BlockSpec((D, TILE), lambda at, m: (0, at)), wide, wide, blk, whole((8, D))],
        (rows // TILE,),
        [pltpu.VMEM((D, FF + D), bf16)] + [pltpu.SemaphoreType.DMA((count,))] * 2,
        rows * D * (FF + D) * 3,
        32,
    )


def down_out(order, hidden, mid, vec, pieces):
    count = len(pieces)
    rows = hidden.shape[0]

    def body(meta, hid, mid, vec, *rest):
        pieces, (out, w, sems) = rest[:count], rest[count:]
        first_step(fill(meta, pieces, w, sems))
        out[...] = (mid[...] + dot(hid[...], w[...]) + vec[7:8]).astype(bf16)

    blk = rows_block((TILE, D))
    return order.run(
        "down_out",
        body,
        [hidden, mid, vec, *pieces],
        [rows_block((TILE, FF)), blk, whole((8, D))] + [ANY] * count,
        [shape((rows, D), bf16)],
        [blk],
        (rows // TILE,),
        [pltpu.VMEM((FF, D), bf16), pltpu.SemaphoreType.DMA((count,))],
        rows * D * FF,
        24,
    )[0]


def normal_grad(grad, gain, hat, rate):
    inner = grad * gain
    return rate * (
        inner
        - jnp.mean(inner, -1, keepdims=True)
        - hat * jnp.mean(inner * hat, -1, keepdims=True)
    )


def back(order, slope, mid, gb, vec, downs, pieces):
    nd, count = len(downs), len(pieces)
    rows = gb.shape[0]

    def body(meta, slope, mid, gb, vec, *rest):
        downs, pieces, rest = rest[:nd], rest[nd : nd + count], rest[nd + count :]
        gpre, gmid, gattn, gatt, sums, up_sum, wd, w, sems_d, sems = rest
        first, others = fill(meta, downs, wd, sems_d), fill(meta, pieces, w, sems)
        begin = pl.program_id(0) == 0

        @pl.when(begin)
        def _():
            for copy in [*first, *others]:
                copy.start()
            sums[...] = jnp.zeros_like(sums)
            up_sum[...] = jnp.zeros_like(up_sum)
            for copy in first:
                copy.wait()

        for at in range(0, FF, 512):
            cols = slice(at, at + 512)
            low = (dot(gb[...], wd[cols], NT) * slope[:, cols].astype(f32)).astype(bf16)
            gpre[:, cols] = low
            up_sum[0:1, cols] += column_sum(low.astype(f32))

        @pl.when(begin)
        def _():
            for copy in others:
                copy.wait()

        grad = dot(gpre[...], w[:, :FF], NT)
        hat, rate = standard(mid[...])
        sums[0:1] += column_sum(grad * hat)
        sums[1:2] += column_sum(grad)
        g = gb[...].astype(f32) + normal_grad(grad, vec[5:6], hat, rate)
        gmid[...] = g
        low = g.astype(bf16)
        gattn[...] = low
        sums[2:3] += column_sum(low.astype(f32))
        gatt[...] = dot(low, w[:, FF:], NT).astype(bf16)

    blk = rows_block((TILE, D))
    wide = rows_block((TILE, FF))
    return order.run(
        "back",
        body,
        [slope, mid, gb, vec, *downs, *pieces],
        [wide, blk, blk, whole((8, D))] + [ANY] * (nd + count),
        [
            shape((rows, FF), bf16),
            shape((rows, D), f32),
            shape((rows, D), bf16),
            shape((rows, D), bf16),
            shape((8, D), f32),
            shape((8, FF), f32),
        ],
        [wide, blk, blk, blk, whole((8, D)), whole((8, FF))],
        (rows // TILE,),
        [
            pltpu.VMEM((FF, D), bf16),
            pltpu.VMEM((D, FF + D), bf16),
            pltpu.SemaphoreType.DMA((nd,)),
            pltpu.SemaphoreType.DMA((count,)),
        ],
        rows * D * (2 * FF + D),
        32,
    )


def attend_back(order, fn_t, q, k, v, att_t, gatt, expo, inv, first, pairs):
    rows = q.shape[0]
    count = rows // LEN
    width = PAIR * pairs

    def body(meta, q, k, v, att_t, g, expo, inv, fn_t, *rest):
        dq, dk, dv, send, own, near, far, sums, grads, held, sems = rest
        s, p = pl.program_id(0), pl.program_id(1)

        def moves():
            return [
                pltpu.make_async_copy(
                    fn_t.at[pl.ds(pl.multiple_of(meta[5 + j] * BAND, BAND), BAND)],
                    held.at[pl.ds(j * BAND, BAND)],
                    sems.at[j],
                )
                for j in range(8)
            ]

        @pl.when((s == 0) & (p == 0))
        def _():
            for copy in moves():
                copy.start()

        queries, values = q[...], v[...]
        kt = k[...].T
        gt = g[...].astype(f32).T
        both = att_t[...].astype(f32) * gt
        parts, dks, dvs = [], [], []
        for h in range(2):
            at = slice(HEAD * h, HEAD * h + HEAD)
            rate = inv[0, h : h + 1]
            delta = jnp.sum(both[at], 0, keepdims=True) * rate
            scaled = (gt[at] * rate).astype(bf16)
            e = expo[h]
            ds = (e.astype(f32) * (dot(values[:, at], scaled) - delta)).astype(bf16)
            parts.append(dot(kt[at], ds))
            dvs.append(dot(e, scaled, NT))
            dks.append(dot(ds, queries[:, at]) * LN2)
        three = (
            (jnp.concatenate(parts, 0).T * HEAD**-0.5).astype(bf16),
            jnp.concatenate(dks, 1).astype(bf16),
            jnp.concatenate(dvs, 1).astype(bf16),
        )
        mine = pl.ds(pl.multiple_of(s * LEN, LEN), LEN)
        for i, (ref, value) in enumerate(zip((dq, dk, dv), three)):
            ref[...] = value
            grads[mine, pl.ds(pl.multiple_of(i * width + p * PAIR, PAIR), PAIR)] = value

        @pl.when((s == count - 1) & (p == pairs - 1))
        def _():
            for copy in moves():
                copy.wait()
            for i in range(blocks):
                right = grads[:, i * D : (i + 1) * D]
                rows_of = slice(i * BAND, (i + 1) * BAND)
                low = dot(held[...], right).astype(bf16)
                for j in range(4):
                    send[j, rows_of] = low[j * BAND : (j + 1) * BAND]
                own[rows_of] = low[4 * BAND : 5 * BAND]
                near[rows_of] = low[5 * BAND : 6 * BAND]
                for j in range(2):
                    far[j, rows_of] = low[(6 + j) * BAND : (7 + j) * BAND]
            right = grads[...]
            sums[...] = jnp.broadcast_to(column_sum(right.astype(f32)), sums.shape)

    blk = pl.BlockSpec((LEN, PAIR), lambda s, p, m: (s, p + first))
    out = pl.BlockSpec((LEN, PAIR), lambda s, p, m: (s, p))
    blocks = 3 * width // D
    bands = [(n, blocks * BAND, D) for n in (4, 2)]
    bands = [bands[0], bands[0][1:], bands[0][1:], bands[1]]
    return order.run(
        "attend_back",
        body,
        [q, k, v, att_t, gatt, expo, inv, fn_t],
        [blk] * 3
        + [
            pl.BlockSpec((PAIR, LEN), lambda s, p, m: (p + first, s)),
            blk,
            pl.BlockSpec((2, LEN, LEN), lambda s, p, m: (s * PAIRS + p + first, 0, 0)),
            pl.BlockSpec((1, 8, LEN), lambda s, p, m: (s * PAIRS + p + first, 0, 0)),
            ANY,
        ],
        [shape((rows, width), bf16)] * 3
        + [shape(d, bf16) for d in bands]
        + [shape((8, 3 * width), f32)],
        [out] * 3 + [whole(d) for d in bands] + [whole((8, 3 * width))],
        (count, pairs),
        [
            pltpu.VMEM((rows, 3 * width), bf16),
            pltpu.VMEM((D, rows), bf16),
            pltpu.SemaphoreType.DMA((8,)),
        ],
        rows * LEN * PAIR * pairs * 9 + rows * D * 3 * width,
        28,
    )


def grad_first(order, dqkv, tokens, gmid, vec, pieces):
    count = len(pieces)
    rows = tokens.shape[0]
    flat = [t for chunk in dqkv for t in chunk]
    starts = [0]
    for chunk in dqkv:
        starts.append(starts[-1] + chunk[0].shape[1])

    def body(meta, tok, gmid, vec, *rest):
        grads, rest = rest[: len(flat)], rest[len(flat) :]
        pieces, (out, sums, w, sems) = rest[:count], rest[count:]
        first_step(fill(meta, pieces, w, sems))

        @pl.when(pl.program_id(0) == 0)
        def _():
            sums[...] = jnp.zeros_like(sums)

        total = None
        for i, ref in enumerate(grads):
            at = (i % 3) * D + starts[i // 3]
            term = dot(ref[...], w[:, at : at + ref.shape[1]], NT)
            total = term if total is None else total + term
        hat, rate = standard(tok[...].astype(f32))
        sums[0:1] += column_sum(total * hat)
        sums[1:2] += column_sum(total)
        out[...] = (gmid[...] + normal_grad(total, vec[0:1], hat, rate)).astype(bf16)

    blk = rows_block((TILE, D))
    return order.run(
        "grad_first",
        body,
        [tokens, gmid, vec, *flat, *pieces],
        [blk, blk, whole((8, D))] + [rows_block((TILE, t.shape[1])) for t in flat] + [ANY] * count,
        [shape((rows, D), bf16), shape((8, D), f32)],
        [blk, whole((8, D))],
        (rows // TILE,),
        [pltpu.VMEM((D, 3 * D), bf16), pltpu.SemaphoreType.DMA((count,))],
        rows * D * D * 3,
        24,
    )


def down_grad(order, hidden, gb, send):
    rows = gb.shape[0]
    band = FF // 8
    first = 5 if send else 9

    def body(meta, hid, gb, *outs):
        low = dot(hid[...], gb[...], TN).astype(bf16)
        if send:
            outs[0][0] = low
            return
        at = pl.program_id(0)
        for j, out in enumerate((outs[0], outs[1], outs[2].at[0], outs[2].at[0])):

            @pl.when(at == j)
            def _(out=out):
                out[...] = low

    dims = [(4, band, D)] if send else [(band, D), (band, D), (2, band, D)]
    specs = [pl.BlockSpec((1, band, D), lambda j, m: (j, 0, 0))]
    if not send:
        specs = [whole((band, D))] * 2
        specs.append(pl.BlockSpec((1, band, D), lambda j, m: (jnp.maximum(j - 2, 0), 0, 0)))
    return order.run(
        "down_grad",
        body,
        [hidden, gb],
        [pl.BlockSpec((rows, band), lambda j, m: (0, m[first + j])), whole((rows, D))],
        [shape(d, bf16) for d in dims],
        specs,
        (4,),
        [],
        rows * D * FF // 2,
        24,
    )


def second_grad(order, up_left, up_right, out_left, out_right):
    rows = up_right.shape[0]
    blocks = FF // D + 1

    def body(meta, up_left, out_left, up_right, out_right, send, own, near, far, held):
        def emit(left, right):
            held[...] = dot(left[...], right[...]).astype(bf16)
            for j in range(8):
                low = held[pl.ds(pl.multiple_of(meta[5 + j] * BAND, BAND), BAND)]
                if j < 4:
                    send[j] = low
                elif j < 6:
                    (own, near)[j - 4][...] = low
                else:
                    far[j - 6] = low

        last = pl.program_id(0) == blocks - 1

        @pl.when(jnp.logical_not(last))
        def _():
            emit(up_left, up_right)

        @pl.when(last)
        def _():
            emit(out_left, out_right)

    many = lambda n: pl.BlockSpec((n, BAND, D), lambda s, m: (0, s, 0))
    one = pl.BlockSpec((BAND, D), lambda s, m: (s, 0))
    flat = (blocks * BAND, D)
    return order.run(
        "second_grad",
        body,
        [up_left, out_left, up_right, out_right],
        [
            whole((D, rows)),
            whole((D, rows)),
            pl.BlockSpec((rows, D), lambda s, m: (0, jnp.minimum(s, blocks - 2))),
            whole((rows, D)),
        ],
        [shape((4, *flat), bf16), shape(flat, bf16), shape(flat, bf16), shape((2, *flat), bf16)],
        [many(4), one, one, many(2)],
        (blocks,),
        [pltpu.VMEM((D, D), bf16)],
        rows * D * blocks * D,
        28,
    )


def collect(order, first_sums, chunk_sums, mid_sums, down_sum, up_sum):
    def body(meta, first, *refs):
        chunks, (mid, down, up, out) = refs[:-4], refs[-4:]
        out[...] = jnp.zeros_like(out)
        out[0:2] = first[0:2]
        at = 0
        for ref in chunks:
            w = ref.shape[1] // 3
            out[2:3, at : at + w] = ref[0:1, :w]
            out[3:4, at : at + w] = ref[0:1, 2 * w :]
            at += w
        out[4:5] = mid[2:3]
        out[5:7] = mid[0:2]
        out[7:8] = down[0:1]
        for i in range(FF // D):
            out[8 + i : 9 + i] = up[0:1, i * D : (i + 1) * D]

    ins = [first_sums, *chunk_sums, mid_sums, down_sum, up_sum]
    return order.small("collect", body, ins, [shape((16, D), f32)])[0]


class Links:
    def __init__(self, mesh):
        self.wide, self.narrow = mesh.shape["wide"], mesh.shape["narrow"]
        self.paired = self.wide == 8 and self.narrow == 4

    def move(self, value, target):
        pairs = []
        for w in range(self.wide):
            for n in range(self.narrow):
                to = target(w, n)
                if to is not None:
                    pairs.append((w * self.narrow + n, to[0] * self.narrow + to[1]))
        return lax.ppermute(value, ("wide", "narrow"), pairs)

    def swap(self, value):
        return self.move(value, lambda w, n: (w ^ 1, n))

    def near(self, value):
        return self.move(value, lambda w, n: (w, n ^ (1 + (w & 1))))

    def far(self, value):
        return self.move(value, lambda w, n: (w, n ^ (2 - (w & 1))))

    def along(self, value, step):
        return self.move(value, lambda w, n: (w, n ^ step))

    def level(self, value, step):
        return self.move(value, lambda w, n: (w ^ (2 * step), n))

    def meta(self):
        table = []
        for w in range(self.wide):
            for n in range(self.narrow):
                core, level = w & 1, w >> 1
                a, b, d = n ^ (1 + core), n ^ (2 - core), n ^ 3
                if not self.paired:
                    row = [0] * 5 + list(range(8)) + [0, 0] + list(range(self.narrow))
                    row += [0] * (24 - len(row))
                else:
                    row = [2 * n, 2 * a, 2 * d + core, 2 * b, 2 * d + 1 - core]
                    row += [2 * s + 1 - core for s in (n, a, b, d)]
                    row += [2 * s + core for s in (n, b, a, d)]
                    row += [core, int(level in (1, 2)), n, n ^ 1, n ^ 2, d]
                    row += [2 * d] + [level ^ j for j in range(4)]
                table.append(row)
        place = lax.axis_index(("wide", "narrow"))
        return lax.dynamic_index_in_dim(jnp.array(table, jnp.int32), place, keepdims=False)

    def shares(self, packed):
        if not self.paired:
            sources = lax.all_gather(packed, "narrow", axis=0)
            return [sources[i] for i in range(self.narrow)]
        return [packed] + [self.along(packed, i) for i in (1, 2, 3)]

    def inward(self, value):
        return self.move(value, lambda w, n: {0: (w + 2, n), 3: (w - 2, n)}.get(w >> 1))

    def across(self, value):
        return self.move(value, lambda w, n: {1: (w + 2, n), 2: (w - 2, n)}.get(w >> 1))

    def outward(self, value):
        return self.move(value, lambda w, n: {1: (w - 2, n), 2: (w + 2, n)}.get(w >> 1))

    def levels(self, bands):
        return [self.level(bands[j], j) for j in (1, 2, 3)]

    def whole_sum(self, sent, own, near, far):
        rest = own.shape[0]
        band = rest if rest == FF // 8 else BAND
        full = jnp.concatenate([sent, own[None], near[None], far], 0)
        full = full.reshape(8, rest // band, band, D)
        mine = lax.psum_scatter(full, "narrow", scatter_dimension=0, tiled=True)
        mine = lax.psum(mine, "wide").transpose(1, 0, 2, 3).reshape(rest // band, -1, D)
        half = mine.shape[1] // 2
        return mine[:, :half].reshape(-1, D), mine[:, half:].reshape(-1, D)


def finish_second(order, pair, half):
    blocks = FF // D
    plan = [(FF, [(0, i, 0, D) for i in range(blocks)]), (D, [(0, blocks, 0, D)])]
    return finish(order, half, [pair], plan)


def finish_down(order, pair):
    return finish(order, pair[0].shape[0], [pair], [(D, [(0, 0, 0, D)])])[0]


def split(got):
    return got[:3], got[3:]


def layer(links, *args):
    (
        tokens,
        segment_ids,
        out_grad,
        first_gain,
        first_shift,
        query_weight,
        query_bias,
        key_weight,
        value_weight,
        value_bias,
        output_weight,
        output_bias,
        second_gain,
        second_shift,
        up_weight,
        up_bias,
        down_weight,
        down_bias,
    ) = args
    order = Order(links.meta())
    paired = links.paired
    share = first_gain.shape[0]
    gather = lambda v: [lax.all_gather(v, "narrow", axis=0, tiled=True)]
    small = (
        first_gain,
        first_shift,
        query_bias,
        value_bias,
        output_bias,
        second_gain,
        second_shift,
        down_bias,
    )
    live = segment_ids.reshape(-1, 1, TILE)

    pack_one = pack(order, [query_weight, key_weight, value_weight])
    pack_two = pack(order, [up_weight, output_weight])
    shares = links.shares(jnp.concatenate([*small, up_bias]).reshape(-1, share))
    if paired:
        near_one = links.near(pack_one)
        far_one, got_one = links.far(near_one), links.swap(near_one)
        w_one = [pack_one, near_one, far_one, got_one]
        order.last.append(got_one)
    vec, up_b = vectors(order, shares)
    if not paired:
        w_one = gather(pack_one)
    if paired:
        order.last.append(far_one)
        pack_two = gate(order, pack_two)
    kept = attend(order, tokens, vec, segment_ids, w_one, 0, None)
    if paired:
        near_two = links.near(pack_two)
        half_two, down_copy = copies(order, [near_two], [down_weight])
        far_two = links.far(half_two)
        got_two, near_down = links.swap(near_two), links.near(down_copy)
    else:
        w_two = gather(pack_two)
    for s in range(1, tokens.shape[0] // LEN):
        kept = attend(order, tokens, vec, segment_ids, w_one, s, list(kept))
    fn_t, q, k, v, att, att_t, expo, inv = kept
    if paired:
        down_half, far_two = copies(order, [down_weight], [far_two])
        w_two = [pack_two, near_two, far_two, got_two, links.swap(far_two)]
        far_down = links.along(down_half, 3)
    else:
        w_down = gather(down_weight)
    mid, sn_t, hidden, slope, gb, down_sum = feed(
        order, att, tokens, out_grad, live, vec, up_b, w_two
    )

    if paired:
        near_down, far_down = copies(order, [], [near_down, far_down])
        w_down = [down_weight, near_down, far_down, links.swap(near_down), links.swap(far_down)]
    (d_send,) = down_grad(order, hidden, gb, True)
    d_own, d_near, d_far = down_grad(order, hidden, gb, False)
    if paired:
        d_got = links.swap(d_send)
    every, pair = ..., slice(2, 4)
    if paired:
        (d_far,) = sums_of(order, [[(d_far, every), (d_got, pair)]])
        d_got2 = links.near(d_far)
    gpre, gmid, gattn, gatt, mid_sums, up_sum = back(order, slope, mid, gb, vec, w_down, w_two)
    if paired:
        d_near, d_own = sums_of(
            order,
            [[(d_near, every), (d_got, 1), (d_got2, 1)]],
            [[(d_own, every), (d_got, 0), (d_got2, 0)]],
        )
        d_got = links.far(d_near)
    s_send, s_own, s_near, s_far = second_grad(order, sn_t, gpre, att_t, gattn)
    if paired:
        s_got = links.swap(s_send)
        (s_far,) = sums_of(order, [[(s_far, every), (s_got, pair)]])
        s_got2 = links.near(s_far)
    c_three, (c_send, c_own, c_near, c_far, c_sums) = split(
        attend_back(order, fn_t, q, k, v, att_t, gatt, expo, inv, 0, CHUNKS[0])
    )
    if paired:
        c_got = links.swap(c_send)
        s_near, s_own, d_own = sums_of(
            order,
            [[(s_near, every), (s_got, 1), (s_got2, 1)]],
            [[(s_own, every), (s_got, 0), (s_got2, 0)]],
            [[(d_own, every), (d_got, every)]],
        )
        s_got = links.far(s_near)
        d_got = links.inward(d_own)
    e_three, (e_send, e_own, e_near, e_far, e_sums) = split(
        attend_back(order, fn_t, q, k, v, att_t, gatt, expo, inv, CHUNKS[0], CHUNKS[1])
    )
    if paired:
        e_got = links.swap(fetch(order, e_send)[0])
        s_own, d_own = sums_of(
            order, [[(s_own, every), (s_got, every)]], [[(d_own, every), (d_got, every)]]
        )
        s_got, d_got = links.inward(s_own), links.across(d_own)
        (g_far,) = sums_of(
            order, [[(c_far, every), (c_got, pair)], [(e_far, every), (e_got, pair)]]
        )
        g_got = links.near(g_far)
    input_grad, first_sums = grad_first(
        order, [c_three, e_three], tokens, gmid, vec, w_one
    )
    if paired:
        s_own, d_own = sums_of(
            order, [[(s_own, every), (s_got, every)]], [[(d_own, every), (d_got, every)]]
        )
        s_got, d_got = links.across(s_own), links.outward(d_own)
    total = collect(order, first_sums, [c_sums, e_sums], mid_sums, down_sum, up_sum)
    if paired:
        t_got = links.near(total)
        cut = c_own.shape[0]
        low, high = (slice(0, cut), slice(None)), (slice(cut, None), slice(None))
        g_near, g_own = sums_of(
            order,
            [
                [(c_near, every), (c_got, 1), (g_got, (1, *low))],
                [(e_near, every), (e_got, 1), (g_got, (1, *high))],
            ],
            [
                [(c_own, every), (c_got, 0), (g_got, (0, *low))],
                [(e_own, every), (e_got, 0), (g_got, (0, *high))],
            ],
        )
        g_got = links.far(g_near)
    layer_out = down_out(order, hidden, mid, vec, w_down)
    if paired:
        g_own, s_own, d_own, total = turn(
            order, g_own, g_got, s_own, s_got, d_own, d_got, total, t_got
        )
        t_got, s_got = links.far(total), links.outward(s_own)
        d_pair = (d_own, links.swap(d_own))
        g_bands = deal(order, [[g_own], [total, t_got]])
        g_gots = links.levels(g_bands)
        down_weight_grad = finish_down(order, d_pair)
        (g_mine,) = sums_of(order, [[(b, every) for b in [g_bands[0], *g_gots]]])
        g_gots = links.levels([g_mine] * 4)
        s_own = pick(order, s_own, s_got)
        s_pair = (s_own, links.swap(s_own))
        up_weight_grad, output_weight_grad = finish_second(order, s_pair, share // 2)
        g_own = undeal(order, [g_mine, *g_gots])
        g_pair = (g_own, links.swap(g_own))
    else:
        s_pair = links.whole_sum(s_send, s_own, s_near, s_far)
        d_pair = links.whole_sum(d_send, d_own, d_near, d_far)
        c_pair = links.whole_sum(c_send, c_own, c_near, c_far)
        e_pair = links.whole_sum(e_send, e_own, e_near, e_far)
        g_pair = [jnp.concatenate([c, e], 0) for c, e in zip(c_pair, e_pair)]
        total = lax.psum(total, ("wide", "narrow"))
        down_weight_grad = finish_down(order, d_pair)
        up_weight_grad, output_weight_grad = finish_second(order, s_pair, share // 2)
    half = share // 2
    plan = []
    for i in range(3):
        parts = []
        for c, pairs in enumerate(CHUNKS):
            at, stop = i * PAIR * pairs, (i + 1) * PAIR * pairs
            while at < stop:
                end = min(stop, (at // D + 1) * D)
                block = at // D + c * (3 * PAIR * CHUNKS[0] // D)
                parts.append((0, block, at % D, end - at))
                at = end
        plan.append((D, parts))
    place = slice(BAND * 3, BAND * 3 + 16) if paired else None
    first_grads = finish(order, half, [g_pair], plan, place)
    if paired:
        total = first_grads[3]

    n = lax.axis_index("narrow")
    mine = lax.dynamic_slice_in_dim(total[:8], n * share, share, 1)
    up_share = up_bias.shape[0]
    up_mine = lax.dynamic_slice_in_dim(total[8:12].reshape(FF), n * up_share, up_share)
    return (
        layer_out,
        input_grad,
        mine[0],
        mine[1],
        first_grads[0],
        mine[2],
        first_grads[1],
        first_grads[2],
        mine[3],
        output_weight_grad,
        mine[4],
        mine[5],
        mine[6],
        up_weight_grad,
        up_mine,
        down_weight_grad,
        mine[7],
    )


def solution(mesh):
    rows, vector, matrix = P(("wide", "narrow"), None), P("narrow"), P("narrow", None)
    in_specs = (rows, P(("wide", "narrow")), rows) + tuple(
        matrix if i in (2, 4, 5, 7, 11, 13) else vector for i in range(15)
    )
    out_specs = (rows, rows) + in_specs[3:]
    return jax.shard_map(
        functools.partial(layer, Links(mesh)),
        mesh=mesh,
        in_specs=in_specs,
        out_specs=out_specs,
        check_vma=False,
    )
```

```python
import functools

import jax
import jax.numpy as jnp
from jax import lax
from jax.experimental import pallas as pl
from jax.experimental.pallas import tpu as pltpu
from jax.sharding import PartitionSpec as P

D = 768
HEADS = 12
HEAD = 64
LEN = 512
FF = 3072
EPSILON = 1e-06
TILE = 256
BAND = D // 8
PAIR = 2 * HEAD
PAIRS = HEADS // 2
CHUNKS = (4, 2)
LOG2E = 1.4426950408889634
LN2 = 0.6931471805599453

bf16 = jnp.bfloat16
f32 = jnp.float32
NN = (((1,), (0,)), ((), ()))
NT = (((1,), (1,)), ((), ()))
TN = (((0,), (0,)), ((), ()))
ANY = pl.BlockSpec(memory_space=pl.ANY)
VM = pl.BlockSpec(memory_space=pltpu.VMEM)


def dot(left, right, dims=NN):
    return lax.dot_general(left, right, dims, preferred_element_type=f32)


def shape(dims, kind):
    return jax.ShapeDtypeStruct(dims, kind)


def column_sum(values):
    return jnp.sum(values, 0, keepdims=True)


def whole(dims):
    return pl.BlockSpec(dims, lambda *at: (0,) * len(dims))


def rows_block(dims):
    return pl.BlockSpec(dims, lambda at, *rest: (at,) + (0,) * (len(dims) - 1))


class Order:
    def __init__(self, meta):
        self.meta, self.last, self.far = meta, [], []

    def run(
        self,
        name,
        body,
        ins,
        in_specs,
        outs,
        out_specs,
        grid,
        scratch,
        macs,
        limit,
        alias={},
        near=False,
    ):
        moved = sum(a.size * a.dtype.itemsize for a in ins)
        moved += sum(o.size * o.dtype.itemsize for o in outs)
        used, extra = len(ins), len(self.last)

        def inner(meta, *refs):
            body(meta, *refs[:used], *refs[used + extra :])

        ins = [
            a if spec is ANY or spec is VM else pltpu.with_memory_space_constraint(a, pltpu.HBM)
            for a, spec in zip(ins, in_specs)
        ]
        if not near:
            outs = [
                (pltpu.VMEM if spec is VM else pltpu.HBM)(o.shape, o.dtype)
                for o, spec in zip(outs, out_specs)
            ]
        got = pl.pallas_call(
            inner,
            out_shape=outs,
            grid_spec=pltpu.PrefetchScalarGridSpec(
                num_scalar_prefetch=1,
                grid=grid,
                in_specs=[*in_specs] + [ANY] * extra,
                out_specs=out_specs,
                scratch_shapes=scratch,
            ),
            input_output_aliases=alias,
            compiler_params=pltpu.CompilerParams(vmem_limit_bytes=limit * 2**20),
            cost_estimate=pl.CostEstimate(flops=1, bytes_accessed=1 if near else 4 * 10**8, transcendentals=0),
            name=name,
        )(self.meta, *ins, *self.tokens())
        self.last = [got[0]]
        if not near:
            self.far += [g for g, spec in zip(got, out_specs) if spec is not VM]
        return got

    def tokens(self):
        return [
            pltpu.with_memory_space_constraint(t, pltpu.HBM)
            if any(t is a for a in self.far)
            else t
            for t in self.last
        ]

    def small(self, name, body, ins, outs, scratch=()):
        used, extra = len(ins), len(self.last)
        far = [any(a is b for b in self.far) for a in ins]
        held = [i for i in range(used) if far[i]]
        wait = len(held)

        def inner(meta, *refs):
            inputs, refs = list(refs[:used]), refs[used + extra :]
            outputs, refs = refs[: len(outs)], refs[len(outs) :]
            buffers, rest = refs[:wait], refs[wait:]
            moves = []
            for n, i in enumerate(held):
                moves.append(pltpu.make_async_copy(inputs[i], buffers[n], rest[0].at[n]))
                inputs[i] = buffers[n]
            for move in moves:
                move.start()
            for move in moves:
                move.wait()
            body(meta, *inputs, *outputs, *rest[1 if wait else 0 :])

        vmem = pl.BlockSpec(memory_space=pltpu.VMEM)
        got = pl.pallas_call(
            inner,
            out_shape=outs,
            in_specs=[pl.BlockSpec(memory_space=pltpu.SMEM)]
            + [ANY if f else vmem for f in far]
            + [ANY] * extra,
            out_specs=[vmem] * len(outs),
            scratch_shapes=[pltpu.VMEM(ins[i].shape, ins[i].dtype) for i in held]
            + ([pltpu.SemaphoreType.DMA((wait,))] if wait else [])
            + list(scratch),
            compiler_params=pltpu.CompilerParams(vmem_limit_bytes=20 * 2**20),
            cost_estimate=pl.CostEstimate(flops=1, bytes_accessed=1, transcendentals=0),
            name=name,
        )(
            self.meta,
            *[
                pltpu.with_memory_space_constraint(a, pltpu.HBM) if f else a
                for a, f in zip(ins, far)
            ],
            *self.tokens(),
        )
        self.last = [got[0]]
        return got


def fill(meta, pieces, target, sems, cols=None):
    count = 1 if len(pieces) == 1 else len(pieces)
    half = target.shape[0] // 8
    copies = []
    for i in range(count):
        place = meta[19] if count == 4 and i == 2 else meta[i]
        start = pl.multiple_of(place * half, half) if count > 1 else 0
        rows = pl.ds(start, pieces[i].shape[0])
        src, dst = pieces[i], target.at[rows]
        if cols is not None:
            src, dst = src.at[:, cols], target.at[rows, cols]
        copies.append(pltpu.make_async_copy(src, dst, sems.at[i]))
    return copies


def first_step(copies):
    @pl.when(pl.program_id(0) == 0)
    def _():
        for copy in copies:
            copy.start()
        for copy in copies:
            copy.wait()


def as_column(row):
    return jnp.broadcast_to(row.astype(f32), (8, row.shape[1])).T[:, :1]


def standard(v):
    center = v - jnp.mean(v, -1, keepdims=True)
    rate = lax.rsqrt(jnp.mean(center * center, -1, keepdims=True) + EPSILON)
    return center * rate, rate


def pack(order, parts):
    rows = parts[0].shape[0]
    width = sum(p.shape[1] for p in parts)
    count = len(parts)

    def body(meta, *refs):
        out, sems = refs[count:]
        moves, at = [], 0
        for i, src in enumerate(refs[:count]):
            cols = out.at[:, at : at + src.shape[1]]
            moves.append(pltpu.make_async_copy(src, cols, sems.at[i]))
            at += src.shape[1]
        for move in moves:
            move.start()
        for move in moves:
            move.wait()

    return order.run(
        "pack",
        body,
        [pltpu.with_memory_space_constraint(p, pltpu.HBM) for p in parts],
        [ANY] * count,
        [shape((rows, width), bf16)],
        [whole((rows, width))],
        (1,),
        [pltpu.SemaphoreType.DMA((count,))],
        0,
        16,
        near=True,
    )[0]


def gate(order, value):
    return order.run(
        "gate",
        lambda meta, *refs: None,
        [value],
        [ANY],
        [shape(value.shape, value.dtype)],
        [ANY],
        (1,),
        [],
        0,
        16,
        alias={1: 0},
        near=True,
    )[0]


def copies(order, halves, wholes=()):
    ins = [*halves, *wholes]
    dims = [(a.shape[0] // 2, a.shape[1]) for a in halves] + [a.shape for a in wholes]

    def body(meta, *refs):
        for i, (src, dst) in enumerate(zip(refs[: len(ins)], refs[len(ins) :])):
            if i < len(halves):
                half = dst.shape[0]
                dst[...] = src[pl.ds(pl.multiple_of(meta[13] * half, half), half)]
            else:
                dst[...] = src[...]

    return order.small("copies", body, ins, [shape(d, bf16) for d in dims])


def sums_of(order, *plan):
    ins = []
    for parts in plan:
        for array, _ in sum(parts, []):
            if not any(array is other for other in ins):
                ins.append(array)
    where = lambda array: [i for i, other in enumerate(ins) if other is array][0]
    places = [[[(where(a), index) for a, index in terms] for terms in parts] for parts in plan]

    def body(meta, *refs):
        for parts, out in zip(places, refs[len(ins) :]):
            at = 0
            for terms in parts:
                total = None
                for i, index in terms:
                    term = refs[i][index].astype(f32)
                    total = term if total is None else total + term
                rows = slice(at, at + total.shape[-2])
                out[..., rows, :] = total.astype(bf16)
                at += total.shape[-2]

    outs = []
    for parts in plan:
        dims = [
            jax.eval_shape(lambda a, i=terms[0][1]: a[i], terms[0][0]).shape for terms in parts
        ]
        rows = sum(d[-2] for d in dims)
        outs.append(shape((*dims[0][:-2], rows, dims[0][-1]), bf16))
    return order.small("sums_of", body, ins, outs)


def pick(order, own, got):
    def body(meta, own, got, out):
        inner = jnp.full(out.shape, meta[14], jnp.int32) == 1
        out[...] = jnp.where(inner, own[...], got[...])

    return order.small("pick", body, [own, got], [shape(own.shape, bf16)])[0]


def deal(order, parts):
    flat = [a for arrays in parts for a in arrays]
    size = -(-sum(arrays[0].shape[0] for arrays in parts) // 64) * 16

    def body(meta, *refs):
        ins, outs, held = refs[: len(flat)], refs[len(flat) : -1], refs[-1]
        held[...] = jnp.zeros_like(held)
        i, at = 0, 0
        for arrays in parts:
            total = None
            for ref in ins[i : i + len(arrays)]:
                term = ref[...].astype(f32)
                total = term if total is None else total + term
            i += len(arrays)
            held[at : at + total.shape[0]] = total.astype(bf16)
            at += total.shape[0]
        for j in range(4):
            outs[j][...] = held[pl.ds(pl.multiple_of(meta[20 + j] * size, size), size)]

    outs = [shape((size, D), bf16)] * 4
    return order.small("deal", body, flat, outs, [pltpu.VMEM((4 * size, D), bf16)])


def undeal(order, bands):
    size = bands[0].shape[0]

    def body(meta, *refs):
        for j in range(4):
            rows = pl.ds(pl.multiple_of(meta[20 + j] * size, size), size)
            refs[4][rows] = refs[j][...]

    return order.small("undeal", body, bands, [shape((4 * size, D), bf16)])[0]


def turn(order, *pairs):
    def body(meta, *refs):
        ins, outs = refs[:8], refs[8:]
        for i, out in enumerate(outs):
            own, got = ins[2 * i], ins[2 * i + 1]
            if i == 2:
                inner = jnp.full(out.shape, meta[14], jnp.int32) == 1
                out[...] = jnp.where(inner, own[...], got[...])
            else:
                out[...] = (own[...].astype(f32) + got[...].astype(f32)).astype(out.dtype)

    outs = [shape(a.shape, a.dtype) for a in pairs[::2]]
    return order.small("turn", body, list(pairs), outs)


def finish(order, half, pairs, plan, last=None):
    flat = [a for pair in pairs for a in pair]

    def body(meta, *refs):
        core = meta[13]
        for (width, parts), out in zip(plan, refs[len(flat) :]):
            at = 0
            for which, block, first, cols in parts:
                for i in range(2):
                    place = core if i == 0 else 1 - core
                    rows = pl.ds(pl.multiple_of(place * half, half), half)
                    value = refs[2 * which + i][
                        block * half : (block + 1) * half, first : first + cols
                    ]
                    out[rows, at : at + cols] = value.astype(f32)
                at += cols
        if last:
            own, other = [ref[last].astype(f32) for ref in refs[:2]]
            refs[-1][...] = own + other

    outs = [shape((2 * half, width), f32) for width, _ in plan]
    if last:
        outs.append(shape((last.stop - last.start, D), f32))
    return order.run(
        "finish",
        body,
        flat,
        [VM] * len(flat),
        outs,
        [whole(o.shape) for o in outs],
        (1,),
        [],
        0,
        24,
    )


def attend(order, tokens, vec, segs, pieces, at_seq, before):
    count = len(pieces)
    rows = tokens.shape[0]
    seqs = rows // LEN
    held = 0 if before is None else len(before)

    def body(meta, tok, vec, seg, *rest):
        pieces, rest = rest[:count], rest[count + held :]
        fn_t, q, k, v, att, att_t, expo, inv, bias, w, sems = rest
        p = pl.program_id(0)

        @pl.when(p == 0)
        def _():
            copies = fill(meta, pieces, w, sems)
            for copy in copies:
                copy.start()
            row = seg[0].astype(f32)
            bias[...] = jnp.where(as_column(row) == row, 0.0, -1e30)
            normed = standard(tok[...].astype(f32))[0] * vec[0:1] + vec[1:2]
            low = normed.astype(bf16)
            fn_t[...] = low.T
            for copy in copies:
                copy.wait()
            q[...] = ((dot(low, w[:, :D]) + vec[2:3]) * (LOG2E * HEAD**-0.5)).astype(bf16)
            k[...] = dot(low, w[:, D : 2 * D]).astype(bf16)
            v[...] = (dot(low, w[:, 2 * D :]) + vec[3:4]).astype(bf16)

        lane = lax.broadcasted_iota(jnp.int32, (LEN, PAIR), 1)
        mine_cols = pl.ds(pl.multiple_of(p * PAIR, PAIR), PAIR)
        vt = v[:, mine_cols].T
        keys = k[:, mine_cols]
        queries = q[:, mine_cols]
        parts = []
        for h in range(2):
            mine = (lane < HEAD) if h == 0 else (lane >= HEAD)
            scores = dot(jnp.where(mine, keys, 0).astype(bf16), queries, NT) + bias[...]
            e = jnp.exp2(scores - jnp.max(scores, 0, keepdims=True))
            rate = 1.0 / jnp.sum(e, 0, keepdims=True)
            low = e.astype(bf16)
            expo[h] = low
            inv[0, h : h + 1] = rate
            parts.append(dot(vt[HEAD * h : HEAD * h + HEAD], low) * rate)
        both = jnp.concatenate(parts, 0)
        att_t[...] = both.astype(bf16)
        att[...] = both.T.astype(bf16)

    seq = pl.BlockSpec((LEN, D), lambda p, m: (at_seq, 0))
    ins = [tokens, vec, segs.reshape(seqs, 1, LEN), *pieces]
    alias = {}
    if before is not None:
        alias = {1 + len(ins) + i: i for i in range(held)}
        ins += before
    return order.run(
        "attend",
        body,
        ins,
        [
            seq,
            whole((8, D)),
            pl.BlockSpec((1, 1, LEN), lambda p, m: (at_seq, 0, 0)),
        ]
        + [ANY] * (count + held),
        [
            shape((D, rows), bf16),
            shape((rows, D), bf16),
            shape((rows, D), bf16),
            shape((rows, D), bf16),
            shape((rows, D), bf16),
            shape((D, rows), bf16),
            shape((seqs * HEADS, LEN, LEN), bf16),
            shape((seqs * PAIRS, 8, LEN), f32),
        ],
        [
            pl.BlockSpec((D, LEN), lambda p, m: (0, at_seq)),
            seq,
            seq,
            seq,
            pl.BlockSpec((LEN, PAIR), lambda p, m: (at_seq, p)),
            pl.BlockSpec((PAIR, LEN), lambda p, m: (p, at_seq)),
            pl.BlockSpec((2, LEN, LEN), lambda p, m: (at_seq * PAIRS + p, 0, 0)),
            pl.BlockSpec((1, 8, LEN), lambda p, m: (at_seq * PAIRS + p, 0, 0)),
        ],
        (PAIRS,),
        [
            pltpu.VMEM((LEN, LEN), f32),
            pltpu.VMEM((D, 3 * D), bf16),
            pltpu.SemaphoreType.DMA((count,)),
        ],
        LEN * D * D * 3 + LEN * LEN * D * 8,
        28,
        alias,
    )


def vectors(order, sources):
    n, share = len(sources), sources[0].shape[1]

    def body(meta, *refs):
        srcs, (vec, ub) = refs[:n], refs[n:]
        rows = []
        for s in range(n):
            total = jnp.zeros((12, share), f32)
            for i in range(n):
                total = jnp.where(meta[15 + i] == s, srcs[i][...].astype(f32), total)
            rows.append(total)
        vec[...] = jnp.concatenate([r[:8] for r in rows], 1)
        ub[...] = jnp.concatenate([r[8 + i : 9 + i] for r in rows for i in range(4)], 1)

    outs = [shape((8, D), f32), shape((1, FF), f32)]
    return order.small("vectors", body, sources, outs)


def gelu_both(x):
    size = jnp.abs(x) * 0.7071067811865476
    t = 1.0 / (1.0 + 0.3275911 * size)
    bell = jnp.exp2(x * x * (-0.5 * LOG2E))
    poly = 0.5 * 1.061405429
    for c in (-1.453152027, 1.421413741, -0.284496736, 0.254829592):
        poly = poly * t + 0.5 * c
    tail = poly * t * bell
    cdf = jnp.where(x >= 0, 1.0 - tail, tail)
    return x * cdf, cdf + x * bell * 0.3989422804014327


def feed(order, attended, tokens, out_grad, live, vec, up_bias, pieces):
    count = len(pieces)
    rows = tokens.shape[0]

    def body(meta, att, tok, og, seg, vec, ub, *rest):
        pieces, rest = rest[:count], rest[count:]
        mid, sn_t, hid, slope, gb, down_sum, w, sems, sems_up = rest
        first = fill(meta, pieces, w, sems, slice(FF, FF + D))
        others = fill(meta, pieces, w, sems_up, slice(0, FF))
        begin = pl.program_id(0) == 0
        mine = pl.ds(pl.multiple_of(pl.program_id(0) * TILE, TILE), TILE)

        @pl.when(begin)
        def _():
            for copy in [*first, *others]:
                copy.start()
            for copy in first:
                copy.wait()

        m = tok[...].astype(f32) + dot(att[...], w[:, FF:]) + vec[4:5]
        mid[...] = m
        low = (standard(m)[0] * vec[5:6] + vec[6:7]).astype(bf16)
        sn_t[:, mine] = low.T
        grad = jnp.where(as_column(seg[0]) >= 0, og[...].astype(f32), 0.0)
        gb[mine] = grad.astype(bf16)

        @pl.when(pl.program_id(0) == 0)
        def _():
            down_sum[...] = jnp.zeros_like(down_sum)

        down_sum[0:1] += column_sum(grad)

        @pl.when(begin)
        def _():
            for copy in others:
                copy.wait()

        for at in range(0, FF, 512):
            pre = dot(low, w[:, at : at + 512]) + ub[:, at : at + 512]
            act, der = gelu_both(pre)
            hid[:, at : at + 512] = act.astype(bf16)
            slope[:, at : at + 512] = der.astype(bf16)

    blk = rows_block((TILE, D))
    wide = rows_block((TILE, FF))
    return order.run(
        "feed",
        body,
        [attended, tokens, out_grad, live, vec, up_bias, *pieces],
        [blk, blk, blk, rows_block((1, 1, TILE)), whole((8, D)), whole((1, FF))] + [ANY] * count,
        [
            shape((rows, D), f32),
            shape((D, rows), bf16),
            shape((rows, FF), bf16),
            shape((rows, FF), bf16),
            shape((rows, D), bf16),
            shape((8, D), f32),
        ],
        [blk, VM, wide, wide, VM, VM],
        (rows // TILE,),
        [pltpu.VMEM((D, FF + D), bf16)] + [pltpu.SemaphoreType.DMA((count,))] * 2,
        rows * D * (FF + D) * 3,
        32,
    )


def down_out(order, hidden, mid, vec, pieces):
    count = len(pieces)
    rows = hidden.shape[0]

    def body(meta, hid, mid, vec, *rest):
        pieces, (out, w, sems) = rest[:count], rest[count:]
        first_step(fill(meta, pieces, w, sems))
        out[...] = (mid[...] + dot(hid[...], w[...]) + vec[7:8]).astype(bf16)

    blk = rows_block((TILE, D))
    return order.run(
        "down_out",
        body,
        [hidden, mid, vec, *pieces],
        [rows_block((TILE, FF)), blk, whole((8, D))] + [ANY] * count,
        [shape((rows, D), bf16)],
        [blk],
        (rows // TILE,),
        [pltpu.VMEM((FF, D), bf16), pltpu.SemaphoreType.DMA((count,))],
        rows * D * FF,
        24,
    )[0]


def normal_grad(grad, gain, hat, rate):
    inner = grad * gain
    return rate * (
        inner
        - jnp.mean(inner, -1, keepdims=True)
        - hat * jnp.mean(inner * hat, -1, keepdims=True)
    )


def back(order, slope, mid, gb, vec, downs, pieces):
    nd, count = len(downs), len(pieces)
    rows = gb.shape[0]

    def body(meta, slope, mid, gb, vec, *rest):
        downs, pieces, rest = rest[:nd], rest[nd : nd + count], rest[nd + count :]
        gpre, gmid, gattn, gatt, sums, up_sum, wd, w, sems_d, sems = rest
        first, others = fill(meta, downs, wd, sems_d), fill(meta, pieces, w, sems)
        begin = pl.program_id(0) == 0
        mine = pl.ds(pl.multiple_of(pl.program_id(0) * TILE, TILE), TILE)

        @pl.when(begin)
        def _():
            for copy in [*first, *others]:
                copy.start()
            sums[...] = jnp.zeros_like(sums)
            up_sum[...] = jnp.zeros_like(up_sum)
            for copy in first:
                copy.wait()

        for at in range(0, FF, 512):
            cols = slice(at, at + 512)
            low = (dot(gb[mine], wd[cols], NT) * slope[:, cols].astype(f32)).astype(bf16)
            gpre[:, cols] = low
            up_sum[0:1, cols] += column_sum(low.astype(f32))

        @pl.when(begin)
        def _():
            for copy in others:
                copy.wait()

        grad = dot(gpre[...], w[:, :FF], NT)
        hat, rate = standard(mid[...])
        sums[0:1] += column_sum(grad * hat)
        sums[1:2] += column_sum(grad)
        g = gb[mine].astype(f32) + normal_grad(grad, vec[5:6], hat, rate)
        gmid[...] = g
        low = g.astype(bf16)
        gattn[mine] = low
        sums[2:3] += column_sum(low.astype(f32))
        gatt[...] = dot(low, w[:, FF:], NT).astype(bf16)

    blk = rows_block((TILE, D))
    wide = rows_block((TILE, FF))
    return order.run(
        "back",
        body,
        [slope, mid, gb, vec, *downs, *pieces],
        [wide, blk, VM, whole((8, D))] + [ANY] * (nd + count),
        [
            shape((rows, FF), bf16),
            shape((rows, D), f32),
            shape((rows, D), bf16),
            shape((rows, D), bf16),
            shape((8, D), f32),
            shape((8, FF), f32),
        ],
        [wide, blk, VM, blk, VM, VM],
        (rows // TILE,),
        [
            pltpu.VMEM((FF, D), bf16),
            pltpu.VMEM((D, FF + D), bf16),
            pltpu.SemaphoreType.DMA((nd,)),
            pltpu.SemaphoreType.DMA((count,)),
        ],
        rows * D * (2 * FF + D),
        32,
    )


def attend_back(order, fn_t, q, k, v, att_t, gatt, expo, inv, first, pairs):
    rows = q.shape[0]
    count = rows // LEN
    width = PAIR * pairs

    def body(meta, q, k, v, att_t, g, expo, inv, fn_t, *rest):
        dq, dk, dv, send, own, near, far, sums, grads, held, sems = rest
        s, p = pl.program_id(0), pl.program_id(1)

        def moves():
            return [
                pltpu.make_async_copy(
                    fn_t.at[pl.ds(pl.multiple_of(meta[5 + j] * BAND, BAND), BAND)],
                    held.at[pl.ds(j * BAND, BAND)],
                    sems.at[j],
                )
                for j in range(8)
            ]

        @pl.when((s == 0) & (p == 0))
        def _():
            for copy in moves():
                copy.start()

        queries, values = q[...], v[...]
        kt = k[...].T
        gt = g[...].astype(f32).T
        both = att_t[...].astype(f32) * gt
        parts, dks, dvs = [], [], []
        for h in range(2):
            at = slice(HEAD * h, HEAD * h + HEAD)
            rate = inv[0, h : h + 1]
            delta = jnp.sum(both[at], 0, keepdims=True) * rate
            scaled = (gt[at] * rate).astype(bf16)
            e = expo[h]
            ds = (e.astype(f32) * (dot(values[:, at], scaled) - delta)).astype(bf16)
            parts.append(dot(kt[at], ds))
            dvs.append(dot(e, scaled, NT))
            dks.append(dot(ds, queries[:, at]) * LN2)
        three = (
            (jnp.concatenate(parts, 0).T * HEAD**-0.5).astype(bf16),
            jnp.concatenate(dks, 1).astype(bf16),
            jnp.concatenate(dvs, 1).astype(bf16),
        )
        mine = pl.ds(pl.multiple_of(s * LEN, LEN), LEN)
        for i, (ref, value) in enumerate(zip((dq, dk, dv), three)):
            ref[...] = value
            grads[mine, pl.ds(pl.multiple_of(i * width + p * PAIR, PAIR), PAIR)] = value

        @pl.when((s == count - 1) & (p == pairs - 1))
        def _():
            for copy in moves():
                copy.wait()
            for i in range(blocks):
                right = grads[:, i * D : (i + 1) * D]
                rows_of = slice(i * BAND, (i + 1) * BAND)
                low = dot(held[...], right).astype(bf16)
                for j in range(4):
                    send[j, rows_of] = low[j * BAND : (j + 1) * BAND]
                own[rows_of] = low[4 * BAND : 5 * BAND]
                near[rows_of] = low[5 * BAND : 6 * BAND]
                for j in range(2):
                    far[j, rows_of] = low[(6 + j) * BAND : (7 + j) * BAND]
            right = grads[...]
            sums[...] = jnp.broadcast_to(column_sum(right.astype(f32)), sums.shape)

    blk = pl.BlockSpec((LEN, PAIR), lambda s, p, m: (s, p + first))
    out = pl.BlockSpec((LEN, PAIR), lambda s, p, m: (s, p))
    blocks = 3 * width // D
    bands = [(n, blocks * BAND, D) for n in (4, 2)]
    bands = [bands[0], bands[0][1:], bands[0][1:], bands[1]]
    return order.run(
        "attend_back",
        body,
        [q, k, v, att_t, gatt, expo, inv, fn_t],
        [blk] * 3
        + [
            pl.BlockSpec((PAIR, LEN), lambda s, p, m: (p + first, s)),
            blk,
            pl.BlockSpec((2, LEN, LEN), lambda s, p, m: (s * PAIRS + p + first, 0, 0)),
            pl.BlockSpec((1, 8, LEN), lambda s, p, m: (s * PAIRS + p + first, 0, 0)),
            ANY,
        ],
        [shape((rows, width), bf16)] * 3
        + [shape(d, bf16) for d in bands]
        + [shape((8, 3 * width), f32)],
        [out] * 3 + [VM] * 5,
        (count, pairs),
        [
            pltpu.VMEM((rows, 3 * width), bf16),
            pltpu.VMEM((D, rows), bf16),
            pltpu.SemaphoreType.DMA((8,)),
        ],
        rows * LEN * PAIR * pairs * 9 + rows * D * 3 * width,
        28,
    )


def grad_first(order, dqkv, tokens, gmid, vec, pieces):
    count = len(pieces)
    rows = tokens.shape[0]
    flat = [t for chunk in dqkv for t in chunk]
    starts = [0]
    for chunk in dqkv:
        starts.append(starts[-1] + chunk[0].shape[1])

    def body(meta, tok, gmid, vec, *rest):
        grads, rest = rest[: len(flat)], rest[len(flat) :]
        pieces, (out, sums, w, sems) = rest[:count], rest[count:]
        first_step(fill(meta, pieces, w, sems))

        @pl.when(pl.program_id(0) == 0)
        def _():
            sums[...] = jnp.zeros_like(sums)

        total = None
        for i, ref in enumerate(grads):
            at = (i % 3) * D + starts[i // 3]
            term = dot(ref[...], w[:, at : at + ref.shape[1]], NT)
            total = term if total is None else total + term
        hat, rate = standard(tok[...].astype(f32))
        sums[0:1] += column_sum(total * hat)
        sums[1:2] += column_sum(total)
        out[...] = (gmid[...] + normal_grad(total, vec[0:1], hat, rate)).astype(bf16)

    blk = rows_block((TILE, D))
    return order.run(
        "grad_first",
        body,
        [tokens, gmid, vec, *flat, *pieces],
        [blk, blk, whole((8, D))] + [rows_block((TILE, t.shape[1])) for t in flat] + [ANY] * count,
        [shape((rows, D), bf16), shape((8, D), f32)],
        [blk, VM],
        (rows // TILE,),
        [pltpu.VMEM((D, 3 * D), bf16), pltpu.SemaphoreType.DMA((count,))],
        rows * D * D * 3,
        24,
    )


def down_grad(order, hidden, gb, send):
    rows = gb.shape[0]
    band = FF // 8
    first = 5 if send else 9

    def body(meta, hid, gb, *outs):
        low = dot(hid[...], gb[...], TN).astype(bf16)
        if send:
            outs[0][pl.program_id(0)] = low
            return
        at = pl.program_id(0)
        for j, out in enumerate((outs[0], outs[1], outs[2].at[0], outs[2].at[1])):

            @pl.when(at == j)
            def _(out=out):
                out[...] = low

    dims = [(4, band, D)] if send else [(band, D), (band, D), (2, band, D)]
    return order.run(
        "down_grad",
        body,
        [hidden, gb],
        [pl.BlockSpec((rows, band), lambda j, m: (0, m[first + j])), VM],
        [shape(d, bf16) for d in dims],
        [VM] * len(dims),
        (4,),
        [],
        rows * D * FF // 2,
        24,
    )


def second_grad(order, up_left, up_right, out_left, out_right):
    rows = up_right.shape[0]
    blocks = FF // D + 1

    def body(meta, up_left, out_left, up_right, out_right, send, own, near, far, held):
        mine = pl.ds(pl.multiple_of(pl.program_id(0) * BAND, BAND), BAND)

        def emit(left, right):
            held[...] = dot(left[...], right[...]).astype(bf16)
            for j in range(8):
                low = held[pl.ds(pl.multiple_of(meta[5 + j] * BAND, BAND), BAND)]
                if j < 4:
                    send[j, mine] = low
                elif j < 6:
                    (own, near)[j - 4][mine] = low
                else:
                    far[j - 6, mine] = low

        last = pl.program_id(0) == blocks - 1

        @pl.when(jnp.logical_not(last))
        def _():
            emit(up_left, up_right)

        @pl.when(last)
        def _():
            emit(out_left, out_right)

    flat = (blocks * BAND, D)
    return order.run(
        "second_grad",
        body,
        [up_left, out_left, up_right, out_right],
        [
            VM,
            whole((D, rows)),
            pl.BlockSpec((rows, D), lambda s, m: (0, jnp.minimum(s, blocks - 2))),
            VM,
        ],
        [shape((4, *flat), bf16), shape(flat, bf16), shape(flat, bf16), shape((2, *flat), bf16)],
        [VM] * 4,
        (blocks,),
        [pltpu.VMEM((D, D), bf16)],
        rows * D * blocks * D,
        28,
    )


def collect(order, first_sums, chunk_sums, mid_sums, down_sum, up_sum):
    def body(meta, first, *refs):
        chunks, (mid, down, up, out) = refs[:-4], refs[-4:]
        out[...] = jnp.zeros_like(out)
        out[0:2] = first[0:2]
        at = 0
        for ref in chunks:
            w = ref.shape[1] // 3
            out[2:3, at : at + w] = ref[0:1, :w]
            out[3:4, at : at + w] = ref[0:1, 2 * w :]
            at += w
        out[4:5] = mid[2:3]
        out[5:7] = mid[0:2]
        out[7:8] = down[0:1]
        for i in range(FF // D):
            out[8 + i : 9 + i] = up[0:1, i * D : (i + 1) * D]

    ins = [first_sums, *chunk_sums, mid_sums, down_sum, up_sum]
    return order.small("collect", body, ins, [shape((16, D), f32)])[0]


class Links:
    def __init__(self, mesh):
        self.wide, self.narrow = mesh.shape["wide"], mesh.shape["narrow"]
        self.paired = self.wide == 8 and self.narrow == 4

    def move(self, value, target):
        pairs = []
        for w in range(self.wide):
            for n in range(self.narrow):
                to = target(w, n)
                if to is not None:
                    pairs.append((w * self.narrow + n, to[0] * self.narrow + to[1]))
        return lax.ppermute(value, ("wide", "narrow"), pairs)

    def swap(self, value):
        return self.move(value, lambda w, n: (w ^ 1, n))

    def near(self, value):
        return self.move(value, lambda w, n: (w, n ^ (1 + (w & 1))))

    def far(self, value):
        return self.move(value, lambda w, n: (w, n ^ (2 - (w & 1))))

    def along(self, value, step):
        return self.move(value, lambda w, n: (w, n ^ step))

    def level(self, value, step):
        return self.move(value, lambda w, n: (w ^ (2 * step), n))

    def meta(self):
        table = []
        for w in range(self.wide):
            for n in range(self.narrow):
                core, level = w & 1, w >> 1
                a, b, d = n ^ (1 + core), n ^ (2 - core), n ^ 3
                if not self.paired:
                    row = [0] * 5 + list(range(8)) + [0, 0] + list(range(self.narrow))
                    row += [0] * (24 - len(row))
                else:
                    row = [2 * n, 2 * a, 2 * d + core, 2 * b, 2 * d + 1 - core]
                    row += [2 * s + 1 - core for s in (n, a, b, d)]
                    row += [2 * s + core for s in (n, b, a, d)]
                    row += [core, int(level in (1, 2)), n, n ^ 1, n ^ 2, d]
                    row += [2 * d] + [level ^ j for j in range(4)]
                table.append(row)
        place = lax.axis_index(("wide", "narrow"))
        return lax.dynamic_index_in_dim(jnp.array(table, jnp.int32), place, keepdims=False)

    def shares(self, packed):
        if not self.paired:
            sources = lax.all_gather(packed, "narrow", axis=0)
            return [sources[i] for i in range(self.narrow)]
        return [packed] + [self.along(packed, i) for i in (1, 2, 3)]

    def inward(self, value):
        return self.move(value, lambda w, n: {0: (w + 2, n), 3: (w - 2, n)}.get(w >> 1))

    def across(self, value):
        return self.move(value, lambda w, n: {1: (w + 2, n), 2: (w - 2, n)}.get(w >> 1))

    def outward(self, value):
        return self.move(value, lambda w, n: {1: (w - 2, n), 2: (w + 2, n)}.get(w >> 1))

    def levels(self, bands):
        return [self.level(bands[j], j) for j in (1, 2, 3)]

    def whole_sum(self, sent, own, near, far):
        rest = own.shape[0]
        band = rest if rest == FF // 8 else BAND
        full = jnp.concatenate([sent, own[None], near[None], far], 0)
        full = full.reshape(8, rest // band, band, D)
        mine = lax.psum_scatter(full, "narrow", scatter_dimension=0, tiled=True)
        mine = lax.psum(mine, "wide").transpose(1, 0, 2, 3).reshape(rest // band, -1, D)
        half = mine.shape[1] // 2
        return mine[:, :half].reshape(-1, D), mine[:, half:].reshape(-1, D)


def finish_second(order, pair, half):
    blocks = FF // D
    plan = [(FF, [(0, i, 0, D) for i in range(blocks)]), (D, [(0, blocks, 0, D)])]
    return finish(order, half, [pair], plan)


def finish_down(order, pair):
    return finish(order, pair[0].shape[0], [pair], [(D, [(0, 0, 0, D)])])[0]


def split(got):
    return got[:3], got[3:]


def layer(links, *args):
    (
        tokens,
        segment_ids,
        out_grad,
        first_gain,
        first_shift,
        query_weight,
        query_bias,
        key_weight,
        value_weight,
        value_bias,
        output_weight,
        output_bias,
        second_gain,
        second_shift,
        up_weight,
        up_bias,
        down_weight,
        down_bias,
    ) = args
    order = Order(links.meta())
    paired = links.paired
    share = first_gain.shape[0]
    gather = lambda v: [lax.all_gather(v, "narrow", axis=0, tiled=True)]
    small = (
        first_gain,
        first_shift,
        query_bias,
        value_bias,
        output_bias,
        second_gain,
        second_shift,
        down_bias,
    )
    live = segment_ids.reshape(-1, 1, TILE)

    pack_one = pack(order, [query_weight, key_weight, value_weight])
    pack_two = pack(order, [up_weight, output_weight])
    shares = links.shares(jnp.concatenate([*small, up_bias]).reshape(-1, share))
    if paired:
        near_one = links.near(pack_one)
        far_one, got_one = links.far(near_one), links.swap(near_one)
        w_one = [pack_one, near_one, far_one, got_one]
        order.last.append(got_one)
    vec, up_b = vectors(order, shares)
    if not paired:
        w_one = gather(pack_one)
    if paired:
        order.last.append(far_one)
        pack_two = gate(order, pack_two)
    kept = attend(order, tokens, vec, segment_ids, w_one, 0, None)
    if paired:
        near_two = links.near(pack_two)
        half_two, down_copy = copies(order, [near_two], [down_weight])
        far_two = links.far(half_two)
        got_two, near_down = links.swap(near_two), links.near(down_copy)
    else:
        w_two = gather(pack_two)
    for s in range(1, tokens.shape[0] // LEN):
        kept = attend(order, tokens, vec, segment_ids, w_one, s, list(kept))
    fn_t, q, k, v, att, att_t, expo, inv = kept
    if paired:
        down_half, far_two = copies(order, [down_weight], [far_two])
        w_two = [pack_two, near_two, far_two, got_two, links.swap(far_two)]
        far_down = links.along(down_half, 3)
    else:
        w_down = gather(down_weight)
    mid, sn_t, hidden, slope, gb, down_sum = feed(
        order, att, tokens, out_grad, live, vec, up_b, w_two
    )

    if paired:
        near_down, far_down = copies(order, [], [near_down, far_down])
        w_down = [down_weight, near_down, far_down, links.swap(near_down), links.swap(far_down)]
    (d_send,) = down_grad(order, hidden, gb, True)
    d_own, d_near, d_far = down_grad(order, hidden, gb, False)
    if paired:
        d_got = links.swap(d_send)
    every, pair = ..., slice(2, 4)
    if paired:
        (d_far,) = sums_of(order, [[(d_far, every), (d_got, pair)]])
        d_got2 = links.near(d_far)
    gpre, gmid, gattn, gatt, mid_sums, up_sum = back(order, slope, mid, gb, vec, w_down, w_two)
    if paired:
        d_near, d_own = sums_of(
            order,
            [[(d_near, every), (d_got, 1), (d_got2, 1)]],
            [[(d_own, every), (d_got, 0), (d_got2, 0)]],
        )
        d_got = links.far(d_near)
    s_send, s_own, s_near, s_far = second_grad(order, sn_t, gpre, att_t, gattn)
    if paired:
        s_got = links.swap(s_send)
        (s_far,) = sums_of(order, [[(s_far, every), (s_got, pair)]])
        s_got2 = links.near(s_far)
    c_three, (c_send, c_own, c_near, c_far, c_sums) = split(
        attend_back(order, fn_t, q, k, v, att_t, gatt, expo, inv, 0, CHUNKS[0])
    )
    if paired:
        c_got = links.swap(c_send)
        s_near, s_own, d_own = sums_of(
            order,
            [[(s_near, every), (s_got, 1), (s_got2, 1)]],
            [[(s_own, every), (s_got, 0), (s_got2, 0)]],
            [[(d_own, every), (d_got, every)]],
        )
        s_got = links.far(s_near)
        d_got = links.inward(d_own)
    e_three, (e_send, e_own, e_near, e_far, e_sums) = split(
        attend_back(order, fn_t, q, k, v, att_t, gatt, expo, inv, CHUNKS[0], CHUNKS[1])
    )
    if paired:
        e_got = links.swap(copies(order, [], [e_send])[0])
        s_own, d_own = sums_of(
            order, [[(s_own, every), (s_got, every)]], [[(d_own, every), (d_got, every)]]
        )
        s_got, d_got = links.inward(s_own), links.across(d_own)
        (g_far,) = sums_of(
            order, [[(c_far, every), (c_got, pair)], [(e_far, every), (e_got, pair)]]
        )
        g_got = links.near(g_far)
    input_grad, first_sums = grad_first(
        order, [c_three, e_three], tokens, gmid, vec, w_one
    )
    if paired:
        s_own, d_own = sums_of(
            order, [[(s_own, every), (s_got, every)]], [[(d_own, every), (d_got, every)]]
        )
        s_got, d_got = links.across(s_own), links.outward(d_own)
    total = collect(order, first_sums, [c_sums, e_sums], mid_sums, down_sum, up_sum)
    if paired:
        t_got = links.near(total)
        cut = c_own.shape[0]
        low, high = (slice(0, cut), slice(None)), (slice(cut, None), slice(None))
        g_near, g_own = sums_of(
            order,
            [
                [(c_near, every), (c_got, 1), (g_got, (1, *low))],
                [(e_near, every), (e_got, 1), (g_got, (1, *high))],
            ],
            [
                [(c_own, every), (c_got, 0), (g_got, (0, *low))],
                [(e_own, every), (e_got, 0), (g_got, (0, *high))],
            ],
        )
        g_got = links.far(g_near)
    layer_out = down_out(order, hidden, mid, vec, w_down)
    if paired:
        g_own, s_own, d_own, total = turn(
            order, g_own, g_got, s_own, s_got, d_own, d_got, total, t_got
        )
        t_got, s_got = links.far(total), links.outward(s_own)
        d_pair = (d_own, links.swap(d_own))
        g_bands = deal(order, [[g_own], [total, t_got]])
        g_gots = links.levels(g_bands)
        down_weight_grad = finish_down(order, d_pair)
        (g_mine,) = sums_of(order, [[(b, every) for b in [g_bands[0], *g_gots]]])
        g_gots = links.levels([g_mine] * 4)
        s_own = pick(order, s_own, s_got)
        s_pair = (s_own, links.swap(s_own))
        up_weight_grad, output_weight_grad = finish_second(order, s_pair, share // 2)
        g_own = undeal(order, [g_mine, *g_gots])
        g_pair = (g_own, links.swap(g_own))
    else:
        s_pair = links.whole_sum(s_send, s_own, s_near, s_far)
        d_pair = links.whole_sum(d_send, d_own, d_near, d_far)
        c_pair = links.whole_sum(c_send, c_own, c_near, c_far)
        e_pair = links.whole_sum(e_send, e_own, e_near, e_far)
        g_pair = [jnp.concatenate([c, e], 0) for c, e in zip(c_pair, e_pair)]
        total = lax.psum(total, ("wide", "narrow"))
        down_weight_grad = finish_down(order, d_pair)
        up_weight_grad, output_weight_grad = finish_second(order, s_pair, share // 2)
    half = share // 2
    plan = []
    for i in range(3):
        parts = []
        for c, pairs in enumerate(CHUNKS):
            at, stop = i * PAIR * pairs, (i + 1) * PAIR * pairs
            while at < stop:
                end = min(stop, (at // D + 1) * D)
                block = at // D + c * (3 * PAIR * CHUNKS[0] // D)
                parts.append((0, block, at % D, end - at))
                at = end
        plan.append((D, parts))
    place = slice(BAND * 3, BAND * 3 + 16) if paired else None
    first_grads = finish(order, half, [g_pair], plan, place)
    if paired:
        total = first_grads[3]

    n = lax.axis_index("narrow")
    mine = lax.dynamic_slice_in_dim(total[:8], n * share, share, 1)
    up_share = up_bias.shape[0]
    up_mine = lax.dynamic_slice_in_dim(total[8:12].reshape(FF), n * up_share, up_share)
    return (
        layer_out,
        input_grad,
        mine[0],
        mine[1],
        first_grads[0],
        mine[2],
        first_grads[1],
        first_grads[2],
        mine[3],
        output_weight_grad,
        mine[4],
        mine[5],
        mine[6],
        up_weight_grad,
        up_mine,
        down_weight_grad,
        mine[7],
    )


def solution(mesh):
    rows, vector, matrix = P(("wide", "narrow"), None), P("narrow"), P("narrow", None)
    in_specs = (rows, P(("wide", "narrow")), rows) + tuple(
        matrix if i in (2, 4, 5, 7, 11, 13) else vector for i in range(15)
    )
    out_specs = (rows, rows) + in_specs[3:]
    return jax.shard_map(
        functools.partial(layer, Links(mesh)),
        mesh=mesh,
        in_specs=in_specs,
        out_specs=out_specs,
        check_vma=False,
    )
```

```python
import functools

import jax
import jax.numpy as jnp
from jax import lax
from jax.experimental import pallas as pl
from jax.experimental.pallas import tpu as pltpu
from jax.sharding import PartitionSpec as P

D = 768
HEADS = 12
HEAD = 64
LEN = 512
FF = 3072
EPSILON = 1e-06
TILE = 256
BAND = D // 8
PAIR = 2 * HEAD
PAIRS = HEADS // 2
CHUNKS = (4, 2)
LOG2E = 1.4426950408889634
LN2 = 0.6931471805599453

bf16 = jnp.bfloat16
f32 = jnp.float32
NN = (((1,), (0,)), ((), ()))
NT = (((1,), (1,)), ((), ()))
TN = (((0,), (0,)), ((), ()))
ANY = pl.BlockSpec(memory_space=pl.ANY)
VM = pl.BlockSpec(memory_space=pltpu.VMEM)


def dot(left, right, dims=NN):
    return lax.dot_general(left, right, dims, preferred_element_type=f32)


def shape(dims, kind):
    return jax.ShapeDtypeStruct(dims, kind)


def column_sum(values):
    return jnp.sum(values, 0, keepdims=True)


def whole(dims):
    return pl.BlockSpec(dims, lambda *at: (0,) * len(dims))


def rows_block(dims):
    return pl.BlockSpec(dims, lambda at, *rest: (at,) + (0,) * (len(dims) - 1))


class Order:
    def __init__(self, meta):
        self.meta, self.last, self.far = meta, [], []

    def run(
        self,
        name,
        body,
        ins,
        in_specs,
        outs,
        out_specs,
        grid,
        scratch,
        macs,
        limit,
        alias={},
        near=False,
    ):
        moved = sum(a.size * a.dtype.itemsize for a in ins)
        moved += sum(o.size * o.dtype.itemsize for o in outs)
        used, extra = len(ins), len(self.last)

        def inner(meta, *refs):
            body(meta, *refs[:used], *refs[used + extra :])

        ins = [
            a if spec is ANY or spec is VM else pltpu.with_memory_space_constraint(a, pltpu.HBM)
            for a, spec in zip(ins, in_specs)
        ]
        if not near:
            outs = [
                (pltpu.VMEM if spec is VM else pltpu.HBM)(o.shape, o.dtype)
                for o, spec in zip(outs, out_specs)
            ]
        got = pl.pallas_call(
            inner,
            out_shape=outs,
            grid_spec=pltpu.PrefetchScalarGridSpec(
                num_scalar_prefetch=1,
                grid=grid,
                in_specs=[*in_specs] + [ANY] * extra,
                out_specs=out_specs,
                scratch_shapes=scratch,
            ),
            input_output_aliases=alias,
            compiler_params=pltpu.CompilerParams(vmem_limit_bytes=limit * 2**20),
            cost_estimate=pl.CostEstimate(flops=1, bytes_accessed=1 if near else 4 * 10**8, transcendentals=0),
            name=name,
        )(self.meta, *ins, *self.tokens())
        self.last = [got[0]]
        if not near:
            self.far += [g for g, spec in zip(got, out_specs) if spec is not VM]
        return got

    def tokens(self):
        return [
            pltpu.with_memory_space_constraint(t, pltpu.HBM)
            if any(t is a for a in self.far)
            else t
            for t in self.last
        ]

    def small(self, name, body, ins, outs, scratch=()):
        used, extra = len(ins), len(self.last)
        far = [any(a is b for b in self.far) for a in ins]
        held = [i for i in range(used) if far[i]]
        wait = len(held)

        def inner(meta, *refs):
            inputs, refs = list(refs[:used]), refs[used + extra :]
            outputs, refs = refs[: len(outs)], refs[len(outs) :]
            buffers, rest = refs[:wait], refs[wait:]
            moves = []
            for n, i in enumerate(held):
                moves.append(pltpu.make_async_copy(inputs[i], buffers[n], rest[0].at[n]))
                inputs[i] = buffers[n]
            for move in moves:
                move.start()
            for move in moves:
                move.wait()
            body(meta, *inputs, *outputs, *rest[1 if wait else 0 :])

        vmem = pl.BlockSpec(memory_space=pltpu.VMEM)
        got = pl.pallas_call(
            inner,
            out_shape=outs,
            in_specs=[pl.BlockSpec(memory_space=pltpu.SMEM)]
            + [ANY if f else vmem for f in far]
            + [ANY] * extra,
            out_specs=[vmem] * len(outs),
            scratch_shapes=[pltpu.VMEM(ins[i].shape, ins[i].dtype) for i in held]
            + ([pltpu.SemaphoreType.DMA((wait,))] if wait else [])
            + list(scratch),
            compiler_params=pltpu.CompilerParams(vmem_limit_bytes=20 * 2**20),
            cost_estimate=pl.CostEstimate(flops=1, bytes_accessed=1, transcendentals=0),
            name=name,
        )(
            self.meta,
            *[
                pltpu.with_memory_space_constraint(a, pltpu.HBM) if f else a
                for a, f in zip(ins, far)
            ],
            *self.tokens(),
        )
        self.last = [got[0]]
        return got


def fill(meta, pieces, target, sems, cols=None):
    count = 1 if len(pieces) == 1 else len(pieces)
    half = target.shape[0] // 8
    copies = []
    for i in range(count):
        place = meta[19] if count == 4 and i == 2 else meta[i]
        start = pl.multiple_of(place * half, half) if count > 1 else 0
        rows = pl.ds(start, pieces[i].shape[0])
        src, dst = pieces[i], target.at[rows]
        if cols is not None:
            src, dst = src.at[:, cols], target.at[rows, cols]
        copies.append(pltpu.make_async_copy(src, dst, sems.at[i]))
    return copies


def first_step(copies):
    @pl.when(pl.program_id(0) == 0)
    def _():
        for copy in copies:
            copy.start()
        for copy in copies:
            copy.wait()


def as_column(row):
    return jnp.broadcast_to(row.astype(f32), (8, row.shape[1])).T[:, :1]


def standard(v):
    center = v - jnp.mean(v, -1, keepdims=True)
    rate = lax.rsqrt(jnp.mean(center * center, -1, keepdims=True) + EPSILON)
    return center * rate, rate


def pack(order, parts):
    rows = parts[0].shape[0]
    width = sum(p.shape[1] for p in parts)
    count = len(parts)

    def body(meta, *refs):
        out, sems = refs[count:]
        moves, at = [], 0
        for i, src in enumerate(refs[:count]):
            cols = out.at[:, at : at + src.shape[1]]
            moves.append(pltpu.make_async_copy(src, cols, sems.at[i]))
            at += src.shape[1]
        for move in moves:
            move.start()
        for move in moves:
            move.wait()

    return order.run(
        "pack",
        body,
        [pltpu.with_memory_space_constraint(p, pltpu.HBM) for p in parts],
        [ANY] * count,
        [shape((rows, width), bf16)],
        [whole((rows, width))],
        (1,),
        [pltpu.SemaphoreType.DMA((count,))],
        0,
        16,
        near=True,
    )[0]


def gate(order, value):
    return order.run(
        "gate",
        lambda meta, *refs: None,
        [value],
        [ANY],
        [shape(value.shape, value.dtype)],
        [ANY],
        (1,),
        [],
        0,
        16,
        alias={1: 0},
        near=True,
    )[0]


def copies(order, halves, wholes=()):
    ins = [*halves, *wholes]
    dims = [(a.shape[0] // 2, a.shape[1]) for a in halves] + [a.shape for a in wholes]

    def body(meta, *refs):
        for i, (src, dst) in enumerate(zip(refs[: len(ins)], refs[len(ins) :])):
            if i < len(halves):
                half = dst.shape[0]
                dst[...] = src[pl.ds(pl.multiple_of(meta[13] * half, half), half)]
            else:
                dst[...] = src[...]

    return order.small("copies", body, ins, [shape(d, bf16) for d in dims])


def sums_of(order, *plan):
    ins = []
    for parts in plan:
        for array, _ in sum(parts, []):
            if not any(array is other for other in ins):
                ins.append(array)
    where = lambda array: [i for i, other in enumerate(ins) if other is array][0]
    places = [[[(where(a), index) for a, index in terms] for terms in parts] for parts in plan]

    def body(meta, *refs):
        for parts, out in zip(places, refs[len(ins) :]):
            at = 0
            for terms in parts:
                total = None
                for i, index in terms:
                    term = refs[i][index].astype(f32)
                    total = term if total is None else total + term
                rows = slice(at, at + total.shape[-2])
                out[..., rows, :] = total.astype(bf16)
                at += total.shape[-2]

    outs = []
    for parts in plan:
        dims = [
            jax.eval_shape(lambda a, i=terms[0][1]: a[i], terms[0][0]).shape for terms in parts
        ]
        rows = sum(d[-2] for d in dims)
        outs.append(shape((*dims[0][:-2], rows, dims[0][-1]), bf16))
    return order.small("sums_of", body, ins, outs)


def pick(order, own, got):
    def body(meta, own, got, out):
        inner = jnp.full(out.shape, meta[14], jnp.int32) == 1
        out[...] = jnp.where(inner, own[...], got[...])

    return order.small("pick", body, [own, got], [shape(own.shape, bf16)])[0]


def deal(order, parts):
    flat = [a for arrays in parts for a in arrays]
    size = -(-sum(arrays[0].shape[0] for arrays in parts) // 64) * 16

    def body(meta, *refs):
        ins, outs, held = refs[: len(flat)], refs[len(flat) : -1], refs[-1]
        held[...] = jnp.zeros_like(held)
        i, at = 0, 0
        for arrays in parts:
            total = None
            for ref in ins[i : i + len(arrays)]:
                term = ref[...].astype(f32)
                total = term if total is None else total + term
            i += len(arrays)
            held[at : at + total.shape[0]] = total.astype(bf16)
            at += total.shape[0]
        for j in range(4):
            outs[j][...] = held[pl.ds(pl.multiple_of(meta[20 + j] * size, size), size)]

    outs = [shape((size, D), bf16)] * 4
    return order.small("deal", body, flat, outs, [pltpu.VMEM((4 * size, D), bf16)])


def undeal(order, bands):
    size = bands[0].shape[0]

    def body(meta, *refs):
        for j in range(4):
            rows = pl.ds(pl.multiple_of(meta[20 + j] * size, size), size)
            refs[4][rows] = refs[j][...]

    return order.small("undeal", body, bands, [shape((4 * size, D), bf16)])[0]


def turn(order, *pairs):
    def body(meta, *refs):
        ins, outs = refs[:8], refs[8:]
        for i, out in enumerate(outs):
            own, got = ins[2 * i], ins[2 * i + 1]
            if i == 2:
                inner = jnp.full(out.shape, meta[14], jnp.int32) == 1
                out[...] = jnp.where(inner, own[...], got[...])
            else:
                out[...] = (own[...].astype(f32) + got[...].astype(f32)).astype(out.dtype)

    outs = [shape(a.shape, a.dtype) for a in pairs[::2]]
    return order.small("turn", body, list(pairs), outs)


def finish(order, half, pairs, plan, last=None):
    flat = [a for pair in pairs for a in pair]

    def body(meta, *refs):
        core = meta[13]
        for (width, parts), out in zip(plan, refs[len(flat) :]):
            at = 0
            for which, block, first, cols in parts:
                for i in range(2):
                    place = core if i == 0 else 1 - core
                    rows = pl.ds(pl.multiple_of(place * half, half), half)
                    value = refs[2 * which + i][
                        block * half : (block + 1) * half, first : first + cols
                    ]
                    out[rows, at : at + cols] = value.astype(f32)
                at += cols
        if last:
            own, other = [ref[last].astype(f32) for ref in refs[:2]]
            refs[-1][...] = own + other

    outs = [shape((2 * half, width), f32) for width, _ in plan]
    if last:
        outs.append(shape((last.stop - last.start, D), f32))
    return order.run(
        "finish",
        body,
        flat,
        [VM] * len(flat),
        outs,
        [whole(o.shape) for o in outs],
        (1,),
        [],
        0,
        24,
    )


def attend(order, tokens, vec, segs, pieces, at_seq, before):
    count = len(pieces)
    rows = tokens.shape[0]
    seqs = rows // LEN
    held = 0 if before is None else len(before)

    def body(meta, tok, vec, seg, *rest):
        pieces, rest = rest[:count], rest[count + held :]
        fn_t, q, k, v, att, att_t, expo, inv, bias, w, sems = rest
        p = pl.program_id(0)

        @pl.when(p == 0)
        def _():
            copies = fill(meta, pieces, w, sems)
            for copy in copies:
                copy.start()
            row = seg[0].astype(f32)
            bias[...] = jnp.where(as_column(row) == row, 0.0, -1e30)
            normed = standard(tok[...].astype(f32))[0] * vec[0:1] + vec[1:2]
            low = normed.astype(bf16)
            fn_t[...] = low.T
            for copy in copies:
                copy.wait()
            q[...] = ((dot(low, w[:, :D]) + vec[2:3]) * (LOG2E * HEAD**-0.5)).astype(bf16)
            k[...] = dot(low, w[:, D : 2 * D]).astype(bf16)
            v[...] = (dot(low, w[:, 2 * D :]) + vec[3:4]).astype(bf16)

        lane = lax.broadcasted_iota(jnp.int32, (LEN, PAIR), 1)
        mine_cols = pl.ds(pl.multiple_of(p * PAIR, PAIR), PAIR)
        vt = v[:, mine_cols].T
        keys = k[:, mine_cols]
        queries = q[:, mine_cols]
        parts = []
        for h in range(2):
            mine = (lane < HEAD) if h == 0 else (lane >= HEAD)
            scores = dot(jnp.where(mine, keys, 0).astype(bf16), queries, NT) + bias[...]
            e = jnp.exp2(scores - jnp.max(scores, 0, keepdims=True))
            rate = 1.0 / jnp.sum(e, 0, keepdims=True)
            low = e.astype(bf16)
            expo[h] = low
            inv[0, h : h + 1] = rate
            parts.append(dot(vt[HEAD * h : HEAD * h + HEAD], low) * rate)
        both = jnp.concatenate(parts, 0)
        att_t[...] = both.astype(bf16)
        att[...] = both.T.astype(bf16)

    seq = pl.BlockSpec((LEN, D), lambda p, m: (at_seq, 0))
    ins = [tokens, vec, segs.reshape(seqs, 1, LEN), *pieces]
    alias = {}
    if before is not None:
        alias = {1 + len(ins) + i: i for i in range(held)}
        ins += before
    return order.run(
        "attend",
        body,
        ins,
        [
            seq,
            whole((8, D)),
            pl.BlockSpec((1, 1, LEN), lambda p, m: (at_seq, 0, 0)),
        ]
        + [ANY] * (count + held),
        [
            shape((D, rows), bf16),
            shape((rows, D), bf16),
            shape((rows, D), bf16),
            shape((rows, D), bf16),
            shape((rows, D), bf16),
            shape((D, rows), bf16),
            shape((seqs * HEADS, LEN, LEN), bf16),
            shape((seqs * PAIRS, 8, LEN), f32),
        ],
        [
            pl.BlockSpec((D, LEN), lambda p, m: (0, at_seq)),
            seq,
            seq,
            seq,
            pl.BlockSpec((LEN, PAIR), lambda p, m: (at_seq, p)),
            pl.BlockSpec((PAIR, LEN), lambda p, m: (p, at_seq)),
            pl.BlockSpec((2, LEN, LEN), lambda p, m: (at_seq * PAIRS + p, 0, 0)),
            pl.BlockSpec((1, 8, LEN), lambda p, m: (at_seq * PAIRS + p, 0, 0)),
        ],
        (PAIRS,),
        [
            pltpu.VMEM((LEN, LEN), f32),
            pltpu.VMEM((D, 3 * D), bf16),
            pltpu.SemaphoreType.DMA((count,)),
        ],
        LEN * D * D * 3 + LEN * LEN * D * 8,
        28,
        alias,
    )


def vectors(order, sources):
    n, share = len(sources), sources[0].shape[1]

    def body(meta, *refs):
        srcs, (vec, ub) = refs[:n], refs[n:]
        rows = []
        for s in range(n):
            total = jnp.zeros((12, share), f32)
            for i in range(n):
                total = jnp.where(meta[15 + i] == s, srcs[i][...].astype(f32), total)
            rows.append(total)
        vec[...] = jnp.concatenate([r[:8] for r in rows], 1)
        ub[...] = jnp.concatenate([r[8 + i : 9 + i] for r in rows for i in range(4)], 1)

    outs = [shape((8, D), f32), shape((1, FF), f32)]
    return order.small("vectors", body, sources, outs)


def gelu_both(x):
    size = jnp.abs(x) * 0.7071067811865476
    t = 1.0 / (1.0 + 0.3275911 * size)
    bell = jnp.exp2(x * x * (-0.5 * LOG2E))
    poly = 0.5 * 1.061405429
    for c in (-1.453152027, 1.421413741, -0.284496736, 0.254829592):
        poly = poly * t + 0.5 * c
    tail = poly * t * bell
    cdf = jnp.where(x >= 0, 1.0 - tail, tail)
    return x * cdf, cdf + x * bell * 0.3989422804014327


def feed(order, attended, tokens, out_grad, live, vec, up_bias, pieces):
    count = len(pieces)
    rows = tokens.shape[0]

    def body(meta, att, tok, og, seg, vec, ub, *rest):
        pieces, rest = rest[:count], rest[count:]
        mid, sn_t, hid, slope, gb, down_sum, w, sems, sems_up = rest
        first = fill(meta, pieces, w, sems, slice(FF, FF + D))
        others = fill(meta, pieces, w, sems_up, slice(0, FF))
        begin = pl.program_id(0) == 0
        mine = pl.ds(pl.multiple_of(pl.program_id(0) * TILE, TILE), TILE)

        @pl.when(begin)
        def _():
            for copy in [*first, *others]:
                copy.start()
            for copy in first:
                copy.wait()

        m = tok[...].astype(f32) + dot(att[...], w[:, FF:]) + vec[4:5]
        mid[...] = m
        low = (standard(m)[0] * vec[5:6] + vec[6:7]).astype(bf16)
        sn_t[:, mine] = low.T
        grad = jnp.where(as_column(seg[0]) >= 0, og[...].astype(f32), 0.0)
        gb[mine] = grad.astype(bf16)

        @pl.when(pl.program_id(0) == 0)
        def _():
            down_sum[...] = jnp.zeros_like(down_sum)

        down_sum[0:1] += column_sum(grad)

        @pl.when(begin)
        def _():
            for copy in others:
                copy.wait()

        for at in range(0, FF, 512):
            pre = dot(low, w[:, at : at + 512]) + ub[:, at : at + 512]
            act, der = gelu_both(pre)
            hid[:, at : at + 512] = act.astype(bf16)
            slope[:, at : at + 512] = der.astype(bf16)

    blk = rows_block((TILE, D))
    wide = rows_block((TILE, FF))
    return order.run(
        "feed",
        body,
        [attended, tokens, out_grad, live, vec, up_bias, *pieces],
        [blk, blk, blk, rows_block((1, 1, TILE)), whole((8, D)), whole((1, FF))] + [ANY] * count,
        [
            shape((rows, D), f32),
            shape((D, rows), bf16),
            shape((rows, FF), bf16),
            shape((rows, FF), bf16),
            shape((rows, D), bf16),
            shape((8, D), f32),
        ],
        [blk, VM, wide, wide, VM, VM],
        (rows // TILE,),
        [pltpu.VMEM((D, FF + D), bf16)] + [pltpu.SemaphoreType.DMA((count,))] * 2,
        rows * D * (FF + D) * 3,
        32,
    )


def down_out(order, hidden, mid, vec, pieces):
    count = len(pieces)
    rows = hidden.shape[0]

    def body(meta, hid, mid, vec, *rest):
        pieces, (out, w, sems) = rest[:count], rest[count:]
        first_step(fill(meta, pieces, w, sems))
        out[...] = (mid[...] + dot(hid[...], w[...]) + vec[7:8]).astype(bf16)

    blk = rows_block((TILE, D))
    return order.run(
        "down_out",
        body,
        [hidden, mid, vec, *pieces],
        [rows_block((TILE, FF)), blk, whole((8, D))] + [ANY] * count,
        [shape((rows, D), bf16)],
        [blk],
        (rows // TILE,),
        [pltpu.VMEM((FF, D), bf16), pltpu.SemaphoreType.DMA((count,))],
        rows * D * FF,
        24,
    )[0]


def normal_grad(grad, gain, hat, rate):
    inner = grad * gain
    return rate * (
        inner
        - jnp.mean(inner, -1, keepdims=True)
        - hat * jnp.mean(inner * hat, -1, keepdims=True)
    )


def back(order, slope, mid, gb, vec, downs, pieces):
    nd, count = len(downs), len(pieces)
    rows = gb.shape[0]

    def body(meta, slope, mid, gb, vec, *rest):
        downs, pieces, rest = rest[:nd], rest[nd : nd + count], rest[nd + count :]
        gpre, gmid, gattn, gatt, sums, up_sum, wd, w, sems_d, sems = rest
        first, others = fill(meta, downs, wd, sems_d), fill(meta, pieces, w, sems)
        begin = pl.program_id(0) == 0
        mine = pl.ds(pl.multiple_of(pl.program_id(0) * TILE, TILE), TILE)

        @pl.when(begin)
        def _():
            for copy in [*first, *others]:
                copy.start()
            sums[...] = jnp.zeros_like(sums)
            up_sum[...] = jnp.zeros_like(up_sum)
            for copy in first:
                copy.wait()

        for at in range(0, FF, 512):
            cols = slice(at, at + 512)
            low = (dot(gb[mine], wd[cols], NT) * slope[:, cols].astype(f32)).astype(bf16)
            gpre[mine, cols] = low
            up_sum[0:1, cols] += column_sum(low.astype(f32))

        @pl.when(begin)
        def _():
            for copy in others:
                copy.wait()

        grad = dot(gpre[mine], w[:, :FF], NT)
        hat, rate = standard(mid[...])
        sums[0:1] += column_sum(grad * hat)
        sums[1:2] += column_sum(grad)
        g = gb[mine].astype(f32) + normal_grad(grad, vec[5:6], hat, rate)
        gmid[...] = g
        low = g.astype(bf16)
        gattn[mine] = low
        sums[2:3] += column_sum(low.astype(f32))
        gatt[...] = dot(low, w[:, FF:], NT).astype(bf16)

    blk = rows_block((TILE, D))
    wide = rows_block((TILE, FF))
    return order.run(
        "back",
        body,
        [slope, mid, gb, vec, *downs, *pieces],
        [wide, blk, VM, whole((8, D))] + [ANY] * (nd + count),
        [
            shape((rows, FF), bf16),
            shape((rows, D), f32),
            shape((rows, D), bf16),
            shape((rows, D), bf16),
            shape((8, D), f32),
            shape((8, FF), f32),
        ],
        [VM, blk, VM, blk, VM, VM],
        (rows // TILE,),
        [
            pltpu.VMEM((FF, D), bf16),
            pltpu.VMEM((D, FF + D), bf16),
            pltpu.SemaphoreType.DMA((nd,)),
            pltpu.SemaphoreType.DMA((count,)),
        ],
        rows * D * (2 * FF + D),
        28,
    )


def attend_back(order, fn_t, q, k, v, att_t, gatt, expo, inv, first, pairs):
    rows = q.shape[0]
    count = rows // LEN
    width = PAIR * pairs

    def body(meta, q, k, v, att_t, g, expo, inv, fn_t, *rest):
        dq, dk, dv, send, own, near, far, sums, grads, held, sems = rest
        s, p = pl.program_id(0), pl.program_id(1)

        def moves():
            return [
                pltpu.make_async_copy(
                    fn_t.at[pl.ds(pl.multiple_of(meta[5 + j] * BAND, BAND), BAND)],
                    held.at[pl.ds(j * BAND, BAND)],
                    sems.at[j],
                )
                for j in range(8)
            ]

        @pl.when((s == 0) & (p == 0))
        def _():
            for copy in moves():
                copy.start()

        queries, values = q[...], v[...]
        kt = k[...].T
        gt = g[...].astype(f32).T
        both = att_t[...].astype(f32) * gt
        parts, dks, dvs = [], [], []
        for h in range(2):
            at = slice(HEAD * h, HEAD * h + HEAD)
            rate = inv[0, h : h + 1]
            delta = jnp.sum(both[at], 0, keepdims=True) * rate
            scaled = (gt[at] * rate).astype(bf16)
            e = expo[h]
            ds = (e.astype(f32) * (dot(values[:, at], scaled) - delta)).astype(bf16)
            parts.append(dot(kt[at], ds))
            dvs.append(dot(e, scaled, NT))
            dks.append(dot(ds, queries[:, at]) * LN2)
        three = (
            (jnp.concatenate(parts, 0).T * HEAD**-0.5).astype(bf16),
            jnp.concatenate(dks, 1).astype(bf16),
            jnp.concatenate(dvs, 1).astype(bf16),
        )
        mine = pl.ds(pl.multiple_of(s * LEN, LEN), LEN)
        for i, (ref, value) in enumerate(zip((dq, dk, dv), three)):
            ref[...] = value
            grads[mine, pl.ds(pl.multiple_of(i * width + p * PAIR, PAIR), PAIR)] = value

        @pl.when((s == count - 1) & (p == pairs - 1))
        def _():
            for copy in moves():
                copy.wait()
            for i in range(blocks):
                right = grads[:, i * D : (i + 1) * D]
                rows_of = slice(i * BAND, (i + 1) * BAND)
                low = dot(held[...], right).astype(bf16)
                for j in range(4):
                    send[j, rows_of] = low[j * BAND : (j + 1) * BAND]
                own[rows_of] = low[4 * BAND : 5 * BAND]
                near[rows_of] = low[5 * BAND : 6 * BAND]
                for j in range(2):
                    far[j, rows_of] = low[(6 + j) * BAND : (7 + j) * BAND]
            right = grads[...]
            sums[...] = jnp.broadcast_to(column_sum(right.astype(f32)), sums.shape)

    blk = pl.BlockSpec((LEN, PAIR), lambda s, p, m: (s, p + first))
    out = pl.BlockSpec((LEN, PAIR), lambda s, p, m: (s, p))
    blocks = 3 * width // D
    bands = [(n, blocks * BAND, D) for n in (4, 2)]
    bands = [bands[0], bands[0][1:], bands[0][1:], bands[1]]
    return order.run(
        "attend_back",
        body,
        [q, k, v, att_t, gatt, expo, inv, fn_t],
        [blk] * 3
        + [
            pl.BlockSpec((PAIR, LEN), lambda s, p, m: (p + first, s)),
            blk,
            pl.BlockSpec((2, LEN, LEN), lambda s, p, m: (s * PAIRS + p + first, 0, 0)),
            pl.BlockSpec((1, 8, LEN), lambda s, p, m: (s * PAIRS + p + first, 0, 0)),
            ANY,
        ],
        [shape((rows, width), bf16)] * 3
        + [shape(d, bf16) for d in bands]
        + [shape((8, 3 * width), f32)],
        [out] * 3 + [VM] * 5,
        (count, pairs),
        [
            pltpu.VMEM((rows, 3 * width), bf16),
            pltpu.VMEM((D, rows), bf16),
            pltpu.SemaphoreType.DMA((8,)),
        ],
        rows * LEN * PAIR * pairs * 9 + rows * D * 3 * width,
        28,
    )


def grad_first(order, dqkv, tokens, gmid, vec, pieces):
    count = len(pieces)
    rows = tokens.shape[0]
    flat = [t for chunk in dqkv for t in chunk]
    starts = [0]
    for chunk in dqkv:
        starts.append(starts[-1] + chunk[0].shape[1])

    def body(meta, tok, gmid, vec, *rest):
        grads, rest = rest[: len(flat)], rest[len(flat) :]
        pieces, (out, sums, w, sems) = rest[:count], rest[count:]
        first_step(fill(meta, pieces, w, sems))

        @pl.when(pl.program_id(0) == 0)
        def _():
            sums[...] = jnp.zeros_like(sums)

        total = None
        for i, ref in enumerate(grads):
            at = (i % 3) * D + starts[i // 3]
            term = dot(ref[...], w[:, at : at + ref.shape[1]], NT)
            total = term if total is None else total + term
        hat, rate = standard(tok[...].astype(f32))
        sums[0:1] += column_sum(total * hat)
        sums[1:2] += column_sum(total)
        out[...] = (gmid[...] + normal_grad(total, vec[0:1], hat, rate)).astype(bf16)

    blk = rows_block((TILE, D))
    return order.run(
        "grad_first",
        body,
        [tokens, gmid, vec, *flat, *pieces],
        [blk, blk, whole((8, D))] + [rows_block((TILE, t.shape[1])) for t in flat] + [ANY] * count,
        [shape((rows, D), bf16), shape((8, D), f32)],
        [blk, VM],
        (rows // TILE,),
        [pltpu.VMEM((D, 3 * D), bf16), pltpu.SemaphoreType.DMA((count,))],
        rows * D * D * 3,
        24,
    )


def down_grad(order, hidden, gb, send):
    rows = gb.shape[0]
    band = FF // 8
    first = 5 if send else 9

    def body(meta, hid, gb, *outs):
        low = dot(hid[...], gb[...], TN).astype(bf16)
        if send:
            outs[0][pl.program_id(0)] = low
            return
        at = pl.program_id(0)
        for j, out in enumerate((outs[0], outs[1], outs[2].at[0], outs[2].at[1])):

            @pl.when(at == j)
            def _(out=out):
                out[...] = low

    dims = [(4, band, D)] if send else [(band, D), (band, D), (2, band, D)]
    return order.run(
        "down_grad",
        body,
        [hidden, gb],
        [pl.BlockSpec((rows, band), lambda j, m: (0, m[first + j])), VM],
        [shape(d, bf16) for d in dims],
        [VM] * len(dims),
        (4,),
        [],
        rows * D * FF // 2,
        24,
    )


def second_grad(order, up_left, up_right, out_left, out_right, send):
    rows = up_right.shape[0]
    blocks = FF // D + 1
    first = 5 if send else 9

    def body(meta, up_left, out_left, up_right, out_right, *outs):
        mine = pl.ds(pl.multiple_of(pl.program_id(0) * BAND, BAND), BAND)

        def emit(left, right):
            bands = [
                left[pl.ds(pl.multiple_of(meta[first + j] * BAND, BAND), BAND)] for j in range(4)
            ]
            low = dot(jnp.concatenate(bands, 0), right[...]).astype(bf16)
            for j in range(4):
                band = low[j * BAND : (j + 1) * BAND]
                if send:
                    outs[0][j, mine] = band
                elif j < 2:
                    outs[j][mine] = band
                else:
                    outs[2][j - 2, mine] = band

        last = pl.program_id(0) == blocks - 1

        @pl.when(jnp.logical_not(last))
        def _():
            at = pl.multiple_of(pl.program_id(0) * D, D)
            emit(up_left, up_right.at[:, pl.ds(at, D)])

        @pl.when(last)
        def _():
            emit(out_left, out_right)

    flat = (blocks * BAND, D)
    dims = [(4, *flat)] if send else [flat, flat, (2, *flat)]
    return order.run(
        "second_grad",
        body,
        [up_left, out_left, up_right, out_right],
        [
            VM,
            whole((D, rows)),
            VM,
            VM,
        ],
        [shape(d, bf16) for d in dims],
        [VM] * len(dims),
        (blocks,),
        [],
        rows * D * blocks * D // 2,
        28,
    )


def collect(order, first_sums, chunk_sums, mid_sums, down_sum, up_sum):
    def body(meta, first, *refs):
        chunks, (mid, down, up, out) = refs[:-4], refs[-4:]
        out[...] = jnp.zeros_like(out)
        out[0:2] = first[0:2]
        at = 0
        for ref in chunks:
            w = ref.shape[1] // 3
            out[2:3, at : at + w] = ref[0:1, :w]
            out[3:4, at : at + w] = ref[0:1, 2 * w :]
            at += w
        out[4:5] = mid[2:3]
        out[5:7] = mid[0:2]
        out[7:8] = down[0:1]
        for i in range(FF // D):
            out[8 + i : 9 + i] = up[0:1, i * D : (i + 1) * D]

    ins = [first_sums, *chunk_sums, mid_sums, down_sum, up_sum]
    return order.small("collect", body, ins, [shape((16, D), f32)])[0]


class Links:
    def __init__(self, mesh):
        self.wide, self.narrow = mesh.shape["wide"], mesh.shape["narrow"]
        self.paired = self.wide == 8 and self.narrow == 4

    def move(self, value, target):
        pairs = []
        for w in range(self.wide):
            for n in range(self.narrow):
                to = target(w, n)
                if to is not None:
                    pairs.append((w * self.narrow + n, to[0] * self.narrow + to[1]))
        return lax.ppermute(value, ("wide", "narrow"), pairs)

    def swap(self, value):
        return self.move(value, lambda w, n: (w ^ 1, n))

    def near(self, value):
        return self.move(value, lambda w, n: (w, n ^ (1 + (w & 1))))

    def far(self, value):
        return self.move(value, lambda w, n: (w, n ^ (2 - (w & 1))))

    def along(self, value, step):
        return self.move(value, lambda w, n: (w, n ^ step))

    def level(self, value, step):
        return self.move(value, lambda w, n: (w ^ (2 * step), n))

    def meta(self):
        table = []
        for w in range(self.wide):
            for n in range(self.narrow):
                core, level = w & 1, w >> 1
                a, b, d = n ^ (1 + core), n ^ (2 - core), n ^ 3
                if not self.paired:
                    row = [0] * 5 + list(range(8)) + [0, 0] + list(range(self.narrow))
                    row += [0] * (24 - len(row))
                else:
                    row = [2 * n, 2 * a, 2 * d + core, 2 * b, 2 * d + 1 - core]
                    row += [2 * s + 1 - core for s in (n, a, b, d)]
                    row += [2 * s + core for s in (n, b, a, d)]
                    row += [core, int(level in (1, 2)), n, n ^ 1, n ^ 2, d]
                    row += [2 * d] + [level ^ j for j in range(4)]
                table.append(row)
        place = lax.axis_index(("wide", "narrow"))
        return lax.dynamic_index_in_dim(jnp.array(table, jnp.int32), place, keepdims=False)

    def shares(self, packed):
        if not self.paired:
            sources = lax.all_gather(packed, "narrow", axis=0)
            return [sources[i] for i in range(self.narrow)]
        return [packed] + [self.along(packed, i) for i in (1, 2, 3)]

    def inward(self, value):
        return self.move(value, lambda w, n: {0: (w + 2, n), 3: (w - 2, n)}.get(w >> 1))

    def across(self, value):
        return self.move(value, lambda w, n: {1: (w + 2, n), 2: (w - 2, n)}.get(w >> 1))

    def outward(self, value):
        return self.move(value, lambda w, n: {1: (w - 2, n), 2: (w + 2, n)}.get(w >> 1))

    def levels(self, bands):
        return [self.level(bands[j], j) for j in (1, 2, 3)]

    def whole_sum(self, sent, own, near, far):
        rest = own.shape[0]
        band = rest if rest == FF // 8 else BAND
        full = jnp.concatenate([sent, own[None], near[None], far], 0)
        full = full.reshape(8, rest // band, band, D)
        mine = lax.psum_scatter(full, "narrow", scatter_dimension=0, tiled=True)
        mine = lax.psum(mine, "wide").transpose(1, 0, 2, 3).reshape(rest // band, -1, D)
        half = mine.shape[1] // 2
        return mine[:, :half].reshape(-1, D), mine[:, half:].reshape(-1, D)


def finish_second(order, pair, half):
    blocks = FF // D
    plan = [(FF, [(0, i, 0, D) for i in range(blocks)]), (D, [(0, blocks, 0, D)])]
    return finish(order, half, [pair], plan)


def finish_down(order, pair):
    return finish(order, pair[0].shape[0], [pair], [(D, [(0, 0, 0, D)])])[0]


def split(got):
    return got[:3], got[3:]


def layer(links, *args):
    (
        tokens,
        segment_ids,
        out_grad,
        first_gain,
        first_shift,
        query_weight,
        query_bias,
        key_weight,
        value_weight,
        value_bias,
        output_weight,
        output_bias,
        second_gain,
        second_shift,
        up_weight,
        up_bias,
        down_weight,
        down_bias,
    ) = args
    order = Order(links.meta())
    paired = links.paired
    share = first_gain.shape[0]
    gather = lambda v: [lax.all_gather(v, "narrow", axis=0, tiled=True)]
    small = (
        first_gain,
        first_shift,
        query_bias,
        value_bias,
        output_bias,
        second_gain,
        second_shift,
        down_bias,
    )
    live = segment_ids.reshape(-1, 1, TILE)

    pack_one = pack(order, [query_weight, key_weight, value_weight])
    pack_two = pack(order, [up_weight, output_weight])
    shares = links.shares(jnp.concatenate([*small, up_bias]).reshape(-1, share))
    if paired:
        near_one = links.near(pack_one)
        far_one, got_one = links.far(near_one), links.swap(near_one)
        w_one = [pack_one, near_one, far_one, got_one]
        order.last.append(got_one)
    vec, up_b = vectors(order, shares)
    if not paired:
        w_one = gather(pack_one)
    if paired:
        order.last.append(far_one)
        pack_two = gate(order, pack_two)
    kept = attend(order, tokens, vec, segment_ids, w_one, 0, None)
    if paired:
        near_two = links.near(pack_two)
        half_two, down_copy = copies(order, [near_two], [down_weight])
        far_two = links.far(half_two)
        got_two, near_down = links.swap(near_two), links.near(down_copy)
    else:
        w_two = gather(pack_two)
    for s in range(1, tokens.shape[0] // LEN):
        kept = attend(order, tokens, vec, segment_ids, w_one, s, list(kept))
    fn_t, q, k, v, att, att_t, expo, inv = kept
    if paired:
        down_half, far_two = copies(order, [down_weight], [far_two])
        w_two = [pack_two, near_two, far_two, got_two, links.swap(far_two)]
        far_down = links.along(down_half, 3)
    else:
        w_down = gather(down_weight)
    mid, sn_t, hidden, slope, gb, down_sum = feed(
        order, att, tokens, out_grad, live, vec, up_b, w_two
    )

    if paired:
        near_down, far_down = copies(order, [], [near_down, far_down])
        w_down = [down_weight, near_down, far_down, links.swap(near_down), links.swap(far_down)]
    (d_send,) = down_grad(order, hidden, gb, True)
    d_own, d_near, d_far = down_grad(order, hidden, gb, False)
    if paired:
        d_got = links.swap(d_send)
    every, pair = ..., slice(2, 4)
    if paired:
        (d_far,) = sums_of(order, [[(d_far, every), (d_got, pair)]])
        d_got2 = links.near(d_far)
    gpre, gmid, gattn, gatt, mid_sums, up_sum = back(order, slope, mid, gb, vec, w_down, w_two)
    if paired:
        d_near, d_own = sums_of(
            order,
            [[(d_near, every), (d_got, 1), (d_got2, 1)]],
            [[(d_own, every), (d_got, 0), (d_got2, 0)]],
        )
        d_got = links.far(d_near)
    (s_send,) = second_grad(order, sn_t, gpre, att_t, gattn, True)
    s_own, s_near, s_far = second_grad(order, sn_t, gpre, att_t, gattn, False)
    if paired:
        s_got = links.swap(s_send)
        (s_far,) = sums_of(order, [[(s_far, every), (s_got, pair)]])
        s_got2 = links.near(s_far)
    c_three, (c_send, c_own, c_near, c_far, c_sums) = split(
        attend_back(order, fn_t, q, k, v, att_t, gatt, expo, inv, 0, CHUNKS[0])
    )
    if paired:
        c_got = links.swap(c_send)
        s_near, s_own, d_own = sums_of(
            order,
            [[(s_near, every), (s_got, 1), (s_got2, 1)]],
            [[(s_own, every), (s_got, 0), (s_got2, 0)]],
            [[(d_own, every), (d_got, every)]],
        )
        s_got = links.far(s_near)
        d_got = links.inward(d_own)
    e_three, (e_send, e_own, e_near, e_far, e_sums) = split(
        attend_back(order, fn_t, q, k, v, att_t, gatt, expo, inv, CHUNKS[0], CHUNKS[1])
    )
    if paired:
        e_got = links.swap(copies(order, [], [e_send])[0])
        s_own, d_own = sums_of(
            order, [[(s_own, every), (s_got, every)]], [[(d_own, every), (d_got, every)]]
        )
        s_got, d_got = links.inward(s_own), links.across(d_own)
        (g_far,) = sums_of(
            order, [[(c_far, every), (c_got, pair)], [(e_far, every), (e_got, pair)]]
        )
        g_got = links.near(g_far)
    input_grad, first_sums = grad_first(
        order, [c_three, e_three], tokens, gmid, vec, w_one
    )
    if paired:
        s_own, d_own = sums_of(
            order, [[(s_own, every), (s_got, every)]], [[(d_own, every), (d_got, every)]]
        )
        s_got, d_got = links.across(s_own), links.outward(d_own)
    total = collect(order, first_sums, [c_sums, e_sums], mid_sums, down_sum, up_sum)
    if paired:
        t_got = links.near(total)
        cut = c_own.shape[0]
        low, high = (slice(0, cut), slice(None)), (slice(cut, None), slice(None))
        g_near, g_own = sums_of(
            order,
            [
                [(c_near, every), (c_got, 1), (g_got, (1, *low))],
                [(e_near, every), (e_got, 1), (g_got, (1, *high))],
            ],
            [
                [(c_own, every), (c_got, 0), (g_got, (0, *low))],
                [(e_own, every), (e_got, 0), (g_got, (0, *high))],
            ],
        )
        g_got = links.far(g_near)
    layer_out = down_out(order, hidden, mid, vec, w_down)
    if paired:
        g_own, s_own, d_own, total = turn(
            order, g_own, g_got, s_own, s_got, d_own, d_got, total, t_got
        )
        t_got, s_got = links.far(total), links.outward(s_own)
        d_pair = (d_own, links.swap(d_own))
        g_bands = deal(order, [[g_own], [total, t_got]])
        g_gots = links.levels(g_bands)
        down_weight_grad = finish_down(order, d_pair)
        (g_mine,) = sums_of(order, [[(b, every) for b in [g_bands[0], *g_gots]]])
        g_gots = links.levels([g_mine] * 4)
        s_own = pick(order, s_own, s_got)
        s_pair = (s_own, links.swap(s_own))
        up_weight_grad, output_weight_grad = finish_second(order, s_pair, share // 2)
        g_own = undeal(order, [g_mine, *g_gots])
        g_pair = (g_own, links.swap(g_own))
    else:
        s_pair = links.whole_sum(s_send, s_own, s_near, s_far)
        d_pair = links.whole_sum(d_send, d_own, d_near, d_far)
        c_pair = links.whole_sum(c_send, c_own, c_near, c_far)
        e_pair = links.whole_sum(e_send, e_own, e_near, e_far)
        g_pair = [jnp.concatenate([c, e], 0) for c, e in zip(c_pair, e_pair)]
        total = lax.psum(total, ("wide", "narrow"))
        down_weight_grad = finish_down(order, d_pair)
        up_weight_grad, output_weight_grad = finish_second(order, s_pair, share // 2)
    half = share // 2
    plan = []
    for i in range(3):
        parts = []
        for c, pairs in enumerate(CHUNKS):
            at, stop = i * PAIR * pairs, (i + 1) * PAIR * pairs
            while at < stop:
                end = min(stop, (at // D + 1) * D)
                block = at // D + c * (3 * PAIR * CHUNKS[0] // D)
                parts.append((0, block, at % D, end - at))
                at = end
        plan.append((D, parts))
    place = slice(BAND * 3, BAND * 3 + 16) if paired else None
    first_grads = finish(order, half, [g_pair], plan, place)
    if paired:
        total = first_grads[3]

    n = lax.axis_index("narrow")
    mine = lax.dynamic_slice_in_dim(total[:8], n * share, share, 1)
    up_share = up_bias.shape[0]
    up_mine = lax.dynamic_slice_in_dim(total[8:12].reshape(FF), n * up_share, up_share)
    return (
        layer_out,
        input_grad,
        mine[0],
        mine[1],
        first_grads[0],
        mine[2],
        first_grads[1],
        first_grads[2],
        mine[3],
        output_weight_grad,
        mine[4],
        mine[5],
        mine[6],
        up_weight_grad,
        up_mine,
        down_weight_grad,
        mine[7],
    )


def solution(mesh):
    rows, vector, matrix = P(("wide", "narrow"), None), P("narrow"), P("narrow", None)
    in_specs = (rows, P(("wide", "narrow")), rows) + tuple(
        matrix if i in (2, 4, 5, 7, 11, 13) else vector for i in range(15)
    )
    out_specs = (rows, rows) + in_specs[3:]
    return jax.shard_map(
        functools.partial(layer, Links(mesh)),
        mesh=mesh,
        in_specs=in_specs,
        out_specs=out_specs,
        check_vma=False,
    )
```

```python
import functools

import jax
import jax.numpy as jnp
from jax import lax
from jax.experimental import pallas as pl
from jax.experimental.pallas import tpu as pltpu
from jax.sharding import PartitionSpec as P

D = 768
HEADS = 12
HEAD = 64
LEN = 512
FF = 3072
EPSILON = 1e-06
TILE = 256
BAND = D // 8
PAIR = 2 * HEAD
PAIRS = HEADS // 2
CHUNKS = (4, 2)
LOG2E = 1.4426950408889634
LN2 = 0.6931471805599453

bf16 = jnp.bfloat16
f32 = jnp.float32
NN = (((1,), (0,)), ((), ()))
NT = (((1,), (1,)), ((), ()))
TN = (((0,), (0,)), ((), ()))
ANY = pl.BlockSpec(memory_space=pl.ANY)
VM = pl.BlockSpec(memory_space=pltpu.VMEM)


def dot(left, right, dims=NN):
    return lax.dot_general(left, right, dims, preferred_element_type=f32)


def shape(dims, kind):
    return jax.ShapeDtypeStruct(dims, kind)


def column_sum(values):
    return jnp.sum(values, 0, keepdims=True)


def whole(dims):
    return pl.BlockSpec(dims, lambda *at: (0,) * len(dims))


def rows_block(dims):
    return pl.BlockSpec(dims, lambda at, *rest: (at,) + (0,) * (len(dims) - 1))


class Order:
    def __init__(self, meta):
        self.meta, self.last, self.far = meta, [], []

    def run(
        self,
        name,
        body,
        ins,
        in_specs,
        outs,
        out_specs,
        grid,
        scratch,
        macs,
        limit,
        alias={},
        near=False,
    ):
        moved = sum(a.size * a.dtype.itemsize for a in ins)
        moved += sum(o.size * o.dtype.itemsize for o in outs)
        used, extra = len(ins), len(self.last)

        def inner(meta, *refs):
            body(meta, *refs[:used], *refs[used + extra :])

        ins = [
            a if spec is ANY or spec is VM else pltpu.with_memory_space_constraint(a, pltpu.HBM)
            for a, spec in zip(ins, in_specs)
        ]
        if not near:
            outs = [
                (pltpu.VMEM if spec is VM else pltpu.HBM)(o.shape, o.dtype)
                for o, spec in zip(outs, out_specs)
            ]
        got = pl.pallas_call(
            inner,
            out_shape=outs,
            grid_spec=pltpu.PrefetchScalarGridSpec(
                num_scalar_prefetch=1,
                grid=grid,
                in_specs=[*in_specs] + [ANY] * extra,
                out_specs=out_specs,
                scratch_shapes=scratch,
            ),
            input_output_aliases=alias,
            compiler_params=pltpu.CompilerParams(vmem_limit_bytes=limit * 2**20),
            cost_estimate=pl.CostEstimate(flops=1, bytes_accessed=1 if near else 4 * 10**8, transcendentals=0),
            name=name,
        )(self.meta, *ins, *self.tokens())
        self.last = [got[0]]
        if not near:
            self.far += [g for g, spec in zip(got, out_specs) if spec is not VM]
        return got

    def tokens(self):
        return [
            pltpu.with_memory_space_constraint(t, pltpu.HBM)
            if any(t is a for a in self.far)
            else t
            for t in self.last
        ]

    def small(self, name, body, ins, outs, scratch=()):
        used, extra = len(ins), len(self.last)
        far = [any(a is b for b in self.far) for a in ins]
        held = [i for i in range(used) if far[i]]
        wait = len(held)

        def inner(meta, *refs):
            inputs, refs = list(refs[:used]), refs[used + extra :]
            outputs, refs = refs[: len(outs)], refs[len(outs) :]
            buffers, rest = refs[:wait], refs[wait:]
            moves = []
            for n, i in enumerate(held):
                moves.append(pltpu.make_async_copy(inputs[i], buffers[n], rest[0].at[n]))
                inputs[i] = buffers[n]
            for move in moves:
                move.start()
            for move in moves:
                move.wait()
            body(meta, *inputs, *outputs, *rest[1 if wait else 0 :])

        vmem = pl.BlockSpec(memory_space=pltpu.VMEM)
        got = pl.pallas_call(
            inner,
            out_shape=outs,
            in_specs=[pl.BlockSpec(memory_space=pltpu.SMEM)]
            + [ANY if f else vmem for f in far]
            + [ANY] * extra,
            out_specs=[vmem] * len(outs),
            scratch_shapes=[pltpu.VMEM(ins[i].shape, ins[i].dtype) for i in held]
            + ([pltpu.SemaphoreType.DMA((wait,))] if wait else [])
            + list(scratch),
            compiler_params=pltpu.CompilerParams(vmem_limit_bytes=20 * 2**20),
            cost_estimate=pl.CostEstimate(flops=1, bytes_accessed=1, transcendentals=0),
            name=name,
        )(
            self.meta,
            *[
                pltpu.with_memory_space_constraint(a, pltpu.HBM) if f else a
                for a, f in zip(ins, far)
            ],
            *self.tokens(),
        )
        self.last = [got[0]]
        return got


def fill(meta, pieces, target, sems, cols=None):
    count = 1 if len(pieces) == 1 else len(pieces)
    half = target.shape[0] // 8
    copies = []
    for i in range(count):
        place = meta[19] if count == 4 and i == 2 else meta[i]
        start = pl.multiple_of(place * half, half) if count > 1 else 0
        rows = pl.ds(start, pieces[i].shape[0])
        src, dst = pieces[i], target.at[rows]
        if cols is not None:
            src, dst = src.at[:, cols], target.at[rows, cols]
        copies.append(pltpu.make_async_copy(src, dst, sems.at[i]))
    return copies


def first_step(copies):
    @pl.when(pl.program_id(0) == 0)
    def _():
        for copy in copies:
            copy.start()
        for copy in copies:
            copy.wait()


def as_column(row):
    return jnp.broadcast_to(row.astype(f32), (8, row.shape[1])).T[:, :1]


def standard(v):
    center = v - jnp.mean(v, -1, keepdims=True)
    rate = lax.rsqrt(jnp.mean(center * center, -1, keepdims=True) + EPSILON)
    return center * rate, rate


def pack(order, parts):
    rows = parts[0].shape[0]
    width = sum(p.shape[1] for p in parts)
    count = len(parts)

    def body(meta, *refs):
        out, sems = refs[count:]
        moves, at = [], 0
        for i, src in enumerate(refs[:count]):
            cols = out.at[:, at : at + src.shape[1]]
            moves.append(pltpu.make_async_copy(src, cols, sems.at[i]))
            at += src.shape[1]
        for move in moves:
            move.start()
        for move in moves:
            move.wait()

    return order.run(
        "pack",
        body,
        [pltpu.with_memory_space_constraint(p, pltpu.HBM) for p in parts],
        [ANY] * count,
        [shape((rows, width), bf16)],
        [whole((rows, width))],
        (1,),
        [pltpu.SemaphoreType.DMA((count,))],
        0,
        16,
        near=True,
    )[0]


def gate(order, value):
    return order.run(
        "gate",
        lambda meta, *refs: None,
        [value],
        [ANY],
        [shape(value.shape, value.dtype)],
        [ANY],
        (1,),
        [],
        0,
        16,
        alias={1: 0},
        near=True,
    )[0]


def copies(order, halves, wholes=()):
    ins = [*halves, *wholes]
    dims = [(a.shape[0] // 2, a.shape[1]) for a in halves] + [a.shape for a in wholes]

    def body(meta, *refs):
        for i, (src, dst) in enumerate(zip(refs[: len(ins)], refs[len(ins) :])):
            if i < len(halves):
                half = dst.shape[0]
                dst[...] = src[pl.ds(pl.multiple_of(meta[13] * half, half), half)]
            else:
                dst[...] = src[...]

    return order.small("copies", body, ins, [shape(d, bf16) for d in dims])


def sums_of(order, *plan):
    ins = []
    for parts in plan:
        for array, _ in sum(parts, []):
            if not any(array is other for other in ins):
                ins.append(array)
    where = lambda array: [i for i, other in enumerate(ins) if other is array][0]
    places = [[[(where(a), index) for a, index in terms] for terms in parts] for parts in plan]

    def body(meta, *refs):
        for parts, out in zip(places, refs[len(ins) :]):
            at = 0
            for terms in parts:
                total = None
                for i, index in terms:
                    term = refs[i][index].astype(f32)
                    total = term if total is None else total + term
                rows = slice(at, at + total.shape[-2])
                out[..., rows, :] = total.astype(bf16)
                at += total.shape[-2]

    outs = []
    for parts in plan:
        dims = [
            jax.eval_shape(lambda a, i=terms[0][1]: a[i], terms[0][0]).shape for terms in parts
        ]
        rows = sum(d[-2] for d in dims)
        outs.append(shape((*dims[0][:-2], rows, dims[0][-1]), bf16))
    return order.small("sums_of", body, ins, outs)


def pick(order, own, got):
    def body(meta, own, got, out):
        inner = jnp.full(out.shape, meta[14], jnp.int32) == 1
        out[...] = jnp.where(inner, own[...], got[...])

    return order.small("pick", body, [own, got], [shape(own.shape, bf16)])[0]


def deal(order, parts):
    flat = [a for arrays in parts for a in arrays]
    size = -(-sum(arrays[0].shape[0] for arrays in parts) // 64) * 16

    def body(meta, *refs):
        ins, outs, held = refs[: len(flat)], refs[len(flat) : -1], refs[-1]
        held[...] = jnp.zeros_like(held)
        i, at = 0, 0
        for arrays in parts:
            total = None
            for ref in ins[i : i + len(arrays)]:
                term = ref[...].astype(f32)
                total = term if total is None else total + term
            i += len(arrays)
            held[at : at + total.shape[0]] = total.astype(bf16)
            at += total.shape[0]
        for j in range(4):
            outs[j][...] = held[pl.ds(pl.multiple_of(meta[20 + j] * size, size), size)]

    outs = [shape((size, D), bf16)] * 4
    return order.small("deal", body, flat, outs, [pltpu.VMEM((4 * size, D), bf16)])


def undeal(order, bands):
    size = bands[0].shape[0]

    def body(meta, *refs):
        for j in range(4):
            rows = pl.ds(pl.multiple_of(meta[20 + j] * size, size), size)
            refs[4][rows] = refs[j][...]

    return order.small("undeal", body, bands, [shape((4 * size, D), bf16)])[0]


def turn(order, *pairs):
    def body(meta, *refs):
        ins, outs = refs[:8], refs[8:]
        for i, out in enumerate(outs):
            own, got = ins[2 * i], ins[2 * i + 1]
            if i == 2:
                inner = jnp.full(out.shape, meta[14], jnp.int32) == 1
                out[...] = jnp.where(inner, own[...], got[...])
            else:
                out[...] = (own[...].astype(f32) + got[...].astype(f32)).astype(out.dtype)

    outs = [shape(a.shape, a.dtype) for a in pairs[::2]]
    return order.small("turn", body, list(pairs), outs)


def finish(order, half, pairs, plan, last=None):
    flat = [a for pair in pairs for a in pair]

    def body(meta, *refs):
        core = meta[13]
        for (width, parts), out in zip(plan, refs[len(flat) :]):
            at = 0
            for which, block, first, cols in parts:
                for i in range(2):
                    place = core if i == 0 else 1 - core
                    rows = pl.ds(pl.multiple_of(place * half, half), half)
                    value = refs[2 * which + i][
                        block * half : (block + 1) * half, first : first + cols
                    ]
                    out[rows, at : at + cols] = value.astype(f32)
                at += cols
        if last:
            own, other = [ref[last].astype(f32) for ref in refs[:2]]
            total = own + other
            mine = jnp.zeros(refs[-2].shape, f32)
            up = jnp.zeros(refs[-1].shape, f32)
            share = mine.shape[1]
            for i in range(D // share):
                mine = jnp.where(meta[15] == i, total[:8, i * share : (i + 1) * share], mine)
                up = jnp.where(meta[15] == i, total[8 + i : 9 + i], up)
            refs[-2][...], refs[-1][...] = mine, up

    outs = [shape((2 * half, width), f32) for width, _ in plan]
    if last:
        outs += [shape((8, 2 * half), f32), shape((1, D), f32)]
    return order.run(
        "finish",
        body,
        flat,
        [VM] * len(flat),
        outs,
        [whole(o.shape) for o in outs],
        (1,),
        [],
        0,
        24,
    )


def attend(order, tokens, vec, segs, pieces, at_seq, before):
    count = len(pieces)
    rows = tokens.shape[0]
    seqs = rows // LEN
    held = 0 if before is None else len(before)

    def body(meta, tok, vec, seg, *rest):
        pieces, rest = rest[:count], rest[count + held :]
        fn_t, q, k, v, att, att_t, expo, inv, bias, w, sems = rest
        p = pl.program_id(0)

        @pl.when(p == 0)
        def _():
            copies = fill(meta, pieces, w, sems)
            for copy in copies:
                copy.start()
            row = seg[0].astype(f32)
            bias[...] = jnp.where(as_column(row) == row, 0.0, -1e30)
            normed = standard(tok[...].astype(f32))[0] * vec[0:1] + vec[1:2]
            low = normed.astype(bf16)
            fn_t[...] = low.T
            for copy in copies:
                copy.wait()
            q[...] = ((dot(low, w[:, :D]) + vec[2:3]) * (LOG2E * HEAD**-0.5)).astype(bf16)
            k[...] = dot(low, w[:, D : 2 * D]).astype(bf16)
            v[...] = (dot(low, w[:, 2 * D :]) + vec[3:4]).astype(bf16)

        lane = lax.broadcasted_iota(jnp.int32, (LEN, PAIR), 1)
        mine_cols = pl.ds(pl.multiple_of(p * PAIR, PAIR), PAIR)
        vt = v[:, mine_cols].T
        keys = k[:, mine_cols]
        queries = q[:, mine_cols]
        parts = []
        for h in range(2):
            mine = (lane < HEAD) if h == 0 else (lane >= HEAD)
            scores = dot(jnp.where(mine, keys, 0).astype(bf16), queries, NT) + bias[...]
            e = jnp.exp2(scores - jnp.max(scores, 0, keepdims=True))
            rate = 1.0 / jnp.sum(e, 0, keepdims=True)
            low = e.astype(bf16)
            expo[h] = low
            inv[0, h : h + 1] = rate
            parts.append(dot(vt[HEAD * h : HEAD * h + HEAD], low) * rate)
        both = jnp.concatenate(parts, 0)
        att_t[...] = both.astype(bf16)
        att[...] = both.T.astype(bf16)

    seq = pl.BlockSpec((LEN, D), lambda p, m: (at_seq, 0))
    ins = [tokens, vec, segs.reshape(seqs, 1, LEN), *pieces]
    alias = {}
    if before is not None:
        alias = {1 + len(ins) + i: i for i in range(held)}
        ins += before
    return order.run(
        "attend",
        body,
        ins,
        [
            seq,
            whole((8, D)),
            pl.BlockSpec((1, 1, LEN), lambda p, m: (at_seq, 0, 0)),
        ]
        + [ANY] * (count + held),
        [
            shape((D, rows), bf16),
            shape((rows, D), bf16),
            shape((rows, D), bf16),
            shape((rows, D), bf16),
            shape((rows, D), bf16),
            shape((D, rows), bf16),
            shape((seqs * HEADS, LEN, LEN), bf16),
            shape((seqs * PAIRS, 8, LEN), f32),
        ],
        [
            pl.BlockSpec((D, LEN), lambda p, m: (0, at_seq)),
            seq,
            seq,
            seq,
            pl.BlockSpec((LEN, PAIR), lambda p, m: (at_seq, p)),
            pl.BlockSpec((PAIR, LEN), lambda p, m: (p, at_seq)),
            pl.BlockSpec((2, LEN, LEN), lambda p, m: (at_seq * PAIRS + p, 0, 0)),
            pl.BlockSpec((1, 8, LEN), lambda p, m: (at_seq * PAIRS + p, 0, 0)),
        ],
        (PAIRS,),
        [
            pltpu.VMEM((LEN, LEN), f32),
            pltpu.VMEM((D, 3 * D), bf16),
            pltpu.SemaphoreType.DMA((count,)),
        ],
        LEN * D * D * 3 + LEN * LEN * D * 8,
        28,
        alias,
    )


def vectors(order, sources):
    n, share = len(sources), sources[0].shape[1]

    def body(meta, *refs):
        srcs, (vec, ub) = refs[:n], refs[n:]
        rows = []
        for s in range(n):
            total = jnp.zeros((12, share), f32)
            for i in range(n):
                total = jnp.where(meta[15 + i] == s, srcs[i][...].astype(f32), total)
            rows.append(total)
        vec[...] = jnp.concatenate([r[:8] for r in rows], 1)
        ub[...] = jnp.concatenate([r[8 + i : 9 + i] for r in rows for i in range(4)], 1)

    outs = [shape((8, D), f32), shape((1, FF), f32)]
    return order.small("vectors", body, sources, outs)


def gelu_both(x):
    size = jnp.abs(x) * 0.7071067811865476
    t = 1.0 / (1.0 + 0.3275911 * size)
    bell = jnp.exp2(x * x * (-0.5 * LOG2E))
    poly = 0.5 * 1.061405429
    for c in (-1.453152027, 1.421413741, -0.284496736, 0.254829592):
        poly = poly * t + 0.5 * c
    tail = poly * t * bell
    cdf = jnp.where(x >= 0, 1.0 - tail, tail)
    return x * cdf, cdf + x * bell * 0.3989422804014327


def feed(order, attended, tokens, out_grad, live, vec, up_bias, pieces):
    count = len(pieces)
    rows = tokens.shape[0]

    def body(meta, att, tok, og, seg, vec, ub, *rest):
        pieces, rest = rest[:count], rest[count:]
        mid, sn_t, hid, slope, gb, down_sum, w, sems, sems_up = rest
        first = fill(meta, pieces, w, sems, slice(FF, FF + D))
        others = fill(meta, pieces, w, sems_up, slice(0, FF))
        begin = pl.program_id(0) == 0
        mine = pl.ds(pl.multiple_of(pl.program_id(0) * TILE, TILE), TILE)

        @pl.when(begin)
        def _():
            for copy in [*first, *others]:
                copy.start()
            for copy in first:
                copy.wait()

        m = tok[...].astype(f32) + dot(att[...], w[:, FF:]) + vec[4:5]
        mid[...] = m
        low = (standard(m)[0] * vec[5:6] + vec[6:7]).astype(bf16)
        sn_t[:, mine] = low.T
        grad = jnp.where(as_column(seg[0]) >= 0, og[...].astype(f32), 0.0)
        gb[mine] = grad.astype(bf16)

        @pl.when(pl.program_id(0) == 0)
        def _():
            down_sum[...] = jnp.zeros_like(down_sum)

        down_sum[0:1] += column_sum(grad)

        @pl.when(begin)
        def _():
            for copy in others:
                copy.wait()

        for at in range(0, FF, 512):
            pre = dot(low, w[:, at : at + 512]) + ub[:, at : at + 512]
            act, der = gelu_both(pre)
            hid[:, at : at + 512] = act.astype(bf16)
            slope[:, at : at + 512] = der.astype(bf16)

    blk = rows_block((TILE, D))
    wide = rows_block((TILE, FF))
    return order.run(
        "feed",
        body,
        [attended, tokens, out_grad, live, vec, up_bias, *pieces],
        [blk, blk, blk, rows_block((1, 1, TILE)), whole((8, D)), whole((1, FF))] + [ANY] * count,
        [
            shape((rows, D), f32),
            shape((D, rows), bf16),
            shape((rows, FF), bf16),
            shape((rows, FF), bf16),
            shape((rows, D), bf16),
            shape((8, D), f32),
        ],
        [blk, VM, wide, wide, VM, VM],
        (rows // TILE,),
        [pltpu.VMEM((D, FF + D), bf16)] + [pltpu.SemaphoreType.DMA((count,))] * 2,
        rows * D * (FF + D) * 3,
        32,
    )


def down_out(order, hidden, mid, vec, pieces):
    count = len(pieces)
    rows = hidden.shape[0]

    def body(meta, hid, mid, vec, *rest):
        pieces, (out, w, sems) = rest[:count], rest[count:]
        first_step(fill(meta, pieces, w, sems))
        out[...] = (mid[...] + dot(hid[...], w[...]) + vec[7:8]).astype(bf16)

    blk = rows_block((TILE, D))
    return order.run(
        "down_out",
        body,
        [hidden, mid, vec, *pieces],
        [rows_block((TILE, FF)), blk, whole((8, D))] + [ANY] * count,
        [shape((rows, D), bf16)],
        [blk],
        (rows // TILE,),
        [pltpu.VMEM((FF, D), bf16), pltpu.SemaphoreType.DMA((count,))],
        rows * D * FF,
        24,
    )[0]


def normal_grad(grad, gain, hat, rate):
    inner = grad * gain
    return rate * (
        inner
        - jnp.mean(inner, -1, keepdims=True)
        - hat * jnp.mean(inner * hat, -1, keepdims=True)
    )


def back(order, slope, mid, gb, vec, downs, pieces):
    nd, count = len(downs), len(pieces)
    rows = gb.shape[0]

    def body(meta, slope, mid, gb, vec, *rest):
        downs, pieces, rest = rest[:nd], rest[nd : nd + count], rest[nd + count :]
        gpre, gmid, gattn, gatt, sums, up_sum, wd, w, sems_d, sems = rest
        first, others = fill(meta, downs, wd, sems_d), fill(meta, pieces, w, sems)
        begin = pl.program_id(0) == 0
        mine = pl.ds(pl.multiple_of(pl.program_id(0) * TILE, TILE), TILE)

        @pl.when(begin)
        def _():
            for copy in [*first, *others]:
                copy.start()
            sums[...] = jnp.zeros_like(sums)
            up_sum[...] = jnp.zeros_like(up_sum)
            for copy in first:
                copy.wait()

        for at in range(0, FF, 512):
            cols = slice(at, at + 512)
            low = (dot(gb[mine], wd[cols], NT) * slope[:, cols].astype(f32)).astype(bf16)
            gpre[mine, cols] = low
            up_sum[0:1, cols] += column_sum(low.astype(f32))

        @pl.when(begin)
        def _():
            for copy in others:
                copy.wait()

        grad = dot(gpre[mine], w[:, :FF], NT)
        hat, rate = standard(mid[...])
        sums[0:1] += column_sum(grad * hat)
        sums[1:2] += column_sum(grad)
        g = gb[mine].astype(f32) + normal_grad(grad, vec[5:6], hat, rate)
        gmid[...] = g
        low = g.astype(bf16)
        gattn[mine] = low
        sums[2:3] += column_sum(low.astype(f32))
        gatt[...] = dot(low, w[:, FF:], NT).astype(bf16)

    blk = rows_block((TILE, D))
    wide = rows_block((TILE, FF))
    return order.run(
        "back",
        body,
        [slope, mid, gb, vec, *downs, *pieces],
        [wide, blk, VM, whole((8, D))] + [ANY] * (nd + count),
        [
            shape((rows, FF), bf16),
            shape((rows, D), f32),
            shape((rows, D), bf16),
            shape((rows, D), bf16),
            shape((8, D), f32),
            shape((8, FF), f32),
        ],
        [VM, blk, VM, blk, VM, VM],
        (rows // TILE,),
        [
            pltpu.VMEM((FF, D), bf16),
            pltpu.VMEM((D, FF + D), bf16),
            pltpu.SemaphoreType.DMA((nd,)),
            pltpu.SemaphoreType.DMA((count,)),
        ],
        rows * D * (2 * FF + D),
        28,
    )


def attend_back(order, fn_t, q, k, v, att_t, gatt, expo, inv, first, pairs):
    rows = q.shape[0]
    count = rows // LEN
    width = PAIR * pairs

    def body(meta, q, k, v, att_t, g, expo, inv, fn_t, *rest):
        dq, dk, dv, send, own, near, far, sums, grads, held, sems = rest
        s, p = pl.program_id(0), pl.program_id(1)

        def moves():
            return [
                pltpu.make_async_copy(
                    fn_t.at[pl.ds(pl.multiple_of(meta[5 + j] * BAND, BAND), BAND)],
                    held.at[pl.ds(j * BAND, BAND)],
                    sems.at[j],
                )
                for j in range(8)
            ]

        @pl.when((s == 0) & (p == 0))
        def _():
            for copy in moves():
                copy.start()

        queries, values = q[...], v[...]
        kt = k[...].T
        gt = g[...].astype(f32).T
        both = att_t[...].astype(f32) * gt
        parts, dks, dvs = [], [], []
        for h in range(2):
            at = slice(HEAD * h, HEAD * h + HEAD)
            rate = inv[0, h : h + 1]
            delta = jnp.sum(both[at], 0, keepdims=True) * rate
            scaled = (gt[at] * rate).astype(bf16)
            e = expo[h]
            ds = (e.astype(f32) * (dot(values[:, at], scaled) - delta)).astype(bf16)
            parts.append(dot(kt[at], ds))
            dvs.append(dot(e, scaled, NT))
            dks.append(dot(ds, queries[:, at]) * LN2)
        three = (
            (jnp.concatenate(parts, 0).T * HEAD**-0.5).astype(bf16),
            jnp.concatenate(dks, 1).astype(bf16),
            jnp.concatenate(dvs, 1).astype(bf16),
        )
        mine = pl.ds(pl.multiple_of(s * LEN, LEN), LEN)
        for i, (ref, value) in enumerate(zip((dq, dk, dv), three)):
            ref[...] = value
            grads[mine, pl.ds(pl.multiple_of(i * width + p * PAIR, PAIR), PAIR)] = value

        @pl.when((s == count - 1) & (p == pairs - 1))
        def _():
            for copy in moves():
                copy.wait()
            for i in range(blocks):
                right = grads[:, i * D : (i + 1) * D]
                rows_of = slice(i * BAND, (i + 1) * BAND)
                low = dot(held[...], right).astype(bf16)
                for j in range(4):
                    send[j, rows_of] = low[j * BAND : (j + 1) * BAND]
                own[rows_of] = low[4 * BAND : 5 * BAND]
                near[rows_of] = low[5 * BAND : 6 * BAND]
                for j in range(2):
                    far[j, rows_of] = low[(6 + j) * BAND : (7 + j) * BAND]
            right = grads[...]
            sums[...] = jnp.broadcast_to(column_sum(right.astype(f32)), sums.shape)

    blk = pl.BlockSpec((LEN, PAIR), lambda s, p, m: (s, p + first))
    out = pl.BlockSpec((LEN, PAIR), lambda s, p, m: (s, p))
    blocks = 3 * width // D
    bands = [(n, blocks * BAND, D) for n in (4, 2)]
    bands = [bands[0], bands[0][1:], bands[0][1:], bands[1]]
    return order.run(
        "attend_back",
        body,
        [q, k, v, att_t, gatt, expo, inv, fn_t],
        [blk] * 3
        + [
            pl.BlockSpec((PAIR, LEN), lambda s, p, m: (p + first, s)),
            blk,
            pl.BlockSpec((2, LEN, LEN), lambda s, p, m: (s * PAIRS + p + first, 0, 0)),
            pl.BlockSpec((1, 8, LEN), lambda s, p, m: (s * PAIRS + p + first, 0, 0)),
            ANY,
        ],
        [shape((rows, width), bf16)] * 3
        + [shape(d, bf16) for d in bands]
        + [shape((8, 3 * width), f32)],
        [out] * 3 + [VM] * 5,
        (count, pairs),
        [
            pltpu.VMEM((rows, 3 * width), bf16),
            pltpu.VMEM((D, rows), bf16),
            pltpu.SemaphoreType.DMA((8,)),
        ],
        rows * LEN * PAIR * pairs * 9 + rows * D * 3 * width,
        28,
    )


def grad_first(order, dqkv, tokens, gmid, vec, pieces):
    count = len(pieces)
    rows = tokens.shape[0]
    flat = [t for chunk in dqkv for t in chunk]
    starts = [0]
    for chunk in dqkv:
        starts.append(starts[-1] + chunk[0].shape[1])

    def body(meta, tok, gmid, vec, *rest):
        grads, rest = rest[: len(flat)], rest[len(flat) :]
        pieces, (out, sums, w, sems) = rest[:count], rest[count:]
        first_step(fill(meta, pieces, w, sems))

        @pl.when(pl.program_id(0) == 0)
        def _():
            sums[...] = jnp.zeros_like(sums)

        total = None
        for i, ref in enumerate(grads):
            at = (i % 3) * D + starts[i // 3]
            term = dot(ref[...], w[:, at : at + ref.shape[1]], NT)
            total = term if total is None else total + term
        hat, rate = standard(tok[...].astype(f32))
        sums[0:1] += column_sum(total * hat)
        sums[1:2] += column_sum(total)
        out[...] = (gmid[...] + normal_grad(total, vec[0:1], hat, rate)).astype(bf16)

    blk = rows_block((TILE, D))
    return order.run(
        "grad_first",
        body,
        [tokens, gmid, vec, *flat, *pieces],
        [blk, blk, whole((8, D))] + [rows_block((TILE, t.shape[1])) for t in flat] + [ANY] * count,
        [shape((rows, D), bf16), shape((8, D), f32)],
        [blk, VM],
        (rows // TILE,),
        [pltpu.VMEM((D, 3 * D), bf16), pltpu.SemaphoreType.DMA((count,))],
        rows * D * D * 3,
        24,
    )


def down_grad(order, hidden, gb, send):
    rows = gb.shape[0]
    band = FF // 8
    first = 5 if send else 9

    def body(meta, hid, gb, *outs):
        low = dot(hid[...], gb[...], TN).astype(bf16)
        if send:
            outs[0][pl.program_id(0)] = low
            return
        at = pl.program_id(0)
        for j, out in enumerate((outs[0], outs[1], outs[2].at[0], outs[2].at[1])):

            @pl.when(at == j)
            def _(out=out):
                out[...] = low

    dims = [(4, band, D)] if send else [(band, D), (band, D), (2, band, D)]
    return order.run(
        "down_grad",
        body,
        [hidden, gb],
        [pl.BlockSpec((rows, band), lambda j, m: (0, m[first + j])), VM],
        [shape(d, bf16) for d in dims],
        [VM] * len(dims),
        (4,),
        [],
        rows * D * FF // 2,
        24,
    )


def second_grad(order, up_left, up_right, out_left, out_right, send):
    rows = up_right.shape[0]
    blocks = FF // D + 1
    first = 5 if send else 9

    def body(meta, up_left, out_left, up_right, out_right, *outs):
        mine = pl.ds(pl.multiple_of(pl.program_id(0) * BAND, BAND), BAND)

        def emit(left, right):
            bands = [
                left[pl.ds(pl.multiple_of(meta[first + j] * BAND, BAND), BAND)] for j in range(4)
            ]
            low = dot(jnp.concatenate(bands, 0), right[...]).astype(bf16)
            for j in range(4):
                band = low[j * BAND : (j + 1) * BAND]
                if send:
                    outs[0][j, mine] = band
                elif j < 2:
                    outs[j][mine] = band
                else:
                    outs[2][j - 2, mine] = band

        last = pl.program_id(0) == blocks - 1

        @pl.when(jnp.logical_not(last))
        def _():
            at = pl.multiple_of(pl.program_id(0) * D, D)
            emit(up_left, up_right.at[:, pl.ds(at, D)])

        @pl.when(last)
        def _():
            emit(out_left, out_right)

    flat = (blocks * BAND, D)
    dims = [(4, *flat)] if send else [flat, flat, (2, *flat)]
    return order.run(
        "second_grad",
        body,
        [up_left, out_left, up_right, out_right],
        [
            VM,
            whole((D, rows)),
            VM,
            VM,
        ],
        [shape(d, bf16) for d in dims],
        [VM] * len(dims),
        (blocks,),
        [],
        rows * D * blocks * D // 2,
        28,
    )


def collect(order, first_sums, chunk_sums, mid_sums, down_sum, up_sum):
    def body(meta, first, *refs):
        chunks, (mid, down, up, out) = refs[:-4], refs[-4:]
        out[...] = jnp.zeros_like(out)
        out[0:2] = first[0:2]
        at = 0
        for ref in chunks:
            w = ref.shape[1] // 3
            out[2:3, at : at + w] = ref[0:1, :w]
            out[3:4, at : at + w] = ref[0:1, 2 * w :]
            at += w
        out[4:5] = mid[2:3]
        out[5:7] = mid[0:2]
        out[7:8] = down[0:1]
        for i in range(FF // D):
            out[8 + i : 9 + i] = up[0:1, i * D : (i + 1) * D]

    ins = [first_sums, *chunk_sums, mid_sums, down_sum, up_sum]
    return order.small("collect", body, ins, [shape((16, D), f32)])[0]


class Links:
    def __init__(self, mesh):
        self.wide, self.narrow = mesh.shape["wide"], mesh.shape["narrow"]
        self.paired = self.wide == 8 and self.narrow == 4

    def move(self, value, target):
        pairs = []
        for w in range(self.wide):
            for n in range(self.narrow):
                to = target(w, n)
                if to is not None:
                    pairs.append((w * self.narrow + n, to[0] * self.narrow + to[1]))
        return lax.ppermute(value, ("wide", "narrow"), pairs)

    def swap(self, value):
        return self.move(value, lambda w, n: (w ^ 1, n))

    def near(self, value):
        return self.move(value, lambda w, n: (w, n ^ (1 + (w & 1))))

    def far(self, value):
        return self.move(value, lambda w, n: (w, n ^ (2 - (w & 1))))

    def along(self, value, step):
        return self.move(value, lambda w, n: (w, n ^ step))

    def level(self, value, step):
        return self.move(value, lambda w, n: (w ^ (2 * step), n))

    def meta(self):
        table = []
        for w in range(self.wide):
            for n in range(self.narrow):
                core, level = w & 1, w >> 1
                a, b, d = n ^ (1 + core), n ^ (2 - core), n ^ 3
                if not self.paired:
                    row = [0] * 5 + list(range(8)) + [0, 0] + list(range(self.narrow))
                    row += [0] * (24 - len(row))
                else:
                    row = [2 * n, 2 * a, 2 * d + core, 2 * b, 2 * d + 1 - core]
                    row += [2 * s + 1 - core for s in (n, a, b, d)]
                    row += [2 * s + core for s in (n, b, a, d)]
                    row += [core, int(level in (1, 2)), n, n ^ 1, n ^ 2, d]
                    row += [2 * d] + [level ^ j for j in range(4)]
                table.append(row)
        place = lax.axis_index(("wide", "narrow"))
        return lax.dynamic_index_in_dim(jnp.array(table, jnp.int32), place, keepdims=False)

    def shares(self, packed):
        if not self.paired:
            sources = lax.all_gather(packed, "narrow", axis=0)
            return [sources[i] for i in range(self.narrow)]
        return [packed] + [self.along(packed, i) for i in (1, 2, 3)]

    def inward(self, value):
        return self.move(value, lambda w, n: {0: (w + 2, n), 3: (w - 2, n)}.get(w >> 1))

    def across(self, value):
        return self.move(value, lambda w, n: {1: (w + 2, n), 2: (w - 2, n)}.get(w >> 1))

    def outward(self, value):
        return self.move(value, lambda w, n: {1: (w - 2, n), 2: (w + 2, n)}.get(w >> 1))

    def levels(self, bands):
        return [self.level(bands[j], j) for j in (1, 2, 3)]

    def whole_sum(self, sent, own, near, far):
        rest = own.shape[0]
        band = rest if rest == FF // 8 else BAND
        full = jnp.concatenate([sent, own[None], near[None], far], 0)
        full = full.reshape(8, rest // band, band, D)
        mine = lax.psum_scatter(full, "narrow", scatter_dimension=0, tiled=True)
        mine = lax.psum(mine, "wide").transpose(1, 0, 2, 3).reshape(rest // band, -1, D)
        half = mine.shape[1] // 2
        return mine[:, :half].reshape(-1, D), mine[:, half:].reshape(-1, D)


def finish_second(order, pair, half):
    blocks = FF // D
    plan = [(FF, [(0, i, 0, D) for i in range(blocks)]), (D, [(0, blocks, 0, D)])]
    return finish(order, half, [pair], plan)


def finish_down(order, pair):
    return finish(order, pair[0].shape[0], [pair], [(D, [(0, 0, 0, D)])])[0]


def split(got):
    return got[:3], got[3:]


def layer(links, *args):
    (
        tokens,
        segment_ids,
        out_grad,
        first_gain,
        first_shift,
        query_weight,
        query_bias,
        key_weight,
        value_weight,
        value_bias,
        output_weight,
        output_bias,
        second_gain,
        second_shift,
        up_weight,
        up_bias,
        down_weight,
        down_bias,
    ) = args
    order = Order(links.meta())
    paired = links.paired
    share = first_gain.shape[0]
    gather = lambda v: [lax.all_gather(v, "narrow", axis=0, tiled=True)]
    small = (
        first_gain,
        first_shift,
        query_bias,
        value_bias,
        output_bias,
        second_gain,
        second_shift,
        down_bias,
    )
    live = segment_ids.reshape(-1, 1, TILE)

    pack_one = pack(order, [query_weight, key_weight, value_weight])
    pack_two = pack(order, [up_weight, output_weight])
    shares = links.shares(jnp.concatenate([*small, up_bias]).reshape(-1, share))
    if paired:
        near_one = links.near(pack_one)
        far_one, got_one = links.far(near_one), links.swap(near_one)
        w_one = [pack_one, near_one, far_one, got_one]
        order.last.append(got_one)
    vec, up_b = vectors(order, shares)
    if not paired:
        w_one = gather(pack_one)
    if paired:
        order.last.append(far_one)
        pack_two = gate(order, pack_two)
    kept = attend(order, tokens, vec, segment_ids, w_one, 0, None)
    if paired:
        near_two = links.near(pack_two)
        half_two, down_copy = copies(order, [near_two], [down_weight])
        far_two = links.far(half_two)
        got_two, near_down = links.swap(near_two), links.near(down_copy)
    else:
        w_two = gather(pack_two)
    for s in range(1, tokens.shape[0] // LEN):
        kept = attend(order, tokens, vec, segment_ids, w_one, s, list(kept))
    fn_t, q, k, v, att, att_t, expo, inv = kept
    if paired:
        down_half, far_two = copies(order, [down_weight], [far_two])
        w_two = [pack_two, near_two, far_two, got_two, links.swap(far_two)]
        far_down = links.along(down_half, 3)
    else:
        w_down = gather(down_weight)
    mid, sn_t, hidden, slope, gb, down_sum = feed(
        order, att, tokens, out_grad, live, vec, up_b, w_two
    )

    if paired:
        near_down, far_down = copies(order, [], [near_down, far_down])
        w_down = [down_weight, near_down, far_down, links.swap(near_down), links.swap(far_down)]
    (d_send,) = down_grad(order, hidden, gb, True)
    d_own, d_near, d_far = down_grad(order, hidden, gb, False)
    if paired:
        d_got = links.swap(d_send)
    every, pair = ..., slice(2, 4)
    if paired:
        (d_far,) = sums_of(order, [[(d_far, every), (d_got, pair)]])
        d_got2 = links.near(d_far)
    gpre, gmid, gattn, gatt, mid_sums, up_sum = back(order, slope, mid, gb, vec, w_down, w_two)
    if paired:
        d_near, d_own = sums_of(
            order,
            [[(d_near, every), (d_got, 1), (d_got2, 1)]],
            [[(d_own, every), (d_got, 0), (d_got2, 0)]],
        )
        d_got = links.far(d_near)
    (s_send,) = second_grad(order, sn_t, gpre, att_t, gattn, True)
    s_own, s_near, s_far = second_grad(order, sn_t, gpre, att_t, gattn, False)
    if paired:
        s_got = links.swap(s_send)
        (s_far,) = sums_of(order, [[(s_far, every), (s_got, pair)]])
        s_got2 = links.near(s_far)
    c_three, (c_send, c_own, c_near, c_far, c_sums) = split(
        attend_back(order, fn_t, q, k, v, att_t, gatt, expo, inv, 0, CHUNKS[0])
    )
    if paired:
        c_got = links.swap(c_send)
        s_near, s_own, d_own = sums_of(
            order,
            [[(s_near, every), (s_got, 1), (s_got2, 1)]],
            [[(s_own, every), (s_got, 0), (s_got2, 0)]],
            [[(d_own, every), (d_got, every)]],
        )
        s_got = links.far(s_near)
        d_got = links.inward(d_own)
    e_three, (e_send, e_own, e_near, e_far, e_sums) = split(
        attend_back(order, fn_t, q, k, v, att_t, gatt, expo, inv, CHUNKS[0], CHUNKS[1])
    )
    if paired:
        e_got = links.swap(copies(order, [], [e_send])[0])
        s_own, d_own = sums_of(
            order, [[(s_own, every), (s_got, every)]], [[(d_own, every), (d_got, every)]]
        )
        s_got, d_got = links.inward(s_own), links.across(d_own)
        (g_far,) = sums_of(
            order, [[(c_far, every), (c_got, pair)], [(e_far, every), (e_got, pair)]]
        )
        g_got = links.near(g_far)
    input_grad, first_sums = grad_first(
        order, [c_three, e_three], tokens, gmid, vec, w_one
    )
    if paired:
        s_own, d_own = sums_of(
            order, [[(s_own, every), (s_got, every)]], [[(d_own, every), (d_got, every)]]
        )
        s_got, d_got = links.across(s_own), links.outward(d_own)
    total = collect(order, first_sums, [c_sums, e_sums], mid_sums, down_sum, up_sum)
    if paired:
        t_got = links.near(total)
        cut = c_own.shape[0]
        low, high = (slice(0, cut), slice(None)), (slice(cut, None), slice(None))
        g_near, g_own = sums_of(
            order,
            [
                [(c_near, every), (c_got, 1), (g_got, (1, *low))],
                [(e_near, every), (e_got, 1), (g_got, (1, *high))],
            ],
            [
                [(c_own, every), (c_got, 0), (g_got, (0, *low))],
                [(e_own, every), (e_got, 0), (g_got, (0, *high))],
            ],
        )
        g_got = links.far(g_near)
    layer_out = down_out(order, hidden, mid, vec, w_down)
    if paired:
        g_own, s_own, d_own, total = turn(
            order, g_own, g_got, s_own, s_got, d_own, d_got, total, t_got
        )
        t_got, s_got = links.far(total), links.outward(s_own)
        d_pair = (d_own, links.swap(d_own))
        g_bands = deal(order, [[g_own], [total, t_got]])
        g_gots = links.levels(g_bands)
        down_weight_grad = finish_down(order, d_pair)
        (g_mine,) = sums_of(order, [[(b, every) for b in [g_bands[0], *g_gots]]])
        g_gots = links.levels([g_mine] * 4)
        s_own = pick(order, s_own, s_got)
        s_pair = (s_own, links.swap(s_own))
        up_weight_grad, output_weight_grad = finish_second(order, s_pair, share // 2)
        g_own = undeal(order, [g_mine, *g_gots])
        g_pair = (g_own, links.swap(g_own))
    else:
        s_pair = links.whole_sum(s_send, s_own, s_near, s_far)
        d_pair = links.whole_sum(d_send, d_own, d_near, d_far)
        c_pair = links.whole_sum(c_send, c_own, c_near, c_far)
        e_pair = links.whole_sum(e_send, e_own, e_near, e_far)
        g_pair = [jnp.concatenate([c, e], 0) for c, e in zip(c_pair, e_pair)]
        total = lax.psum(total, ("wide", "narrow"))
        down_weight_grad = finish_down(order, d_pair)
        up_weight_grad, output_weight_grad = finish_second(order, s_pair, share // 2)
    half = share // 2
    plan = []
    for i in range(3):
        parts = []
        for c, pairs in enumerate(CHUNKS):
            at, stop = i * PAIR * pairs, (i + 1) * PAIR * pairs
            while at < stop:
                end = min(stop, (at // D + 1) * D)
                block = at // D + c * (3 * PAIR * CHUNKS[0] // D)
                parts.append((0, block, at % D, end - at))
                at = end
        plan.append((D, parts))
    place = slice(BAND * 3, BAND * 3 + 16) if paired else None
    first_grads = finish(order, half, [g_pair], plan, place)
    if paired:
        mine, up_mine = first_grads[3], first_grads[4].reshape(-1)
    else:
        n = lax.axis_index("narrow")
        mine = lax.dynamic_slice_in_dim(total[:8], n * share, share, 1)
        up_share = up_bias.shape[0]
        up_mine = lax.dynamic_slice_in_dim(total[8:12].reshape(FF), n * up_share, up_share)
    return (
        layer_out,
        input_grad,
        mine[0],
        mine[1],
        first_grads[0],
        mine[2],
        first_grads[1],
        first_grads[2],
        mine[3],
        output_weight_grad,
        mine[4],
        mine[5],
        mine[6],
        up_weight_grad,
        up_mine,
        down_weight_grad,
        mine[7],
    )


def solution(mesh):
    rows, vector, matrix = P(("wide", "narrow"), None), P("narrow"), P("narrow", None)
    in_specs = (rows, P(("wide", "narrow")), rows) + tuple(
        matrix if i in (2, 4, 5, 7, 11, 13) else vector for i in range(15)
    )
    out_specs = (rows, rows) + in_specs[3:]
    return jax.shard_map(
        functools.partial(layer, Links(mesh)),
        mesh=mesh,
        in_specs=in_specs,
        out_specs=out_specs,
        check_vma=False,
    )
```
